32 devices in a mesh: fsdp: 8 (over z, y), rep: 4 (over x, core).
Axes of the slice: x: 2, y: 2, z: 4, core: 2. Of those that a mesh axis runs over, the one named last changes fastest.
Arguments:
- tokens: bfloat16 [4096, 2048], P(('fsdp', 'rep')), may hold values from -9 to 9
- w_query: bfloat16 [2048, 2048], P('fsdp'), may hold values from -0.03125 to 0.03125
- w_key: bfloat16 [2048, 2048], P('fsdp'), may hold values from -0.125 to 0.125
- w_value: bfloat16 [2048, 2048], P('fsdp'), may hold values from -0.125 to 0.125
- w_attn_out: bfloat16 [2048, 2048], P('fsdp'), may hold values from -0.5 to 0.5
- w_gate: bfloat16 [2048, 5120], P('fsdp'), may hold values from -0.125 to 0.125
- w_up: bfloat16 [2048, 5120], P('fsdp'), may hold values from -0.125 to 0.125
- w_ff_out: bfloat16 [2048, 5120], P('fsdp'), may hold values from -0.078125 to 0.078125
- gain_attn: float32 [2048], replicated, may hold values from 0.1 to 1.9
- gain_ffn: float32 [2048], replicated, may hold values from 0.1 to 1.9
- rel_table: float32 [32, 32], replicated, may hold values from -4 to 4
- doc_lengths: int32 [8, 8], P('fsdp'), may hold values from 1 to 505, as said below
- cotangent: bfloat16 [4096, 2048], P(('fsdp', 'rep')), may hold values from -9 to 9
Outputs:
- out: bfloat16 [4096, 2048], P(('fsdp', 'rep'))
- grad_input: float32 [4096, 2048], P(('fsdp', 'rep'))
- grad_w_query: float32 [2048, 2048], P('fsdp')
- grad_w_key: float32 [2048, 2048], P('fsdp')
- grad_w_value: float32 [2048, 2048], P('fsdp')
- grad_w_attn_out: float32 [2048, 2048], P('fsdp')
- grad_w_gate: float32 [2048, 5120], P('fsdp')
- grad_w_up: float32 [2048, 5120], P('fsdp')
- grad_w_ff_out: float32 [2048, 5120], P('fsdp')
- grad_gain_attn: float32 [2048], replicated
- grad_gain_ffn: float32 [2048], replicated
- grad_rel_table: float32 [32, 32], replicated
- norms: float32 [2], replicated
The draws below stay inside these ranges and needn't reach their ends.
Inputs may be any that keep to these rules, and one draw needn't show every extreme that they name: `doc_lengths`: each row gives the lengths of 8 documents packed from the start of a sequence of 512 tokens; the tokens after them, at most 32, are padding; each row holds one document longer than three quarters of 512.
All inputs are finite; a program needn't handle non-finite values.
Results may differ from the reference program's by a relative error of at most 0.015.
The reference program's roundings to bfloat16 on the way count: a program that leaves them out, or rounds other values in their place, can miss the bound.
Values may be sent and summed in bfloat16 or wider, within the bound.
A program may use at most 640 MiB of HBM per device.

```python
import jax
import jax.numpy as jnp
from jax import lax

D = 2048
HEADS = 32
HEAD_DIM = 64
FF = 5120
BUCKETS = 32
DOCS = 8
HD = 2048
SEQ_LEN = 512
SEQS = 8
TOKENS = 4096


def rising_scale(count):
    return 0.5 * 3.0 ** (jnp.arange(count, dtype=jnp.float32) / max(count - 1, 1))


def draw_tokens(key, part):
    key = jax.random.fold_in(key, 1)
    first = jax.random.fold_in(key, 0)
    base = jnp.clip(jax.random.normal(first, (TOKENS, D), jnp.float32), -6.0, 6.0)
    return (base * rising_scale(TOKENS)[:, None]).astype(jnp.bfloat16)


def draw_cotangent(key, part):
    key = jax.random.fold_in(key, 2)
    first = jax.random.fold_in(key, 0)
    base = jnp.clip(jax.random.normal(first, (TOKENS, D), jnp.float32), -6.0, 6.0)
    return (base * rising_scale(TOKENS)[::-1][:, None]).astype(jnp.bfloat16)


def draw_doc_lengths(key, part):
    key = jax.random.fold_in(key, 3)
    k_pad, k_long, k_weights, k_slot, k_pick = jax.random.split(key, 5)
    chosen = jax.random.randint(k_pick, (), 0, SEQS)
    rows_index = jnp.arange(SEQS, dtype=jnp.int32)
    padding = jax.random.randint(k_pad, (SEQS,), 0, SEQ_LEN // 16 + 1)
    padding = jnp.where(rows_index == chosen, 0, padding)
    least_long = 3 * SEQ_LEN // 4 + 1
    most_long = SEQ_LEN - padding - (DOCS - 1)
    longest = least_long + jax.random.randint(k_long, (SEQS,), 0, 1 << 20) % (most_long - least_long + 1)
    longest = jnp.where(rows_index == chosen, most_long, longest)
    rest = SEQ_LEN - padding - longest
    weights = jax.random.randint(k_weights, (SEQS, DOCS - 1), 1, 6)
    extra = rest - (DOCS - 1)
    others = 1 + weights * extra[:, None] // jnp.sum(weights, axis=1, keepdims=True)
    others = jnp.concatenate([others[:, :-1], (rest - jnp.sum(others[:, :-1], axis=1))[:, None]], axis=1)
    slot = jax.random.randint(k_slot, (SEQS,), 0, DOCS)
    index = jnp.arange(DOCS, dtype=jnp.int32)[None, :]
    source = jnp.minimum(index - (index > slot[:, None]).astype(jnp.int32), DOCS - 2)
    picked = jnp.take_along_axis(others, source, axis=1)
    return jnp.where(index == slot[:, None], longest[:, None], picked).astype(jnp.int32)


def block_scale(stream_key, extent, pieces, low, largest):
    def one(axis_at, blocks):
        steps = jax.random.uniform(jax.random.fold_in(jax.random.fold_in(stream_key, 6), axis_at), (blocks,), jnp.float32, low / len(pieces), largest / len(pieces))
        return jnp.repeat(jnp.exp(steps), extent[axis_at] // blocks).reshape((-1,) + (1,) * (len(extent) - axis_at - 1))

    gain = one(*pieces[0])
    for cut in pieces[1:]:
        gain = gain * one(*cut)
    return gain


def scatter_about(rng, dims, width, bound, shards=(), kind=jnp.bfloat16):
    entries = jax.random.normal(rng, dims, jnp.float32) * width
    if len(shards) > 0:
        entries = block_scale(rng, dims, shards, -0.22, 0.18) * entries
    return jnp.clip(entries, min=-bound, max=bound).astype(kind)


def setup_inputs(seed: int = 0) -> dict:
    arg_keys = jax.random.split(jax.random.key(seed), 14)
    tokens = draw_tokens(jax.random.fold_in(arg_keys[13], 71), 0)
    w_query = scatter_about(arg_keys[1], (D, HD), (D * HEAD_DIM // 4) ** -0.5, 0.03125, ((0, 8),))
    w_key = scatter_about(arg_keys[2], (D, HD), D ** -0.5, 0.125, ((0, 8),))
    w_value = scatter_about(arg_keys[3], (D, HD), D ** -0.5, 0.125, ((0, 8),))
    w_attn_out = scatter_about(arg_keys[4], (D, HD), (HD // 16) ** -0.5, 0.5, ((0, 8),))
    w_gate = scatter_about(arg_keys[5], (D, FF), D ** -0.5, 0.125, ((0, 8),))
    w_up = scatter_about(arg_keys[6], (D, FF), D ** -0.5, 0.125, ((0, 8),))
    w_ff_out = scatter_about(arg_keys[7], (D, FF), FF ** -0.5, 0.078125, ((0, 8),))
    gain_attn = jnp.clip(1.0 + 0.18 * jax.random.normal(arg_keys[8], (D,), jnp.float32), 0.1, 1.9)
    gain_ffn = jnp.clip(1.0 + 0.18 * jax.random.normal(arg_keys[9], (D,), jnp.float32), 0.1, 1.9)
    rel_table = scatter_about(arg_keys[10], (BUCKETS, HEADS), 1.0, 4.0, (), jnp.float32)
    doc_lengths = draw_doc_lengths(jax.random.fold_in(arg_keys[13], 71), 0)
    cotangent = draw_cotangent(jax.random.fold_in(arg_keys[13], 71), 0)
    return dict(tokens=tokens, w_query=w_query, w_key=w_key, w_value=w_value, w_attn_out=w_attn_out, w_gate=w_gate, w_up=w_up, w_ff_out=w_ff_out, gain_attn=gain_attn, gain_ffn=gain_ffn, rel_table=rel_table, doc_lengths=doc_lengths, cotangent=cotangent)


@jax.custom_vjp
def low(v):
    return lax.optimization_barrier(v.astype(jnp.bfloat16)).astype(jnp.float32)

@jax.custom_vjp
def low_back(v):
    return v

def low_keep(v):
    return (low(v), None)

def low_pass(kept, grad):
    return (grad,)

def back_keep(v):
    return (v, None)

def back_low(kept, grad):
    return (low(grad),)
low.defvjp(low_keep, low_pass)
low_back.defvjp(back_keep, back_low)
eps = 1e-06
thresholds = (12, 16, 23, 32, 46, 64, 91)

def gelu_tanh(v):
    return jax.nn.gelu(v, approximate=True)

def matmul(left, right):
    return jnp.dot(left, right, precision=lax.Precision.HIGHEST, preferred_element_type=jnp.float32)

def bucket_grid(length):
    position = jnp.arange(length, dtype=jnp.int32)
    offset = position[None, :] - position[:, None]
    distance = jnp.abs(offset)
    far = jnp.full(distance.shape, 8, jnp.int32)
    for edge in thresholds:
        far = far + (distance >= edge).astype(jnp.int32)
    return jnp.where(offset > 0, 16, 0).astype(jnp.int32) + jnp.where(distance < 8, distance, far)

def layer(xf, wq, wk, wv, wo, wg, wu, wf, g1, g2, table, segments, keep, buckets):
    inv1 = lax.rsqrt(lax.optimization_barrier(jnp.mean(xf * xf, axis=-1, keepdims=True)) + eps)
    n1 = low(xf * inv1 * g1)
    query = low(low_back(matmul(n1, wq)))
    key_rows = low(low_back(matmul(n1, wk)))
    value = low(low_back(matmul(n1, wv)))
    bias = jnp.transpose(table[buckets], (2, 0, 1))

    def attend(items):
        q_seq, k_seq, v_seq, seg_seq = items
        logits = low_back(jnp.einsum('qhd,khd->hqk', q_seq, k_seq, precision=lax.Precision.HIGHEST))
        same = seg_seq[:, None] == seg_seq[None, :]
        scores = jnp.where(same[None], logits + bias, -1e+30)
        probs = low(jax.nn.softmax(scores, axis=-1))
        return jnp.einsum('hqk,khd->qhd', probs, v_seq, precision=lax.Precision.HIGHEST)
    shape4 = (SEQS, SEQ_LEN, HEADS, HEAD_DIM)
    ctx = lax.map(jax.checkpoint(attend), (query.reshape(shape4), key_rows.reshape(shape4), value.reshape(shape4), segments))
    ctx = low(low_back(ctx.reshape(TOKENS, HEADS * HEAD_DIM)))
    attn = keep[:, None] * low_back(matmul(ctx, wo.T))
    resid = xf + attn
    inv2 = lax.rsqrt(lax.optimization_barrier(jnp.mean(resid * resid, axis=-1, keepdims=True)) + eps)
    n2 = low(resid * inv2 * g2)
    gate = low_back(matmul(n2, wg))
    up = low_back(matmul(n2, wu))
    hidden = low(gelu_tanh(gate) * up)
    branch = low_back(matmul(hidden, wf.T))
    return (resid + branch, resid)

def reference(tokens, w_query, w_key, w_value, w_attn_out, w_gate, w_up, w_ff_out, gain_attn, gain_ffn, rel_table, doc_lengths, cotangent):
    ends = jnp.cumsum(doc_lengths, axis=1).astype(jnp.int32)
    position = jnp.arange(SEQ_LEN, dtype=jnp.int32)
    segments = lax.optimization_barrier(jnp.sum((position[None, :, None] >= ends[:, None, :]).astype(jnp.int32), axis=-1)).astype(jnp.int32)
    keep = (segments < DOCS).astype(jnp.float32).reshape(TOKENS)
    buckets = bucket_grid(SEQ_LEN)

    def forward(xf, wq, wk, wv, wo, wg, wu, wf, g1, g2, table):
        return layer(xf, wq, wk, wv, wo, wg, wu, wf, g1, g2, table, segments, keep, buckets)
    primals = (tokens.astype(jnp.float32), w_query.astype(jnp.float32), w_key.astype(jnp.float32), w_value.astype(jnp.float32), w_attn_out.astype(jnp.float32), w_gate.astype(jnp.float32), w_up.astype(jnp.float32), w_ff_out.astype(jnp.float32), gain_attn.astype(jnp.float32), gain_ffn.astype(jnp.float32), rel_table.astype(jnp.float32))
    out_f, pullback, resid = jax.vjp(forward, *primals, has_aux=True)
    grads = pullback(cotangent.astype(jnp.float32))
    norms = jnp.stack([jnp.sqrt(jnp.mean(resid * resid)), jnp.sqrt(jnp.mean(out_f * out_f))])
    return (out_f.astype(jnp.bfloat16), grads[0], grads[1], grads[2], grads[3], grads[4], grads[5], grads[6], grads[7], grads[8], grads[9], grads[10], norms)
```

```python
import functools

import jax
import jax.numpy as jnp
from jax import lax
from jax.experimental import pallas as pl
from jax.experimental.pallas import tpu as pltpu
from jax.sharding import Mesh
from jax.sharding import PartitionSpec as P

eps = 1e-06
thresholds = (12, 16, 23, 32, 46, 64, 91)
highest = lax.Precision.HIGHEST
F32 = jnp.float32
BF16 = jnp.bfloat16
far_below = -1e30
MESH = pl.DeviceIdType.MESH
swap = ((0, 1), (1, 0))
MIB = 1 << 20


def gelu_tanh(v):
    return jax.nn.gelu(v, approximate=True)


def flat_dot(left, right):
    return jnp.dot(left, right, preferred_element_type=F32)


def dot_last(left, right):
    return lax.dot_general(left, right, (((1,), (1,)), ((), ())), preferred_element_type=F32)


def dot_first(left, right):
    return lax.dot_general(left, right, (((0,), (0,)), ((), ())), preferred_element_type=F32)


def shear_bias(row, length):
    wide = jnp.broadcast_to(row, (length, 2 * length))
    return pltpu.roll(wide, length, 1, stride=1, stride_axis=0)[:, :length]


def attend_kernel(heads, hd, q_ref, k_ref, v_ref, vec_ref, segc_ref, segr_ref, ctx_ref, lse_ref, bias_ref):
    length = q_ref.shape[0]

    @pl.when(pl.program_id(0) == 0)
    def _():
        for h in range(heads):
            bias_ref[h] = shear_bias(vec_ref[pl.ds(h, 1), :], length)

    same = segc_ref[0] == segr_ref[0]
    contexts, logs = [], []
    for h in range(heads):
        cols = slice(h * hd, (h + 1) * hd)
        scores = jnp.where(same, dot_last(q_ref[:, cols], k_ref[:, cols]) + bias_ref[h], far_below)
        top = jnp.max(scores, axis=1, keepdims=True)
        expo = jnp.exp(scores - top)
        total = jnp.sum(expo, axis=1, keepdims=True)
        probs = (expo * (1.0 / total)).astype(BF16)
        contexts.append(flat_dot(probs, v_ref[:, cols]).astype(BF16))
        logs.append(top + jnp.log(total))
    ctx_ref[...] = jnp.concatenate(contexts, axis=1)
    lse_ref[...] = jnp.concatenate(logs, axis=1)


def attend(qkv, vec, seg, heads, hd):
    rows = qkv.shape[0]
    seqs, length = seg.shape
    wide = heads * hd

    def block(n):
        return pl.BlockSpec((length, wide), lambda i: (i, n))

    return pl.pallas_call(
        functools.partial(attend_kernel, heads, hd),
        grid=(seqs,),
        in_specs=[
            block(0),
            block(1),
            block(2),
            pl.BlockSpec((heads, 2 * length), lambda i: (0, 0)),
            pl.BlockSpec((1, length, 1), lambda i: (i, 0, 0)),
            pl.BlockSpec((1, 1, length), lambda i: (i, 0, 0)),
        ],
        out_specs=[block(0), pl.BlockSpec((length, heads), lambda i: (i, 0))],
        out_shape=[jax.ShapeDtypeStruct((rows, wide), BF16), jax.ShapeDtypeStruct((rows, heads), F32)],
        scratch_shapes=[pltpu.VMEM((heads, length, length), F32)],
        compiler_params=pltpu.CompilerParams(vmem_limit_bytes=48 * MIB),
        cost_estimate=pl.CostEstimate(flops=10_000_000_000, bytes_accessed=4_000_000, transcendentals=2_000_000),
    )(qkv, qkv, qkv, vec, seg[:, :, None], seg[:, None, :])


def attend_back_kernel(
    heads, hd, seqs, q_ref, k_ref, v_ref, d_ref, lse_ref, vec_ref, segc_ref, segr_ref, dq_ref, dk_ref, dv_ref, diag_ref, bias_ref, acc_ref
):
    length = q_ref.shape[0]
    step = pl.program_id(0)

    @pl.when(step == 0)
    def _():
        for h in range(heads):
            bias_ref[h] = shear_bias(vec_ref[pl.ds(h, 1), :], length)
            acc_ref[h] = jnp.zeros((length, length), F32)

    same = segc_ref[0] == segr_ref[0]
    dqs, dks, dvs = [], [], []
    for h in range(heads):
        cols = slice(h * hd, (h + 1) * hd)
        q, k, v, d = q_ref[:, cols], k_ref[:, cols], v_ref[:, cols], d_ref[:, cols]
        scores = jnp.where(same, dot_last(q, k) + bias_ref[h], far_below)
        probs = jnp.exp(scores - lse_ref[:, h : h + 1])
        dprobs = dot_last(d, v)
        dvs.append(dot_first(probs.astype(BF16), d).astype(BF16))
        product = probs * dprobs
        dscores = product - probs * jnp.sum(product, axis=1, keepdims=True)
        acc_ref[h] += dscores
        dlogits = dscores.astype(BF16)
        dqs.append(flat_dot(dlogits, k).astype(BF16))
        dks.append(dot_first(dlogits, q).astype(BF16))
    dq_ref[...] = jnp.concatenate(dqs, axis=1)
    dk_ref[...] = jnp.concatenate(dks, axis=1)
    dv_ref[...] = jnp.concatenate(dvs, axis=1)

    @pl.when(step == seqs - 1)
    def _():
        def add(g, total):
            at = pl.multiple_of(g * 8, 8)
            rows = acc_ref[:, pl.ds(at, 8), :].reshape(heads * 8, length)
            wide = jnp.concatenate([rows, jnp.zeros_like(rows)], axis=1)
            return total + pltpu.roll(wide, 2 * length - g * 8, 1)

        total = lax.fori_loop(0, length // 8, add, jnp.zeros((heads * 8, 2 * length), F32))
        total = total.reshape(heads, 8, 2 * length)
        out = total[:, 0, :]
        for r in range(1, 8):
            out = out + pltpu.roll(total[:, r, :], 2 * length - r, 1)
        diag_ref[...] = out


def attend_back(qkv, dctx, lse, vec, seg, heads, hd):
    rows = qkv.shape[0]
    seqs, length = seg.shape
    wide = heads * hd

    def block(n):
        return pl.BlockSpec((length, wide), lambda i: (i, n))

    whole = pl.BlockSpec((heads, 2 * length), lambda i: (0, 0))
    return pl.pallas_call(
        functools.partial(attend_back_kernel, heads, hd, seqs),
        grid=(seqs,),
        in_specs=[
            block(0),
            block(1),
            block(2),
            block(0),
            pl.BlockSpec((length, heads), lambda i: (i, 0)),
            whole,
            pl.BlockSpec((1, length, 1), lambda i: (i, 0, 0)),
            pl.BlockSpec((1, 1, length), lambda i: (i, 0, 0)),
        ],
        out_specs=[block(0), block(0), block(0), whole],
        out_shape=[jax.ShapeDtypeStruct((rows, wide), BF16)] * 3 + [jax.ShapeDtypeStruct((heads, 2 * length), F32)],
        scratch_shapes=[pltpu.VMEM((heads, length, length), F32)] * 2,
        compiler_params=pltpu.CompilerParams(vmem_limit_bytes=56 * MIB),
        cost_estimate=pl.CostEstimate(flops=20_000_000_000, bytes_accessed=8_000_000, transcendentals=2_000_000),
    )(qkv, qkv, qkv, dctx, lse, vec, seg[:, :, None], seg[:, None, :])


def place():
    return lax.axis_index("b"), lax.axis_index("x"), lax.axis_index("c")


def slot(b, x, c):
    return b * 4 + x * 2 + c


def meet():
    b, x, c = place()
    barrier = pltpu.get_barrier_semaphore()
    for axis, other in (("b", 1 - b), ("x", 1 - x), ("c", 1 - c)):
        pl.semaphore_signal(barrier, inc=1, device_id={axis: other}, device_id_type=MESH)
    pl.semaphore_wait(barrier, 3)


def remote(src, dst, sends, recvs, n, axis):
    return pltpu.make_async_remote_copy(
        src_ref=src,
        dst_ref=dst,
        send_sem=sends.at[n],
        recv_sem=recvs.at[n],
        device_id={axis: 1 - lax.axis_index(axis)},
        device_id_type=MESH,
    )


def gather_steps(src, out, sends, recvs, local):
    b, x, c = place()
    rows = src.shape[0]
    half = rows // 2
    top, low = pl.ds(0, half), pl.ds(half, half)
    own, at_x, at_b, at_d = slot(b, x, c), slot(b, 1 - x, c), slot(1 - b, x, c), slot(1 - b, 1 - x, c)
    copies = [
        remote(src, out.at[own], sends, recvs, 0, "x"),
        remote(src, out.at[own], sends, recvs, 1, "b"),
        remote(out.at[at_b, top], out.at[at_b, top], sends, recvs, 2, "x"),
        remote(out.at[at_x, low], out.at[at_x, low], sends, recvs, 3, "b"),
        remote(src, out.at[own], sends, recvs, 4, "c"),
        remote(out.at[at_x], out.at[at_x], sends, recvs, 5, "c"),
        remote(out.at[at_b], out.at[at_b], sends, recvs, 6, "c"),
        remote(out.at[at_d, top], out.at[at_d, top], sends, recvs, 7, "c"),
        remote(out.at[at_d, low], out.at[at_d, low], sends, recvs, 8, "c"),
    ]
    keep = pltpu.make_async_copy(src, out.at[own], local)
    for n in (0, 1, 4):
        copies[n].start()
    keep.start()
    copies[0].wait_recv()
    copies[3].start()
    copies[5].start()
    copies[1].wait_recv()
    copies[2].start()
    copies[6].start()
    copies[2].wait_recv()
    copies[7].start()
    copies[3].wait_recv()
    copies[8].start()
    for n in (4, 5, 6, 7, 8):
        copies[n].wait_recv()
    for copy in copies:
        copy.wait_send()
    keep.wait()


def gather_kernel(src, out, sends, recvs, local):
    meet()
    gather_steps(src, out, sends, recvs, local)


def gather_group(rows, number):
    count, width = rows.shape
    return pl.pallas_call(
        gather_kernel,
        out_shape=jax.ShapeDtypeStruct((8, count, width), rows.dtype),
        in_specs=[pl.BlockSpec(memory_space=pl.ANY)],
        out_specs=pl.BlockSpec(memory_space=pl.ANY),
        scratch_shapes=[pltpu.SemaphoreType.DMA((9,)), pltpu.SemaphoreType.DMA((9,)), pltpu.SemaphoreType.DMA],
        compiler_params=pltpu.CompilerParams(collective_id=number, has_side_effects=True),
        cost_estimate=pl.CostEstimate(flops=0, bytes_accessed=80_000_000, transcendentals=0),
    )(rows).reshape(8 * count, width)


def in_rows(first, count, body, chunk=16):
    def step(i, _):
        body(pl.ds(pl.multiple_of(first + i * chunk, chunk), chunk))
        return 0

    lax.fori_loop(0, count // chunk, step, 0)


def scatter_steps(parts, acc, mine, sib, out, diag, last, sends, recvs, local):
    b, x, c = place()
    rows = parts.shape[1]
    half = rows // 2
    top, low = pl.ds(0, half), pl.ds(half, half)
    seats = [(b, x), (b, 1 - x), (1 - b, x), (1 - b, 1 - x)]
    to_core = [remote(parts.at[slot(*seats[q], 1 - c)], sib.at[q], sends, recvs, q, "c") for q in range(4)]
    here = [pltpu.make_async_copy(parts.at[slot(*seats[q], c)], mine.at[q], local.at[q]) for q in range(4)]
    for q in (3, 1, 2, 0):
        to_core[q].start()
        here[q].start()
    diag_x = remote(out.at[2, top], diag.at[0], sends, recvs, 4, "x")
    diag_b = remote(out.at[2, low], diag.at[1], sends, recvs, 5, "b")
    x_top = remote(out.at[0, top], last.at[0, top], sends, recvs, 6, "x")
    x_low = remote(out.at[0, low], last.at[0, low], sends, recvs, 7, "x")
    b_top = remote(out.at[1, top], last.at[1, top], sends, recvs, 8, "b")
    b_low = remote(out.at[1, low], last.at[1, low], sends, recvs, 9, "b")

    def ready(q):
        to_core[q].wait_recv()
        here[q].wait()

    def both(q, at):
        return mine[q, at, :].astype(F32) + sib[q, at, :].astype(F32)

    def put(n, q, first):
        def body(at):
            out[n, at, :] = both(q, at).astype(BF16)

        in_rows(first, half, body)

    ready(3)
    put(2, 3, 0)
    diag_x.start()
    put(2, 3, half)
    diag_b.start()
    ready(1)
    put(0, 1, 0)
    x_top.start()
    ready(2)
    put(1, 2, half)
    b_low.start()
    ready(0)

    def own(at):
        acc[at, :] = both(0, at)

    in_rows(0, rows, own)
    diag_b.wait_recv()

    def add_low(i, _):
        at = pl.ds(pl.multiple_of(half + i * 16, 16), 16)
        out[0, at, :] = (both(1, at) + diag[1, pl.ds(pl.multiple_of(i * 16, 16), 16), :].astype(F32)).astype(BF16)
        return 0

    lax.fori_loop(0, half // 16, add_low, 0)
    x_low.start()
    diag_x.wait_recv()

    def add_top(i, _):
        at = pl.ds(pl.multiple_of(i * 16, 16), 16)
        out[1, at, :] = (both(2, at) + diag[0, at, :].astype(F32)).astype(BF16)
        return 0

    lax.fori_loop(0, half // 16, add_top, 0)
    b_top.start()
    for copy in (x_top, b_low, x_low, b_top):
        copy.wait_recv()
    for copy in to_core + [diag_x, diag_b, x_top, x_low, b_top, b_low]:
        copy.wait_send()

    def finish(at):
        acc[at, :] += last[0, at, :].astype(F32) + last[1, at, :].astype(F32)

    in_rows(0, rows, finish)


def scatter_scratch(rows, width):
    return [
        pltpu.VMEM((4, rows, width), BF16),
        pltpu.VMEM((4, rows, width), BF16),
        pltpu.VMEM((3, rows, width), BF16),
        pltpu.VMEM((2, rows // 2, width), BF16),
        pltpu.VMEM((2, rows, width), BF16),
        pltpu.SemaphoreType.DMA((10,)),
        pltpu.SemaphoreType.DMA((10,)),
        pltpu.SemaphoreType.DMA((4,)),
    ]


def scatter_kernel(parts, acc, *scratch):
    meet()
    scatter_steps(parts, acc, *scratch)


any_space = pl.BlockSpec(memory_space=pl.ANY)
in_vmem = pl.BlockSpec(memory_space=pltpu.VMEM)


def scatter_group(parts, number):
    rows, width = parts.shape[0] // 8, parts.shape[1]
    return pl.pallas_call(
        scatter_kernel,
        out_shape=jax.ShapeDtypeStruct((rows, width), F32),
        in_specs=[any_space],
        out_specs=in_vmem,
        scratch_shapes=scatter_scratch(rows, width),
        compiler_params=pltpu.CompilerParams(collective_id=number, has_side_effects=True, vmem_limit_bytes=32 * MIB),
        cost_estimate=pl.CostEstimate(flops=0, bytes_accessed=80_000_000, transcendentals=0),
    )(parts.reshape(8, rows, width))


def middle_kernel(parts, tokens, keep, gain, resid, n2_all, acc, n2, sends2, recvs2, local2, *scratch):
    meet()
    scatter_steps(parts, acc, *scratch)

    def body(at):
        value = tokens[at, :].astype(F32) + keep[at, :] * acc[at, :]
        resid[at, :] = value
        inv = lax.rsqrt(jnp.mean(value * value, axis=-1, keepdims=True) + eps)
        n2[at, :] = (value * inv * gain[...]).astype(BF16)

    in_rows(0, tokens.shape[0], body)
    gather_steps(n2, n2_all, sends2, recvs2, local2)


def middle(parts, tokens, keep, gain, number):
    rows, width = tokens.shape
    resid, n2_all = pl.pallas_call(
        middle_kernel,
        out_shape=[jax.ShapeDtypeStruct((rows, width), F32), jax.ShapeDtypeStruct((8, rows, width), BF16)],
        in_specs=[any_space, in_vmem, in_vmem, in_vmem],
        out_specs=[in_vmem, any_space],
        scratch_shapes=[
            pltpu.VMEM((rows, width), F32),
            pltpu.VMEM((rows, width), BF16),
            pltpu.SemaphoreType.DMA((9,)),
            pltpu.SemaphoreType.DMA((9,)),
            pltpu.SemaphoreType.DMA,
        ]
        + scatter_scratch(rows, width),
        compiler_params=pltpu.CompilerParams(collective_id=number, has_side_effects=True, vmem_limit_bytes=32 * MIB),
        cost_estimate=pl.CostEstimate(flops=0, bytes_accessed=160_000_000, transcendentals=0),
    )(parts.reshape(8, rows, width), tokens, keep, gain[None, :])
    return resid, n2_all.reshape(8 * rows, width)


def middle_back_kernel(
    parts, resid, cotangent, keep, gain, dresid, dattn_all, dgain, acc, dattn, sends2, recvs2, local2, *scratch
):
    meet()
    scatter_steps(parts, acc, *scratch)
    dgain[...] = jnp.zeros_like(dgain)

    def body(at):
        value, dn2 = resid[at, :], acc[at, :]
        inv = lax.rsqrt(jnp.mean(value * value, axis=-1, keepdims=True) + eps)
        inner = dn2 * gain[...]
        grad = (
            cotangent[at, :].astype(F32)
            + inv * inner
            - value * (inv * inv * inv * jnp.mean(inner * value, axis=-1, keepdims=True))
        )
        dresid[at, :] = grad
        dgain[...] += jnp.sum(dn2 * value * inv, axis=0, keepdims=True)
        dattn[at, :] = (keep[at, :] * grad).astype(BF16)

    in_rows(0, resid.shape[0], body)
    gather_steps(dattn, dattn_all, sends2, recvs2, local2)


def middle_back(parts, resid, cotangent, keep, gain, number):
    rows, width = resid.shape
    dresid, dattn_all, dgain = pl.pallas_call(
        middle_back_kernel,
        out_shape=[
            jax.ShapeDtypeStruct((rows, width), F32),
            jax.ShapeDtypeStruct((8, rows, width), BF16),
            jax.ShapeDtypeStruct((1, width), F32),
        ],
        in_specs=[any_space, in_vmem, in_vmem, in_vmem, in_vmem],
        out_specs=[in_vmem, any_space, in_vmem],
        scratch_shapes=[
            pltpu.VMEM((rows, width), F32),
            pltpu.VMEM((rows, width), BF16),
            pltpu.SemaphoreType.DMA((9,)),
            pltpu.SemaphoreType.DMA((9,)),
            pltpu.SemaphoreType.DMA,
        ]
        + scatter_scratch(rows, width),
        compiler_params=pltpu.CompilerParams(collective_id=number, has_side_effects=True, vmem_limit_bytes=32 * MIB),
        cost_estimate=pl.CostEstimate(flops=0, bytes_accessed=160_000_000, transcendentals=0),
    )(parts.reshape(8, rows, width), resid, cotangent, keep, gain[None, :])
    return dresid, dattn_all.reshape(8 * rows, width), dgain[0]


def in_order(index, own, other):
    first = index == 0
    return jnp.stack([jnp.where(first, own, other), jnp.where(first, other, own)])


def gather_weights(weights):
    a, y = lax.axis_index("a"), lax.axis_index("y")
    b, x, c = place()
    spans = lax.axis_size("a")

    def columns(to):
        at = slot(to, x, c)
        return jnp.concatenate(
            [lax.dynamic_slice_in_dim(w, at * (w.shape[1] // 8), w.shape[1] // 8, 1) for w in weights], axis=1
        )

    pair = in_order(b, columns(b), lax.ppermute(columns(1 - b), "b", swap))
    blocks = [pair]
    for _ in range(spans - 1):
        blocks.append(lax.ppermute(blocks[-1], "a", [(i, (i + 1) % spans) for i in range(spans)]))
    full = [in_order(y, block, lax.ppermute(block, "y", swap)) for block in blocks]
    if spans == 2:
        stacked = in_order(a, full[0], full[1])
    else:
        stacked = jnp.zeros((spans,) + full[0].shape, full[0].dtype)
        for k, block in enumerate(full):
            stacked = lax.dynamic_update_slice_in_dim(stacked, block[None], (a - k) % spans, 0)
    stacked = stacked.transpose(0, 2, 1, 3, 4)
    return stacked.reshape(-1, stacked.shape[-1])


def scatter_gradient(grad):
    a, y = lax.axis_index("a"), lax.axis_index("y")
    b, x, c = place()
    spans = lax.axis_size("a")
    blocks = grad.reshape(spans, 2, 2, -1, grad.shape[-1])

    def take(at_a, at_y):
        return blocks[at_a % spans, :, at_y]

    def plus(*terms):
        return functools.reduce(jnp.add, [t.astype(F32) for t in terms]).astype(BF16)

    def pair_sum(at_a):
        return plus(take(at_a, y), lax.ppermute(take(at_a, 1 - y), "y", swap))

    total = pair_sum(a + spans - 1) if spans > 1 else None
    for k in range(spans - 1, 0, -1):
        total = lax.ppermute(total, "a", [(i, (i + 1) % spans) for i in range(spans)])
        if k > 1:
            total = plus(total, pair_sum(a + k - 1))
    got = lax.ppermute(take(a, 1 - y), "y", swap)
    total = plus(take(a, y), got, total)
    mine, theirs = total[b], lax.ppermute(total[1 - b], "b", swap)
    held = in_order(b, mine, theirs)
    held = in_order(x, held, lax.ppermute(held, "x", swap))
    held = in_order(c, held, lax.ppermute(held, "c", swap))
    held = held.transpose(2, 1, 0, 3, 4)
    return held.reshape((8,) + held.shape[3:])


def side_by_side(held, first, count):
    part = held[:, :, first : first + count].astype(F32)
    return part.transpose(1, 0, 2).reshape(part.shape[1], 8 * count)


def per_device(
    tokens,
    w_query,
    w_key,
    w_value,
    w_attn_out,
    w_gate,
    w_up,
    w_ff_out,
    gain_attn,
    gain_ffn,
    rel_table,
    doc_lengths,
    cotangent,
):
    rows, width = tokens.shape
    n_buckets, heads_all = rel_table.shape
    heads = heads_all // 8
    hc = w_query.shape[1] // 8
    fc = w_gate.shape[1] // 8
    hd = hc // heads
    length = 4 * rows
    b, x, c = place()
    me = slot(b, x, c)

    other_docs = lax.ppermute(doc_lengths, "b", swap)
    ends = jnp.cumsum(in_order(b, doc_lengths[0], other_docs[0]), axis=1)
    positions = jnp.arange(length, dtype=jnp.int32)
    seg = jnp.sum((positions[None, :, None] >= ends[:, None, :]).astype(jnp.int32), axis=2)
    own_seg = lax.dynamic_slice(seg, (b, (x * 2 + c) * rows), (1, rows))[0]
    keep = (own_seg < doc_lengths.shape[1]).astype(F32)[:, None]
    offset = jnp.arange(-length, length, dtype=jnp.int32)
    distance = jnp.abs(offset)
    far = 8 + jnp.sum((distance[:, None] >= jnp.array(thresholds, jnp.int32)).astype(jnp.int32), axis=1)
    bucket = jnp.where(offset > 0, 16, 0) + jnp.where(distance < 8, distance, far)
    onehot = (jnp.arange(n_buckets, dtype=jnp.int32)[:, None] == bucket[None, :]).astype(F32)
    table = lax.dynamic_slice_in_dim(rel_table, me * heads, heads, 1)
    vec = lax.dot_general(table, onehot, (((0,), (0,)), ((), ())), precision=highest, preferred_element_type=F32)

    wqkv = gather_weights([w_query, w_key, w_value])
    wo = gather_weights([w_attn_out])
    wgu = gather_weights([w_gate, w_up])
    wf = gather_weights([w_ff_out])

    xf_all = gather_group(tokens, 0).astype(F32)
    inv_all = lax.rsqrt(jnp.mean(xf_all * xf_all, axis=-1, keepdims=True) + eps)
    n1 = (xf_all * inv_all * gain_attn).astype(BF16)
    qkv = flat_dot(n1, wqkv).astype(BF16)
    ctx, lse = attend(qkv, vec, seg, heads, hd)
    attn_part = dot_last(ctx, wo).astype(BF16)
    resid, n2 = middle(attn_part, tokens, keep, gain_ffn, 1)
    cot_all = gather_group(cotangent, 2)
    gate_up = flat_dot(n2, wgu)
    gate, up = gate_up[:, :fc], gate_up[:, fc:]
    activ, activ_back = jax.vjp(gelu_tanh, gate)
    hidden = (activ * up).astype(BF16)
    out_part = dot_last(hidden, wf).astype(BF16)
    out_f = resid + scatter_group(out_part, 3)

    dhidden = flat_dot(cot_all, wf)
    dgate = activ_back(dhidden * up)[0].astype(BF16)
    dup = (dhidden * activ).astype(BF16)
    dgu = jnp.concatenate([dgate, dup], axis=1)
    dn2_part = dot_last(dgu, wgu).astype(BF16)
    dresid, dattn, dgain_ffn = middle_back(dn2_part, resid, cotangent, keep, gain_ffn, 4)
    grad_f = scatter_gradient(dot_first(cot_all, hidden).astype(BF16))
    grad_gu = scatter_gradient(dot_first(n2, dgu).astype(BF16))
    dctx = flat_dot(dattn, wo).astype(BF16)
    grad_o = scatter_gradient(dot_first(dattn, ctx).astype(BF16))
    dq, dk, dv, diag = attend_back(qkv, dctx, lse, vec, seg, heads, hd)
    dqkv = jnp.concatenate([dq, dk, dv], axis=1)
    dn1 = scatter_group(dot_last(dqkv, wqkv).astype(BF16), 5)
    grad_qkv = scatter_gradient(dot_first(n1, dqkv).astype(BF16))

    xf = tokens.astype(F32)
    inv1 = lax.rsqrt(jnp.mean(xf * xf, axis=-1, keepdims=True) + eps)
    inner1 = dn1 * gain_attn
    grad_input = dresid + inv1 * inner1 - xf * inv1**3 * jnp.mean(inner1 * xf, axis=-1, keepdims=True)
    dgain_attn = jnp.sum(dn1 * xf * inv1, axis=0)

    order = jnp.roll(diag, length, axis=1)
    dtable_own = lax.dot_general(onehot, order, (((1,), (1,)), ((), ())), precision=highest, preferred_element_type=F32)
    dtable = lax.dynamic_update_slice(jnp.zeros((n_buckets, heads_all), F32), dtable_own, (0, me * heads))
    squares = jnp.stack([jnp.sum(resid * resid), jnp.sum(out_f * out_f)])
    everywhere = ("a", "b", "y", "x", "c")
    dgain_attn, dgain_ffn, dtable, squares = lax.psum((dgain_attn, dgain_ffn, dtable, squares), everywhere)
    entries = rows * width * 8 * 2 * lax.axis_size("a")
    norms = jnp.sqrt(squares / entries)
    return (
        out_f.astype(BF16),
        grad_input,
        side_by_side(grad_qkv, 0, hc),
        side_by_side(grad_qkv, hc, hc),
        side_by_side(grad_qkv, 2 * hc, hc),
        side_by_side(grad_o, 0, hc),
        side_by_side(grad_gu, 0, fc),
        side_by_side(grad_gu, fc, fc),
        side_by_side(grad_f, 0, fc),
        dgain_attn,
        dgain_ffn,
        dtable,
        norms,
    )


def solution(mesh):
    owners, copies = mesh.shape["fsdp"], mesh.shape["rep"]
    finer = Mesh(mesh.devices.reshape(owners // 4, 2, 2, copies // 2, 2), ("a", "b", "y", "x", "c"))
    owner = ("a", "b", "y")
    piece = P(owner + ("x", "c"), None)
    shard = P(owner, None)
    return jax.shard_map(
        per_device,
        mesh=finer,
        in_specs=(piece,) + (shard,) * 7 + (P(), P(), P(), shard, piece),
        out_specs=(piece, piece) + (shard,) * 7 + (P(), P(), P(), P()),
        check_vma=False,
    )
```

```python
import functools

import jax
import jax.numpy as jnp
from jax import lax
from jax.experimental import pallas as pl
from jax.experimental.pallas import tpu as pltpu
from jax.sharding import Mesh
from jax.sharding import PartitionSpec as P

eps = 1e-06
thresholds = (12, 16, 23, 32, 46, 64, 91)
highest = lax.Precision.HIGHEST
F32 = jnp.float32
BF16 = jnp.bfloat16
far_below = -1e30
MESH = pl.DeviceIdType.MESH
swap = ((0, 1), (1, 0))
MIB = 1 << 20


def gelu_tanh(v):
    return jax.nn.gelu(v, approximate=True)


def flat_dot(left, right):
    return jnp.dot(left, right, preferred_element_type=F32)


def dot_last(left, right):
    return lax.dot_general(left, right, (((1,), (1,)), ((), ())), preferred_element_type=F32)


def dot_first(left, right):
    return lax.dot_general(left, right, (((0,), (0,)), ((), ())), preferred_element_type=F32)


def shear_bias(row, length):
    wide = jnp.broadcast_to(row, (length, 2 * length))
    return pltpu.roll(wide, length, 1, stride=1, stride_axis=0)[:, :length]


def attend_kernel(heads, hd, q_ref, k_ref, v_ref, vec_ref, segc_ref, segr_ref, ctx_ref, lse_ref, bias_ref):
    length = q_ref.shape[0]

    @pl.when(pl.program_id(0) == 0)
    def _():
        for h in range(heads):
            bias_ref[h] = shear_bias(vec_ref[pl.ds(h, 1), :], length)

    same = segc_ref[0] == segr_ref[0]
    contexts, logs = [], []
    for h in range(heads):
        cols = slice(h * hd, (h + 1) * hd)
        scores = jnp.where(same, dot_last(q_ref[:, cols], k_ref[:, cols]) + bias_ref[h], far_below)
        top = jnp.max(scores, axis=1, keepdims=True)
        expo = jnp.exp(scores - top)
        total = jnp.sum(expo, axis=1, keepdims=True)
        probs = (expo * (1.0 / total)).astype(BF16)
        contexts.append(flat_dot(probs, v_ref[:, cols]).astype(BF16))
        logs.append(top + jnp.log(total))
    ctx_ref[...] = jnp.concatenate(contexts, axis=1)
    lse_ref[...] = jnp.concatenate(logs, axis=1)


def attend(qkv, vec, seg, heads, hd):
    rows = qkv.shape[0]
    seqs, length = seg.shape
    wide = heads * hd

    def block(n):
        return pl.BlockSpec((length, wide), lambda i: (i, n))

    return pl.pallas_call(
        functools.partial(attend_kernel, heads, hd),
        grid=(seqs,),
        in_specs=[
            block(0),
            block(1),
            block(2),
            pl.BlockSpec((heads, 2 * length), lambda i: (0, 0)),
            pl.BlockSpec((1, length, 1), lambda i: (i, 0, 0)),
            pl.BlockSpec((1, 1, length), lambda i: (i, 0, 0)),
        ],
        out_specs=[block(0), pl.BlockSpec((length, heads), lambda i: (i, 0))],
        out_shape=[jax.ShapeDtypeStruct((rows, wide), BF16), jax.ShapeDtypeStruct((rows, heads), F32)],
        scratch_shapes=[pltpu.VMEM((heads, length, length), F32)],
        compiler_params=pltpu.CompilerParams(vmem_limit_bytes=48 * MIB),
        cost_estimate=pl.CostEstimate(flops=10_000_000_000, bytes_accessed=4_000_000, transcendentals=2_000_000),
    )(qkv, qkv, qkv, vec, seg[:, :, None], seg[:, None, :])


def attend_back_kernel(
    heads, hd, seqs, q_ref, k_ref, v_ref, d_ref, lse_ref, vec_ref, segc_ref, segr_ref, dq_ref, dk_ref, dv_ref, diag_ref, bias_ref, acc_ref
):
    length = q_ref.shape[0]
    step = pl.program_id(0)

    @pl.when(step == 0)
    def _():
        for h in range(heads):
            bias_ref[h] = shear_bias(vec_ref[pl.ds(h, 1), :], length)
            acc_ref[h] = jnp.zeros((length, length), F32)

    same = segc_ref[0] == segr_ref[0]
    dqs, dks, dvs = [], [], []
    for h in range(heads):
        cols = slice(h * hd, (h + 1) * hd)
        q, k, v, d = q_ref[:, cols], k_ref[:, cols], v_ref[:, cols], d_ref[:, cols]
        scores = jnp.where(same, dot_last(q, k) + bias_ref[h], far_below)
        probs = jnp.exp(scores - lse_ref[:, h : h + 1])
        dprobs = dot_last(d, v)
        dvs.append(dot_first(probs.astype(BF16), d).astype(BF16))
        product = probs * dprobs
        dscores = product - probs * jnp.sum(product, axis=1, keepdims=True)
        acc_ref[h] += dscores
        dlogits = dscores.astype(BF16)
        dqs.append(flat_dot(dlogits, k).astype(BF16))
        dks.append(dot_first(dlogits, q).astype(BF16))
    dq_ref[...] = jnp.concatenate(dqs, axis=1)
    dk_ref[...] = jnp.concatenate(dks, axis=1)
    dv_ref[...] = jnp.concatenate(dvs, axis=1)

    @pl.when(step == seqs - 1)
    def _():
        def add(g, total):
            at = pl.multiple_of(g * 8, 8)
            rows = acc_ref[:, pl.ds(at, 8), :].reshape(heads * 8, length)
            wide = jnp.concatenate([rows, jnp.zeros_like(rows)], axis=1)
            return total + pltpu.roll(wide, 2 * length - g * 8, 1)

        total = lax.fori_loop(0, length // 8, add, jnp.zeros((heads * 8, 2 * length), F32))
        total = total.reshape(heads, 8, 2 * length)
        out = total[:, 0, :]
        for r in range(1, 8):
            out = out + pltpu.roll(total[:, r, :], 2 * length - r, 1)
        diag_ref[...] = out


def attend_back(qkv, dctx, lse, vec, seg, heads, hd):
    rows = qkv.shape[0]
    seqs, length = seg.shape
    wide = heads * hd

    def block(n):
        return pl.BlockSpec((length, wide), lambda i: (i, n))

    whole = pl.BlockSpec((heads, 2 * length), lambda i: (0, 0))
    return pl.pallas_call(
        functools.partial(attend_back_kernel, heads, hd, seqs),
        grid=(seqs,),
        in_specs=[
            block(0),
            block(1),
            block(2),
            block(0),
            pl.BlockSpec((length, heads), lambda i: (i, 0)),
            whole,
            pl.BlockSpec((1, length, 1), lambda i: (i, 0, 0)),
            pl.BlockSpec((1, 1, length), lambda i: (i, 0, 0)),
        ],
        out_specs=[block(0), block(0), block(0), whole],
        out_shape=[jax.ShapeDtypeStruct((rows, wide), BF16)] * 3 + [jax.ShapeDtypeStruct((heads, 2 * length), F32)],
        scratch_shapes=[pltpu.VMEM((heads, length, length), F32)] * 2,
        compiler_params=pltpu.CompilerParams(vmem_limit_bytes=56 * MIB),
        cost_estimate=pl.CostEstimate(flops=20_000_000_000, bytes_accessed=8_000_000, transcendentals=2_000_000),
    )(qkv, qkv, qkv, dctx, lse, vec, seg[:, :, None], seg[:, None, :])


def place():
    return lax.axis_index("b"), lax.axis_index("x"), lax.axis_index("c")


def slot(b, x, c):
    return b * 4 + x * 2 + c


def meet():
    b, x, c = place()
    barrier = pltpu.get_barrier_semaphore()
    for axis, other in (("b", 1 - b), ("x", 1 - x), ("c", 1 - c)):
        pl.semaphore_signal(barrier, inc=1, device_id={axis: other}, device_id_type=MESH)
    pl.semaphore_wait(barrier, 3)


def remote(src, dst, sends, recvs, n, axis):
    return pltpu.make_async_remote_copy(
        src_ref=src,
        dst_ref=dst,
        send_sem=sends.at[n],
        recv_sem=recvs.at[n],
        device_id={axis: 1 - lax.axis_index(axis)},
        device_id_type=MESH,
    )


def gather_steps(src, out, sends, recvs, local):
    b, x, c = place()
    rows = src.shape[0]
    half = rows // 2
    top, low = pl.ds(0, half), pl.ds(half, half)
    own, at_x, at_b, at_d = slot(b, x, c), slot(b, 1 - x, c), slot(1 - b, x, c), slot(1 - b, 1 - x, c)
    copies = [
        remote(src, out.at[own], sends, recvs, 0, "x"),
        remote(src, out.at[own], sends, recvs, 1, "b"),
        remote(out.at[at_b, top], out.at[at_b, top], sends, recvs, 2, "x"),
        remote(out.at[at_x, low], out.at[at_x, low], sends, recvs, 3, "b"),
        remote(src, out.at[own], sends, recvs, 4, "c"),
        remote(out.at[at_x], out.at[at_x], sends, recvs, 5, "c"),
        remote(out.at[at_b], out.at[at_b], sends, recvs, 6, "c"),
        remote(out.at[at_d, top], out.at[at_d, top], sends, recvs, 7, "c"),
        remote(out.at[at_d, low], out.at[at_d, low], sends, recvs, 8, "c"),
    ]
    keep = pltpu.make_async_copy(src, out.at[own], local)
    for n in (0, 1, 4):
        copies[n].start()
    keep.start()
    copies[0].wait_recv()
    copies[3].start()
    copies[5].start()
    copies[1].wait_recv()
    copies[2].start()
    copies[6].start()
    copies[2].wait_recv()
    copies[7].start()
    copies[3].wait_recv()
    copies[8].start()
    for n in (4, 5, 6, 7, 8):
        copies[n].wait_recv()
    for copy in copies:
        copy.wait_send()
    keep.wait()


def gather_kernel(src, out, sends, recvs, local):
    meet()
    gather_steps(src, out, sends, recvs, local)


def gather_group(rows, number):
    count, width = rows.shape
    return pl.pallas_call(
        gather_kernel,
        out_shape=jax.ShapeDtypeStruct((8, count, width), rows.dtype),
        in_specs=[pl.BlockSpec(memory_space=pl.ANY)],
        out_specs=pl.BlockSpec(memory_space=pl.ANY),
        scratch_shapes=[pltpu.SemaphoreType.DMA((9,)), pltpu.SemaphoreType.DMA((9,)), pltpu.SemaphoreType.DMA],
        compiler_params=pltpu.CompilerParams(collective_id=number, has_side_effects=True),
        cost_estimate=pl.CostEstimate(flops=0, bytes_accessed=80_000_000, transcendentals=0),
    )(rows).reshape(8 * count, width)


def in_rows(first, count, body, chunk=16):
    def step(i, _):
        body(pl.ds(pl.multiple_of(first + i * chunk, chunk), chunk))
        return 0

    lax.fori_loop(0, count // chunk, step, 0)


def scatter_steps(parts, acc, mine, sib, out, diag, last, sends, recvs, local):
    b, x, c = place()
    rows = parts.shape[1]
    half = rows // 2
    top, low = pl.ds(0, half), pl.ds(half, half)
    seats = [(b, x), (b, 1 - x), (1 - b, x), (1 - b, 1 - x)]
    to_core = [remote(parts.at[slot(*seats[q], 1 - c)], sib.at[q], sends, recvs, q, "c") for q in range(4)]
    here = [pltpu.make_async_copy(parts.at[slot(*seats[q], c)], mine.at[q], local.at[q]) for q in range(4)]
    for q in (3, 1, 2, 0):
        to_core[q].start()
        here[q].start()
    diag_x = remote(out.at[2, top], diag.at[0], sends, recvs, 4, "x")
    diag_b = remote(out.at[2, low], diag.at[1], sends, recvs, 5, "b")
    x_top = remote(out.at[0, top], last.at[0, top], sends, recvs, 6, "x")
    x_low = remote(out.at[0, low], last.at[0, low], sends, recvs, 7, "x")
    b_top = remote(out.at[1, top], last.at[1, top], sends, recvs, 8, "b")
    b_low = remote(out.at[1, low], last.at[1, low], sends, recvs, 9, "b")

    def ready(q):
        to_core[q].wait_recv()
        here[q].wait()

    def both(q, at):
        return mine[q, at, :].astype(F32) + sib[q, at, :].astype(F32)

    def put(n, q, first):
        def body(at):
            out[n, at, :] = both(q, at).astype(BF16)

        in_rows(first, half, body)

    ready(3)
    put(2, 3, 0)
    diag_x.start()
    put(2, 3, half)
    diag_b.start()
    ready(1)
    put(0, 1, 0)
    x_top.start()
    ready(2)
    put(1, 2, half)
    b_low.start()
    ready(0)

    def own(at):
        acc[at, :] = both(0, at)

    in_rows(0, rows, own)
    diag_b.wait_recv()

    def add_low(i, _):
        at = pl.ds(pl.multiple_of(half + i * 16, 16), 16)
        out[0, at, :] = (both(1, at) + diag[1, pl.ds(pl.multiple_of(i * 16, 16), 16), :].astype(F32)).astype(BF16)
        return 0

    lax.fori_loop(0, half // 16, add_low, 0)
    x_low.start()
    diag_x.wait_recv()

    def add_top(i, _):
        at = pl.ds(pl.multiple_of(i * 16, 16), 16)
        out[1, at, :] = (both(2, at) + diag[0, at, :].astype(F32)).astype(BF16)
        return 0

    lax.fori_loop(0, half // 16, add_top, 0)
    b_top.start()
    for copy in (x_top, b_low, x_low, b_top):
        copy.wait_recv()
    for copy in to_core + [diag_x, diag_b, x_top, x_low, b_top, b_low]:
        copy.wait_send()

    def finish(at):
        acc[at, :] += last[0, at, :].astype(F32) + last[1, at, :].astype(F32)

    in_rows(0, rows, finish)


def scatter_scratch(rows, width):
    return [
        pltpu.VMEM((4, rows, width), BF16),
        pltpu.VMEM((4, rows, width), BF16),
        pltpu.VMEM((3, rows, width), BF16),
        pltpu.VMEM((2, rows // 2, width), BF16),
        pltpu.VMEM((2, rows, width), BF16),
        pltpu.SemaphoreType.DMA((10,)),
        pltpu.SemaphoreType.DMA((10,)),
        pltpu.SemaphoreType.DMA((4,)),
    ]


def scatter_kernel(parts, acc, *scratch):
    meet()
    scatter_steps(parts, acc, *scratch)


any_space = pl.BlockSpec(memory_space=pl.ANY)
in_vmem = pl.BlockSpec(memory_space=pltpu.VMEM)


def scatter_group(parts, number):
    rows, width = parts.shape[0] // 8, parts.shape[1]
    return pl.pallas_call(
        scatter_kernel,
        out_shape=jax.ShapeDtypeStruct((rows, width), F32),
        in_specs=[any_space],
        out_specs=in_vmem,
        scratch_shapes=scatter_scratch(rows, width),
        compiler_params=pltpu.CompilerParams(collective_id=number, has_side_effects=True, vmem_limit_bytes=32 * MIB),
        cost_estimate=pl.CostEstimate(flops=0, bytes_accessed=80_000_000, transcendentals=0),
    )(parts.reshape(8, rows, width))


def middle_kernel(parts, tokens, keep, gain, resid, n2_all, acc, n2, sends2, recvs2, local2, *scratch):
    meet()
    scatter_steps(parts, acc, *scratch)

    def body(at):
        value = tokens[at, :].astype(F32) + keep[at, :] * acc[at, :]
        resid[at, :] = value
        inv = lax.rsqrt(jnp.mean(value * value, axis=-1, keepdims=True) + eps)
        n2[at, :] = (value * inv * gain[...]).astype(BF16)

    in_rows(0, tokens.shape[0], body)
    gather_steps(n2, n2_all, sends2, recvs2, local2)


def middle(parts, tokens, keep, gain, number):
    rows, width = tokens.shape
    resid, n2_all = pl.pallas_call(
        middle_kernel,
        out_shape=[jax.ShapeDtypeStruct((rows, width), F32), jax.ShapeDtypeStruct((8, rows, width), BF16)],
        in_specs=[any_space, in_vmem, in_vmem, in_vmem],
        out_specs=[in_vmem, any_space],
        scratch_shapes=[
            pltpu.VMEM((rows, width), F32),
            pltpu.VMEM((rows, width), BF16),
            pltpu.SemaphoreType.DMA((9,)),
            pltpu.SemaphoreType.DMA((9,)),
            pltpu.SemaphoreType.DMA,
        ]
        + scatter_scratch(rows, width),
        compiler_params=pltpu.CompilerParams(collective_id=number, has_side_effects=True, vmem_limit_bytes=32 * MIB),
        cost_estimate=pl.CostEstimate(flops=0, bytes_accessed=160_000_000, transcendentals=0),
    )(parts.reshape(8, rows, width), tokens, keep, gain[None, :])
    return resid, n2_all.reshape(8 * rows, width)


def middle_back_kernel(
    parts, resid, cotangent, keep, gain, dresid, dattn_all, dgain, acc, dattn, sends2, recvs2, local2, *scratch
):
    meet()
    scatter_steps(parts, acc, *scratch)
    dgain[...] = jnp.zeros_like(dgain)

    def body(at):
        value, dn2 = resid[at, :], acc[at, :]
        inv = lax.rsqrt(jnp.mean(value * value, axis=-1, keepdims=True) + eps)
        inner = dn2 * gain[...]
        grad = (
            cotangent[at, :].astype(F32)
            + inv * inner
            - value * (inv * inv * inv * jnp.mean(inner * value, axis=-1, keepdims=True))
        )
        dresid[at, :] = grad
        dgain[...] += jnp.sum(dn2 * value * inv, axis=0, keepdims=True)
        dattn[at, :] = (keep[at, :] * grad).astype(BF16)

    in_rows(0, resid.shape[0], body)
    gather_steps(dattn, dattn_all, sends2, recvs2, local2)


def middle_back(parts, resid, cotangent, keep, gain, number):
    rows, width = resid.shape
    dresid, dattn_all, dgain = pl.pallas_call(
        middle_back_kernel,
        out_shape=[
            jax.ShapeDtypeStruct((rows, width), F32),
            jax.ShapeDtypeStruct((8, rows, width), BF16),
            jax.ShapeDtypeStruct((1, width), F32),
        ],
        in_specs=[any_space, in_vmem, in_vmem, in_vmem, in_vmem],
        out_specs=[in_vmem, any_space, in_vmem],
        scratch_shapes=[
            pltpu.VMEM((rows, width), F32),
            pltpu.VMEM((rows, width), BF16),
            pltpu.SemaphoreType.DMA((9,)),
            pltpu.SemaphoreType.DMA((9,)),
            pltpu.SemaphoreType.DMA,
        ]
        + scatter_scratch(rows, width),
        compiler_params=pltpu.CompilerParams(collective_id=number, has_side_effects=True, vmem_limit_bytes=32 * MIB),
        cost_estimate=pl.CostEstimate(flops=0, bytes_accessed=160_000_000, transcendentals=0),
    )(parts.reshape(8, rows, width), resid, cotangent, keep, gain[None, :])
    return dresid, dattn_all.reshape(8 * rows, width), dgain[0]


def in_order(index, own, other):
    first = index == 0
    return jnp.stack([jnp.where(first, own, other), jnp.where(first, other, own)])


def remote_to(src, dst, send, recv, axis, to):
    return pltpu.make_async_remote_copy(
        src_ref=src, dst_ref=dst, send_sem=send, recv_sem=recv, device_id={axis: to}, device_id_type=MESH
    )


def meet_all(spans):
    a, y = lax.axis_index("a"), lax.axis_index("y")
    b, x, c = place()
    barrier = pltpu.get_barrier_semaphore()
    others = [("b", 1 - b), ("x", 1 - x), ("c", 1 - c), ("y", 1 - y)] + [("a", lax.rem(a + k, spans)) for k in range(1, spans)]
    for axis, other in others:
        pl.semaphore_signal(barrier, inc=1, device_id={axis: other}, device_id_type=MESH)
    pl.semaphore_wait(barrier, len(others))


def fetch_steps(spans, shards, fulls, sends, recvs, local):
    a, y = lax.axis_index("a"), lax.axis_index("y")
    b, x, c = place()
    me, pair = slot(b, x, c), slot(1 - b, x, c)
    count = shards[0].shape[0]

    def rows(at_a, at_b, at_y):
        return pl.ds(pl.multiple_of((at_a * 4 + at_b * 2 + at_y) * count, count), count)

    first, second, third, last = [], [], [], []
    for i, (shard, (full, start)) in enumerate(zip(shards, fulls)):
        n = shard.shape[1] // 8
        cols = pl.ds(start, n)
        mine = shard.at[:, pl.ds(pl.multiple_of(me * n, 128), n)]
        theirs = shard.at[:, pl.ds(pl.multiple_of(pair * n, 128), n)]
        own, other = rows(a, b, y), rows(a, 1 - b, y)

        def block(at, full=full, cols=cols):
            return full.at[at, cols]

        def copy(src, dst, k, axis, to, i=i):
            return remote_to(src, dst, sends.at[i, k], recvs.at[i, k], axis, to)

        keep = pltpu.make_async_copy(mine, block(own), local.at[i])
        to_b = copy(theirs, block(own), 0, "b", 1 - b)
        y_own = copy(mine, block(own), 1, "y", 1 - y)
        y_other = copy(block(other), block(other), 2, "y", 1 - y)
        a_own, a_other, on_own, on_other = [], [], [], []
        for k in range(1, spans):
            to, source = lax.rem(a + k, spans), lax.rem(a + spans - k, spans)
            a_own.append(copy(mine, block(own), 4 * k - 1, "a", to))
            a_other.append(copy(block(other), block(other), 4 * k, "a", to))
            for b_at, which, out in ((b, 1, on_own), (1 - b, 2, on_other)):
                at = rows(source, b_at, y)
                out.append(copy(block(at), block(at), 4 * k + which, "y", 1 - y))

        def begin(keep=keep, now=(to_b, *a_own, y_own)):
            for item in now:
                item.start()
            keep.start()

        def hand(to_b=to_b, now=(*a_other, y_other)):
            to_b.wait_recv()
            for item in now:
                item.start()

        def hand_on(a_own=a_own, a_other=a_other, on_own=on_own, on_other=on_other):
            for got, item in zip(a_own + a_other, on_own + on_other):
                got.wait_recv()
                item.start()

        def end(keep=keep, arrive=(y_own, y_other, *on_own, *on_other), sent=(to_b, y_own, y_other, *a_own, *a_other, *on_own, *on_other)):
            for item in arrive:
                item.wait_recv()
            for item in sent:
                item.wait_send()
            keep.wait()

        first.append(begin)
        second.append(hand)
        third.append(hand_on)
        last.append(end)
    return first, second, third, last


def fetch_kernel(spans, tokens, cotangent, wq, wk, wv, wo, wg, wu, wf, tok_all, cot_all, fqkv, fo, fgu, ff, sends, recvs, local, *scratch):
    hc, fc = wq.shape[1] // 8, wg.shape[1] // 8
    meet_all(spans)
    fulls = [(fqkv, 0), (fqkv, hc), (fqkv, 2 * hc), (fo, 0), (fgu, 0), (fgu, fc), (ff, 0)]
    steps = fetch_steps(spans, [wq, wk, wv, wo, wg, wu, wf], fulls, sends, recvs, local)
    for step in steps[0]:
        step()
    gather_steps(tokens, tok_all, *scratch[:3])
    for step in steps[1]:
        step()
    gather_steps(cotangent, cot_all, *scratch[3:])
    for step in steps[2] + steps[3]:
        step()


def fetch(spans, tokens, cotangent, weights, number):
    rows, width = tokens.shape
    total = weights[0].shape[0] * 4 * spans
    hc, fc = weights[0].shape[1] // 8, weights[4].shape[1] // 8
    shapes = [(8, rows, width)] * 2 + [(total, 3 * hc), (total, hc), (total, 2 * fc), (total, fc)]
    dma = pltpu.SemaphoreType.DMA
    outs = pl.pallas_call(
        functools.partial(fetch_kernel, spans),
        out_shape=[jax.ShapeDtypeStruct(shape, BF16) for shape in shapes],
        in_specs=[any_space] * 9,
        out_specs=[any_space] * 6,
        scratch_shapes=[dma((7, 4 * spans - 1)), dma((7, 4 * spans - 1)), dma((7,))] + [dma((9,)), dma((9,)), dma] * 2,
        compiler_params=pltpu.CompilerParams(collective_id=number, has_side_effects=True),
    )(tokens, cotangent, *weights)
    return (outs[0].reshape(8 * rows, width), outs[1].reshape(8 * rows, width), *outs[2:])


def return_steps(spans, part, start, n, at, out, got_y, here, to_a, got_a, total, got_b, sends, recvs, local):
    a, y = lax.axis_index("a"), lax.axis_index("y")
    b, x, c = place()
    me, pair, x_me, x_pair = slot(b, x, c), slot(1 - b, x, c), slot(b, 1 - x, c), slot(1 - b, 1 - x, c)
    cols = pl.ds(start, n)
    count = here.shape[2]
    far = [lax.rem(a + k, spans) for k in range(1, spans)] + [a]

    def copy(src, dst, k, axis, to):
        return remote_to(src, dst, sends.at[k], recvs.at[k], axis, to)

    def place_in(member):
        return out.at[at, pl.ds(pl.multiple_of(member * n, 128), n)]

    to_y = [copy(part.at[f, :, 1 - y, at, cols], got_y.at[k], k, "y", 1 - y) for k, f in enumerate(far)]
    load = [pltpu.make_async_copy(part.at[f, :, y, at, cols], here.at[k], local.at[k]) for k, f in enumerate(far)]
    over_a = [copy(to_a.at[k], got_a.at[k], spans + k, "a", f) for k, f in enumerate(far[:-1])]
    base = 2 * spans - 1
    over_b = copy(total.at[1 - b], got_b, base, "b", 1 - b)
    x_own = copy(total.at[b], place_in(me), base + 1, "x", 1 - x)
    x_other = copy(got_b, place_in(pair), base + 2, "x", 1 - x)
    c_own = copy(total.at[b], place_in(me), base + 3, "c", 1 - c)
    c_other = copy(got_b, place_in(pair), base + 4, "c", 1 - c)
    c_x_own = copy(place_in(x_me), place_in(x_me), base + 5, "c", 1 - c)
    c_x_other = copy(place_in(x_pair), place_in(x_pair), base + 6, "c", 1 - c)
    keep_own = pltpu.make_async_copy(total.at[b], place_in(me), local.at[spans])
    keep_other = pltpu.make_async_copy(got_b, place_in(pair), local.at[spans + 1])

    def each(body):
        for half in range(2):
            in_rows(0, count, functools.partial(body, half))

    def begin():
        for send, item in zip(to_y, load):
            send.start()
            item.start()

    def across():
        for k in range(spans - 1):
            to_y[k].wait_recv()
            load[k].wait()

            def body(half, r, k=k):
                to_a[k, half, r, :] = (here[k, half, r, :].astype(F32) + got_y[k, half, r, :].astype(F32)).astype(BF16)

            each(body)
            over_a[k].start()

    def finish():
        to_y[spans - 1].wait_recv()
        load[spans - 1].wait()
        for item in over_a:
            item.wait_recv()

        def body(half, r):
            value = here[spans - 1, half, r, :].astype(F32) + got_y[spans - 1, half, r, :].astype(F32)
            for k in range(spans - 1):
                value = value + got_a[k, half, r, :].astype(F32)
            total[half, r, :] = value.astype(BF16)

        each(body)
        for item in (over_b, x_own, c_own, keep_own):
            item.start()

    def pass_on():
        over_b.wait_recv()
        for item in (x_other, c_other, keep_other):
            item.start()

    def share():
        x_own.wait_recv()
        c_x_own.start()
        x_other.wait_recv()
        c_x_other.start()

    def end():
        for item in (c_own, c_other, c_x_own, c_x_other):
            item.wait_recv()
        for item in (*to_y, *over_a, over_b, x_own, x_other, c_own, c_other, c_x_own, c_x_other):
            item.wait_send()
        keep_own.wait()
        keep_other.wait()

    return [begin, across, finish, pass_on, share, end]


def return_scratch(spans, count, n):
    dma = pltpu.SemaphoreType.DMA
    return [
        pltpu.VMEM((spans, 2, count, n), BF16),
        pltpu.VMEM((spans, 2, count, n), BF16),
        pltpu.VMEM((max(spans - 1, 1), 2, count, n), BF16),
        pltpu.VMEM((max(spans - 1, 1), 2, count, n), BF16),
        pltpu.VMEM((2, count, n), BF16),
        pltpu.VMEM((count, n), BF16),
        dma((2 * spans + 6,)),
        dma((2 * spans + 6,)),
        dma((spans + 2,)),
    ]


def return_kernel(spans, plan, n_in, n_out, *refs):
    parts, outs, scratch = refs[:n_in], refs[n_in : n_in + n_out], refs[n_in + n_out :]
    meet_all(spans)
    pieces = []
    for i, (part, start, n, out, first, count) in enumerate(plan):
        pieces.append(return_steps(spans, parts[part], start, n, pl.ds(first, count), outs[out], *scratch[9 * i : 9 * i + 9]))
    depth, total = len(pieces[0]), len(pieces)
    for wave in range(total + depth - 1):
        for stage in range(depth):
            if 0 <= wave - stage < total:
                pieces[wave - stage][stage]()


def return_gradients(spans, parts, plan, out_widths, number):
    count = parts[0].shape[0] // (4 * spans)
    shaped = [part.reshape(spans, 2, 2, count, part.shape[1]) for part in parts]
    scratch = []
    for _, _, n, _, _, r in plan:
        scratch += return_scratch(spans, r, n)
    return pl.pallas_call(
        functools.partial(return_kernel, spans, plan, len(parts), len(out_widths)),
        out_shape=[jax.ShapeDtypeStruct((count, n), BF16) for n in out_widths],
        in_specs=[any_space] * len(parts),
        out_specs=[any_space] * len(out_widths),
        scratch_shapes=scratch,
        compiler_params=pltpu.CompilerParams(collective_id=number, has_side_effects=True, vmem_limit_bytes=56 * MIB),
    )(*shaped)


def sum_kernel(spans, src, out, got, sends, recvs):
    meet_all(spans)
    a, y = lax.axis_index("a"), lax.axis_index("y")
    b, x, c = place()
    out[...] = src[...]
    step = 0
    for axis, other in (("c", 1 - c), ("x", 1 - x), ("b", 1 - b), ("y", 1 - y)):
        copy = remote_to(out, got.at[step], sends.at[step], recvs.at[step], axis, other)
        copy.start()
        copy.wait()
        out[...] += got[step]
        step += 1
    copies = []
    for k in range(1, spans):
        copies.append(remote_to(out, got.at[step], sends.at[step], recvs.at[step], "a", lax.rem(a + k, spans)))
        copies[-1].start()
        step += 1
    for copy in copies:
        copy.wait()
    out[...] += functools.reduce(jnp.add, [got[4 + k] for k in range(spans - 1)])


def sum_everywhere(spans, values, number):
    flat = jnp.concatenate([value.reshape(-1) for value in values])
    rows = -(-flat.shape[0] // 1024) * 8
    flat = jnp.pad(flat, (0, rows * 128 - flat.shape[0])).reshape(rows, 128)
    dma = pltpu.SemaphoreType.DMA
    summed = pl.pallas_call(
        functools.partial(sum_kernel, spans),
        out_shape=jax.ShapeDtypeStruct(flat.shape, F32),
        in_specs=[in_vmem],
        out_specs=in_vmem,
        scratch_shapes=[pltpu.VMEM((3 + spans, rows, 128), F32), dma((3 + spans,)), dma((3 + spans,))],
        compiler_params=pltpu.CompilerParams(collective_id=number, has_side_effects=True),
    )(flat).reshape(-1)
    out, at = [], 0
    for value in values:
        out.append(summed[at : at + value.size].reshape(value.shape))
        at += value.size
    return out


def per_device(
    tokens,
    w_query,
    w_key,
    w_value,
    w_attn_out,
    w_gate,
    w_up,
    w_ff_out,
    gain_attn,
    gain_ffn,
    rel_table,
    doc_lengths,
    cotangent,
):
    rows, width = tokens.shape
    n_buckets, heads_all = rel_table.shape
    heads = heads_all // 8
    hc = w_query.shape[1] // 8
    fc = w_gate.shape[1] // 8
    hd = hc // heads
    length = 4 * rows
    b, x, c = place()
    me = slot(b, x, c)

    other_docs = lax.ppermute(doc_lengths, "b", swap)
    ends = jnp.cumsum(in_order(b, doc_lengths[0], other_docs[0]), axis=1)
    positions = jnp.arange(length, dtype=jnp.int32)
    seg = jnp.sum((positions[None, :, None] >= ends[:, None, :]).astype(jnp.int32), axis=2)
    own_seg = lax.dynamic_slice(seg, (b, (x * 2 + c) * rows), (1, rows))[0]
    keep = (own_seg < doc_lengths.shape[1]).astype(F32)[:, None]
    offset = jnp.arange(-length, length, dtype=jnp.int32)
    distance = jnp.abs(offset)
    far = 8 + jnp.sum((distance[:, None] >= jnp.array(thresholds, jnp.int32)).astype(jnp.int32), axis=1)
    bucket = jnp.where(offset > 0, 16, 0) + jnp.where(distance < 8, distance, far)
    onehot = (jnp.arange(n_buckets, dtype=jnp.int32)[:, None] == bucket[None, :]).astype(F32)
    table = lax.dynamic_slice_in_dim(rel_table, me * heads, heads, 1)
    vec = lax.dot_general(table, onehot, (((0,), (0,)), ((), ())), precision=highest, preferred_element_type=F32)

    spans = lax.axis_size("a")
    weights = (w_query, w_key, w_value, w_attn_out, w_gate, w_up, w_ff_out)
    tok_all, cot_all, wqkv, wo, wgu, wf = fetch(spans, tokens, cotangent, weights, 0)

    xf_all = tok_all.astype(F32)
    inv_all = lax.rsqrt(jnp.mean(xf_all * xf_all, axis=-1, keepdims=True) + eps)
    n1 = (xf_all * inv_all * gain_attn).astype(BF16)
    qkv = flat_dot(n1, wqkv).astype(BF16)
    ctx, lse = attend(qkv, vec, seg, heads, hd)
    attn_part = dot_last(ctx, wo).astype(BF16)
    resid, n2 = middle(attn_part, tokens, keep, gain_ffn, 1)
    gate_up = flat_dot(n2, wgu)
    gate, up = gate_up[:, :fc], gate_up[:, fc:]
    activ, activ_back = jax.vjp(gelu_tanh, gate)
    hidden = (activ * up).astype(BF16)
    out_part = dot_last(hidden, wf).astype(BF16)
    out_f = resid + scatter_group(out_part, 3)

    dhidden = flat_dot(cot_all, wf)
    dgate = activ_back(dhidden * up)[0].astype(BF16)
    dup = (dhidden * activ).astype(BF16)
    dgu = jnp.concatenate([dgate, dup], axis=1)
    dn2_part = dot_last(dgu, wgu).astype(BF16)
    dresid, dattn, dgain_ffn = middle_back(dn2_part, resid, cotangent, keep, gain_ffn, 4)
    count = w_gate.shape[0]
    pieces = [(0, 0, fc, 0), (1, 0, fc, 1), (1, fc, fc, 2)]
    plan = [piece + (first, count // 2) for piece in pieces for first in (0, count // 2)]
    grad_f, grad_g, grad_u = return_gradients(
        spans, [dot_first(cot_all, hidden).astype(BF16), dot_first(n2, dgu).astype(BF16)], plan, [8 * fc] * 3, 6
    )
    dctx = flat_dot(dattn, wo).astype(BF16)
    part_o = dot_first(dattn, ctx).astype(BF16)
    dq, dk, dv, diag = attend_back(qkv, dctx, lse, vec, seg, heads, hd)
    dqkv = jnp.concatenate([dq, dk, dv], axis=1)
    dn1 = scatter_group(dot_last(dqkv, wqkv).astype(BF16), 5)
    plan = [(0, 0, hc, 0, 0, count)] + [(1, k * hc, hc, 1 + k, 0, count) for k in range(3)]
    grad_o, grad_q, grad_k, grad_v = return_gradients(
        spans, [part_o, dot_first(n1, dqkv).astype(BF16)], plan, [8 * hc] * 4, 7
    )

    xf = tokens.astype(F32)
    inv1 = lax.rsqrt(jnp.mean(xf * xf, axis=-1, keepdims=True) + eps)
    inner1 = dn1 * gain_attn
    grad_input = dresid + inv1 * inner1 - xf * inv1**3 * jnp.mean(inner1 * xf, axis=-1, keepdims=True)
    dgain_attn = jnp.sum(dn1 * xf * inv1, axis=0)

    order = jnp.roll(diag, length, axis=1)
    dtable_own = lax.dot_general(onehot, order, (((1,), (1,)), ((), ())), precision=highest, preferred_element_type=F32)
    dtable = lax.dynamic_update_slice(jnp.zeros((n_buckets, heads_all), F32), dtable_own, (0, me * heads))
    squares = jnp.stack([jnp.sum(resid * resid), jnp.sum(out_f * out_f)])
    dgain_attn, dgain_ffn, dtable, squares = sum_everywhere(spans, (dgain_attn, dgain_ffn, dtable, squares), 8)
    entries = rows * width * 16 * spans
    norms = jnp.sqrt(squares / entries)
    return (
        out_f.astype(BF16),
        grad_input,
        grad_q.astype(F32),
        grad_k.astype(F32),
        grad_v.astype(F32),
        grad_o.astype(F32),
        grad_g.astype(F32),
        grad_u.astype(F32),
        grad_f.astype(F32),
        dgain_attn,
        dgain_ffn,
        dtable,
        norms,
    )


def solution(mesh):
    owners, copies = mesh.shape["fsdp"], mesh.shape["rep"]
    finer = Mesh(mesh.devices.reshape(owners // 4, 2, 2, copies // 2, 2), ("a", "b", "y", "x", "c"))
    owner = ("a", "b", "y")
    piece = P(owner + ("x", "c"), None)
    shard = P(owner, None)
    return jax.shard_map(
        per_device,
        mesh=finer,
        in_specs=(piece,) + (shard,) * 7 + (P(), P(), P(), shard, piece),
        out_specs=(piece, piece) + (shard,) * 7 + (P(), P(), P(), P()),
        check_vma=False,
    )
```

```python
import functools

import jax
import jax.numpy as jnp
from jax import lax
from jax.experimental import pallas as pl
from jax.experimental.pallas import tpu as pltpu
from jax.sharding import Mesh
from jax.sharding import PartitionSpec as P

eps = 1e-06
thresholds = (12, 16, 23, 32, 46, 64, 91)
highest = lax.Precision.HIGHEST
F32 = jnp.float32
BF16 = jnp.bfloat16
far_below = -1e30
MESH = pl.DeviceIdType.MESH
swap = ((0, 1), (1, 0))
MIB = 1 << 20


def gelu_tanh(v):
    return jax.nn.gelu(v, approximate=True)


def flat_dot(left, right):
    return jnp.dot(left, right, preferred_element_type=F32)


def dot_last(left, right):
    return lax.dot_general(left, right, (((1,), (1,)), ((), ())), preferred_element_type=F32)


def dot_first(left, right):
    return lax.dot_general(left, right, (((0,), (0,)), ((), ())), preferred_element_type=F32)


def shear_bias(row, length):
    wide = jnp.broadcast_to(row, (length, 2 * length))
    return pltpu.roll(wide, length, 1, stride=1, stride_axis=0)[:, :length]


def attend_back_kernel(
    heads, hd, seqs, q_ref, k_ref, v_ref, d_ref, lse_ref, bias_ref, segc_ref, segr_ref, dq_ref, dk_ref, dv_ref, diag_ref, acc_ref
):
    length = q_ref.shape[0]
    step = pl.program_id(0)

    @pl.when(step == 0)
    def _():
        acc_ref[...] = jnp.zeros_like(acc_ref)

    same = segc_ref[0] == segr_ref[0]
    dqs, dks, dvs = [], [], []
    for h in range(heads):
        cols = slice(h * hd, (h + 1) * hd)
        q, k, v, d = q_ref[:, cols], k_ref[:, cols], v_ref[:, cols], d_ref[:, cols]
        scores = jnp.where(same, dot_last(q, k) + bias_ref[h], far_below)
        probs = jnp.exp(scores - lse_ref[:, h : h + 1])
        dprobs = dot_last(d, v)
        dvs.append(dot_first(probs.astype(BF16), d).astype(BF16))
        product = probs * dprobs
        dscores = product - probs * jnp.sum(product, axis=1, keepdims=True)
        acc_ref[h] += dscores
        dlogits = dscores.astype(BF16)
        dqs.append(flat_dot(dlogits, k).astype(BF16))
        dks.append(dot_first(dlogits, q).astype(BF16))
    dq_ref[...] = jnp.concatenate(dqs, axis=1)
    dk_ref[...] = jnp.concatenate(dks, axis=1)
    dv_ref[...] = jnp.concatenate(dvs, axis=1)

    @pl.when(step == seqs - 1)
    def _():
        def add(g, total):
            at = pl.multiple_of(g * 8, 8)
            rows = acc_ref[:, pl.ds(at, 8), :].reshape(heads * 8, length)
            wide = jnp.concatenate([rows, jnp.zeros_like(rows)], axis=1)
            return total + pltpu.roll(wide, 2 * length - g * 8, 1)

        total = lax.fori_loop(0, length // 8, add, jnp.zeros((heads * 8, 2 * length), F32))
        total = total.reshape(heads, 8, 2 * length)
        out = total[:, 0, :]
        for r in range(1, 8):
            out = out + pltpu.roll(total[:, r, :], 2 * length - r, 1)
        diag_ref[...] = out


def attend_back(qkv, dctx, lse, bias, seg, heads, hd):
    rows = qkv.shape[0]
    seqs, length = seg.shape
    wide = heads * hd

    def block(n):
        return pl.BlockSpec((length, wide), lambda i: (i, n))

    whole = pl.BlockSpec((heads, 2 * length), lambda i: (0, 0))
    return pl.pallas_call(
        functools.partial(attend_back_kernel, heads, hd, seqs),
        grid=(seqs,),
        in_specs=[
            block(0),
            block(1),
            block(2),
            block(0),
            pl.BlockSpec((length, heads), lambda i: (i, 0)),
            pl.BlockSpec((heads, length, length), lambda i: (0, 0, 0)),
            pl.BlockSpec((1, length, 1), lambda i: (i, 0, 0)),
            pl.BlockSpec((1, 1, length), lambda i: (i, 0, 0)),
        ],
        out_specs=[block(0), block(0), block(0), whole],
        out_shape=[jax.ShapeDtypeStruct((rows, wide), BF16)] * 3 + [jax.ShapeDtypeStruct((heads, 2 * length), F32)],
        scratch_shapes=[pltpu.VMEM((heads, length, length), F32)],
        compiler_params=pltpu.CompilerParams(vmem_limit_bytes=56 * MIB),
        cost_estimate=pl.CostEstimate(flops=20_000_000_000, bytes_accessed=8_000_000, transcendentals=2_000_000),
    )(qkv, qkv, qkv, dctx, lse, bias, seg[:, :, None], seg[:, None, :])


def place():
    return lax.axis_index("b"), lax.axis_index("x"), lax.axis_index("c")


def slot(b, x, c):
    return b * 4 + x * 2 + c


def meet():
    b, x, c = place()
    barrier = pltpu.get_barrier_semaphore()
    for axis, other in (("b", 1 - b), ("x", 1 - x), ("c", 1 - c)):
        pl.semaphore_signal(barrier, inc=1, device_id={axis: other}, device_id_type=MESH)
    pl.semaphore_wait(barrier, 3)


def remote(src, dst, sends, recvs, n, axis):
    return pltpu.make_async_remote_copy(
        src_ref=src,
        dst_ref=dst,
        send_sem=sends.at[n],
        recv_sem=recvs.at[n],
        device_id={axis: 1 - lax.axis_index(axis)},
        device_id_type=MESH,
    )


def gather_parts(src, out, sends, recvs, local):
    b, x, c = place()
    rows = src.shape[0]
    half = rows // 2
    top, low = pl.ds(0, half), pl.ds(half, half)
    own, at_x, at_b, at_d = slot(b, x, c), slot(b, 1 - x, c), slot(1 - b, x, c), slot(1 - b, 1 - x, c)
    copies = [
        remote(src, out.at[own], sends, recvs, 0, "x"),
        remote(src, out.at[own], sends, recvs, 1, "b"),
        remote(out.at[at_b, top], out.at[at_b, top], sends, recvs, 2, "x"),
        remote(out.at[at_x, low], out.at[at_x, low], sends, recvs, 3, "b"),
        remote(src, out.at[own], sends, recvs, 4, "c"),
        remote(out.at[at_x], out.at[at_x], sends, recvs, 5, "c"),
        remote(out.at[at_b], out.at[at_b], sends, recvs, 6, "c"),
        remote(out.at[at_d, top], out.at[at_d, top], sends, recvs, 7, "c"),
        remote(out.at[at_d, low], out.at[at_d, low], sends, recvs, 8, "c"),
    ]
    keep = pltpu.make_async_copy(src, out.at[own], local)

    def begin():
        for n in (0, 1, 4):
            copies[n].start()
        keep.start()

    def from_x():
        copies[0].wait_recv()
        copies[3].start()
        copies[5].start()

    def from_b():
        copies[1].wait_recv()
        copies[2].start()
        copies[6].start()

    def from_both():
        copies[2].wait_recv()
        copies[7].start()
        copies[3].wait_recv()
        copies[8].start()

    def end():
        for n in (4, 5, 6, 7, 8):
            copies[n].wait_recv()
        for copy in copies:
            copy.wait_send()
        keep.wait()

    return [begin, from_x, from_b, from_both, end]


def gather_steps(src, out, sends, recvs, local):
    for step in gather_parts(src, out, sends, recvs, local):
        step()


def in_rows(first, count, body, chunk=16):
    def step(i, _):
        body(pl.ds(pl.multiple_of(first + i * chunk, chunk), chunk))
        return 0

    lax.fori_loop(0, count // chunk, step, 0)


def scatter_steps(parts, acc, sib, out, diag, last, sends, recvs, mine=None, local=None):
    b, x, c = place()
    rows = parts.shape[1]
    half = rows // 2
    top, low = pl.ds(0, half), pl.ds(half, half)
    seats = [(b, x), (b, 1 - x), (1 - b, x), (1 - b, 1 - x)]
    to_core = [remote(parts.at[slot(*seats[q], 1 - c)], sib.at[q], sends, recvs, q, "c") for q in range(4)]
    here = []
    if mine is not None:
        here = [pltpu.make_async_copy(parts.at[slot(*seats[q], c)], mine.at[q], local.at[q]) for q in range(4)]
    for q in (3, 1, 2, 0):
        to_core[q].start()
        for copy in here[q : q + 1]:
            copy.start()
    diag_x = remote(out.at[2, top], diag.at[0], sends, recvs, 4, "x")
    diag_b = remote(out.at[2, low], diag.at[1], sends, recvs, 5, "b")
    x_top = remote(out.at[0, top], last.at[0, top], sends, recvs, 6, "x")
    x_low = remote(out.at[0, low], last.at[0, low], sends, recvs, 7, "x")
    b_top = remote(out.at[1, top], last.at[1, top], sends, recvs, 8, "b")
    b_low = remote(out.at[1, low], last.at[1, low], sends, recvs, 9, "b")

    def ready(q):
        to_core[q].wait_recv()
        for copy in here[q : q + 1]:
            copy.wait()

    def both(q, at):
        held = parts[slot(*seats[q], c), at, :] if mine is None else mine[q, at, :]
        return held.astype(F32) + sib[q, at, :].astype(F32)

    def put(n, q, first):
        def body(at):
            out[n, at, :] = both(q, at).astype(BF16)

        in_rows(first, half, body)

    ready(3)
    put(2, 3, 0)
    diag_x.start()
    put(2, 3, half)
    diag_b.start()
    ready(1)
    put(0, 1, 0)
    x_top.start()
    ready(2)
    put(1, 2, half)
    b_low.start()
    ready(0)

    def own(at):
        acc[at, :] = both(0, at)

    in_rows(0, rows, own)
    diag_b.wait_recv()

    def add_low(i, _):
        at = pl.ds(pl.multiple_of(half + i * 16, 16), 16)
        out[0, at, :] = (both(1, at) + diag[1, pl.ds(pl.multiple_of(i * 16, 16), 16), :].astype(F32)).astype(BF16)
        return 0

    lax.fori_loop(0, half // 16, add_low, 0)
    x_low.start()
    diag_x.wait_recv()

    def add_top(i, _):
        at = pl.ds(pl.multiple_of(i * 16, 16), 16)
        out[1, at, :] = (both(2, at) + diag[0, at, :].astype(F32)).astype(BF16)
        return 0

    lax.fori_loop(0, half // 16, add_top, 0)
    b_top.start()
    for copy in (x_top, b_low, x_low, b_top):
        copy.wait_recv()
    for copy in to_core + [diag_x, diag_b, x_top, x_low, b_top, b_low]:
        copy.wait_send()

    def finish(at):
        acc[at, :] += last[0, at, :].astype(F32) + last[1, at, :].astype(F32)

    in_rows(0, rows, finish)


def scatter_scratch(rows, width, copied=True):
    scratch = [
        pltpu.VMEM((4, rows, width), BF16),
        pltpu.VMEM((3, rows, width), BF16),
        pltpu.VMEM((2, rows // 2, width), BF16),
        pltpu.VMEM((2, rows, width), BF16),
        pltpu.SemaphoreType.DMA((10,)),
        pltpu.SemaphoreType.DMA((10,)),
    ]
    if copied:
        scratch += [pltpu.VMEM((4, rows, width), BF16), pltpu.SemaphoreType.DMA((4,))]
    return scratch


def scatter_kernel(parts, acc, *scratch):
    meet()
    scatter_steps(parts, acc, *scratch)


any_space = pl.BlockSpec(memory_space=pl.ANY)
in_vmem = pl.BlockSpec(memory_space=pltpu.VMEM)


def scatter_group(parts, number):
    rows, width = parts.shape[0] // 8, parts.shape[1]
    return pl.pallas_call(
        scatter_kernel,
        out_shape=jax.ShapeDtypeStruct((rows, width), F32),
        in_specs=[any_space],
        out_specs=in_vmem,
        scratch_shapes=scatter_scratch(rows, width),
        compiler_params=pltpu.CompilerParams(collective_id=number, has_side_effects=True, vmem_limit_bytes=32 * MIB),
        cost_estimate=pl.CostEstimate(flops=0, bytes_accessed=80_000_000, transcendentals=0),
    )(parts.reshape(8, rows, width))


def middle_back_kernel(
    parts, resid, cotangent, keep, gain, dresid, dattn_all, dgain, acc, dattn, sends2, recvs2, local2, *scratch
):
    meet()
    scatter_steps(parts, acc, *scratch)
    dgain[...] = jnp.zeros_like(dgain)

    def body(at):
        value, dn2 = resid[at, :], acc[at, :]
        inv = lax.rsqrt(jnp.mean(value * value, axis=-1, keepdims=True) + eps)
        inner = dn2 * gain[...]
        grad = (
            cotangent[at, :].astype(F32)
            + inv * inner
            - value * (inv * inv * inv * jnp.mean(inner * value, axis=-1, keepdims=True))
        )
        dresid[at, :] = grad
        dgain[...] += jnp.sum(dn2 * value * inv, axis=0, keepdims=True)
        dattn[at, :] = (keep[at, :] * grad).astype(BF16)

    in_rows(0, resid.shape[0], body)
    gather_steps(dattn, dattn_all, sends2, recvs2, local2)


def middle_back(parts, resid, cotangent, keep, gain, number):
    rows, width = resid.shape
    dresid, dattn_all, dgain = pl.pallas_call(
        middle_back_kernel,
        out_shape=[
            jax.ShapeDtypeStruct((rows, width), F32),
            jax.ShapeDtypeStruct((8, rows, width), BF16),
            jax.ShapeDtypeStruct((1, width), F32),
        ],
        in_specs=[any_space, in_vmem, in_vmem, in_vmem, in_vmem],
        out_specs=[in_vmem, any_space, in_vmem],
        scratch_shapes=[
            pltpu.VMEM((rows, width), F32),
            pltpu.VMEM((rows, width), BF16),
            pltpu.SemaphoreType.DMA((9,)),
            pltpu.SemaphoreType.DMA((9,)),
            pltpu.SemaphoreType.DMA,
        ]
        + scatter_scratch(rows, width),
        compiler_params=pltpu.CompilerParams(collective_id=number, has_side_effects=True, vmem_limit_bytes=32 * MIB),
        cost_estimate=pl.CostEstimate(flops=0, bytes_accessed=160_000_000, transcendentals=0),
    )(parts.reshape(8, rows, width), resid, cotangent, keep, gain[None, :])
    return dresid, dattn_all.reshape(8 * rows, width), dgain[0]


def in_order(index, own, other):
    first = index == 0
    return jnp.stack([jnp.where(first, own, other), jnp.where(first, other, own)])


def remote_to(src, dst, send, recv, axis, to):
    return pltpu.make_async_remote_copy(
        src_ref=src, dst_ref=dst, send_sem=send, recv_sem=recv, device_id={axis: to}, device_id_type=MESH
    )


def meet_all(spans):
    a, y = lax.axis_index("a"), lax.axis_index("y")
    b, x, c = place()
    barrier = pltpu.get_barrier_semaphore()
    others = [("b", 1 - b), ("x", 1 - x), ("c", 1 - c), ("y", 1 - y)] + [("a", lax.rem(a + k, spans)) for k in range(1, spans)]
    for axis, other in others:
        pl.semaphore_signal(barrier, inc=1, device_id={axis: other}, device_id_type=MESH)
    pl.semaphore_wait(barrier, len(others))


def fetch_parts(spans, shards, fulls, sends, recvs, local):
    a, y = lax.axis_index("a"), lax.axis_index("y")
    b, x, c = place()
    me, pair = slot(b, x, c), slot(1 - b, x, c)
    count = shards[0].shape[0]

    def rows(at_a, at_b, at_y):
        return pl.ds(pl.multiple_of((at_a * 4 + at_b * 2 + at_y) * count, count), count)

    weights = []
    for i, (shard, (full, start)) in enumerate(zip(shards, fulls)):
        n = shard.shape[1] // 8
        cols = pl.ds(start, n)
        mine = shard.at[:, pl.ds(pl.multiple_of(me * n, 128), n)]
        theirs = shard.at[:, pl.ds(pl.multiple_of(pair * n, 128), n)]
        own, other = rows(a, b, y), rows(a, 1 - b, y)

        def block(at, full=full, cols=cols):
            return full.at[at, cols]

        def copy(src, dst, k, axis, to, i=i):
            return remote_to(src, dst, sends.at[i, k], recvs.at[i, k], axis, to)

        copies = {
            "keep": pltpu.make_async_copy(mine, block(own), local.at[i]),
            "b": copy(theirs, block(own), 0, "b", 1 - b),
            "y": copy(mine, block(own), 1, "y", 1 - y),
            "y_pair": copy(block(other), block(other), 2, "y", 1 - y),
            "a": [],
            "a_pair": [],
            "on": [],
            "on_pair": [],
        }
        for k in range(1, spans):
            to, source = lax.rem(a + k, spans), lax.rem(a + spans - k, spans)
            copies["a"].append(copy(mine, block(own), 4 * k - 1, "a", to))
            copies["a_pair"].append(copy(block(other), block(other), 4 * k, "a", to))
            far, far_pair = block(rows(source, b, y)), block(rows(source, 1 - b, y))
            copies["on"].append(copy(far, far, 4 * k + 1, "y", 1 - y))
            copies["on_pair"].append(copy(far_pair, far_pair, 4 * k + 2, "y", 1 - y))
        weights.append(copies)
    return weights


def start_all(copies):
    for copy in copies:
        copy.start()


def pair_in(copies):
    copies["b"].wait_recv()
    start_all([*copies["a_pair"], copies["y_pair"]])


def hand_on(copies, came, on):
    for got, copy in zip(copies[came], copies[on]):
        got.wait_recv()
        copy.start()


def weight_in(copies):
    copies["keep"].wait()
    for copy in (copies["y"], copies["y_pair"], *copies["on"], *copies["on_pair"]):
        copy.wait_recv()


def weight_out(copies):
    for copy in (copies["b"], copies["y"], copies["y_pair"]):
        copy.wait_send()
    for kind in ("a", "a_pair", "on", "on_pair"):
        for copy in copies[kind]:
            copy.wait_send()


def forward_kernel(
    spans, heads, hd, tokens, cotangent, wq, wk, wv, wo, wg, wu, wf, keep, gain1, gain2, vec, segc, segr,
    cot_all, n2_all, n1_out, bias_out, fqkv, fo, fgu, ff, qkv, ctx, lse, resid,
    tok_all, n1, vqkv, vo, bias, parts, acc, n2, sends, recvs, local, moves, *scratch
):
    hc, fc = wq.shape[1] // 8, wg.shape[1] // 8
    rows, width = tok_all.shape[1:]
    length = segr.shape[2]
    meet_all(spans)
    fulls = [(fqkv, 0), (fqkv, hc), (fqkv, 2 * hc), (fo, 0), (fgu, 0), (fgu, fc), (ff, 0)]
    weights = fetch_parts(spans, [wq, wk, wv, wo, wg, wu, wf], fulls, sends, recvs, local)
    small, large = weights[:4], weights[4:]
    tok = gather_parts(tokens, tok_all, *scratch[0:3])
    cot = gather_parts(cotangent, cot_all, *scratch[3:6])
    n2s = gather_parts(n2, n2_all, *scratch[6:9])

    tok[0]()
    for w in weights:
        w["b"].start()
        w["keep"].start()
    for w in small:
        start_all([*w["a"], w["y"]])
    large[0]["y"].start()
    for h in range(heads):
        bias[h] = shear_bias(vec[h : h + 1, :], length)
    bias_move = pltpu.make_async_copy(bias, bias_out, moves.at[0])
    bias_move.start()
    tok[1]()
    for w in small:
        pair_in(w)
    for w in large:
        start_all(w["a"])
    tok[2]()
    for w in small:
        hand_on(w, "a", "on")
    for w in large[1:]:
        w["y"].start()
    tok[3]()
    tok[4]()

    def norm(i, _):
        m = i // (rows // 16)
        at = pl.multiple_of(lax.rem(i, rows // 16) * 16, 16)
        value = tok_all[m, pl.ds(at, 16), :].astype(F32)
        inv = lax.rsqrt(jnp.mean(value * value, axis=-1, keepdims=True) + eps)
        n1[pl.ds(pl.multiple_of(i * 16, 16), 16), :] = (value * inv * gain1[...]).astype(BF16)
        return 0

    lax.fori_loop(0, 8 * rows // 16, norm, 0)
    n1_move = pltpu.make_async_copy(n1, n1_out, moves.at[1])
    n1_move.start()
    for w in small:
        hand_on(w, "a_pair", "on_pair")
    for w in small[:3]:
        weight_in(w)
    load = pltpu.make_async_copy(fqkv, vqkv, moves.at[2])
    load.start()
    load.wait()

    def project(i, _):
        at = pl.ds(pl.multiple_of(i * 128, 128), 128)
        qkv[at, :] = flat_dot(n1[at, :], vqkv[...]).astype(BF16)
        return 0

    lax.fori_loop(0, 8 * rows // 128, project, 0)
    cot[0]()
    for w in large:
        pair_in(w)
    for s in range(2):
        at = slice(s * length, (s + 1) * length)
        same = segc[s] == segr[s]
        for h in range(heads):
            q_cols, k_cols, v_cols = (slice(k * hc + h * hd, k * hc + (h + 1) * hd) for k in range(3))
            scores = jnp.where(same, dot_last(qkv[at, q_cols], qkv[at, k_cols]) + bias[h], far_below)
            top = jnp.max(scores, axis=1, keepdims=True)
            expo = jnp.exp(scores - top)
            total = jnp.sum(expo, axis=1, keepdims=True)
            probs = (expo * (1.0 / total)).astype(BF16)
            ctx[at, q_cols] = flat_dot(probs, qkv[at, v_cols]).astype(BF16)
            lse[at, h : h + 1] = top + jnp.log(total)
        if s == 0:
            hand_on(large[0], "a", "on")
            cot[1]()
    weight_in(small[3])
    load = pltpu.make_async_copy(fo, vo, moves.at[3])
    load.start()
    load.wait()

    def spread(m, _):
        at = pl.ds(pl.multiple_of(m * rows, rows), rows)
        parts[m] = dot_last(ctx[at, :], vo[...]).astype(BF16)
        return 0

    lax.fori_loop(0, 8, spread, 0)
    scatter_steps(parts, acc, *scratch[9:])

    def residual(at):
        value = tokens_rows(tokens, tok_all, at) + keep[at, :] * acc[at, :]
        resid[at, :] = value
        inv = lax.rsqrt(jnp.mean(value * value, axis=-1, keepdims=True) + eps)
        n2[at, :] = (value * inv * gain2[...]).astype(BF16)

    in_rows(0, rows, residual)
    n2s[0]()
    hand_on(large[1], "a", "on")
    n2s[1]()
    n2s[2]()
    n2s[3]()
    cot[2]()
    cot[3]()
    hand_on(large[2], "a", "on")
    for w in large:
        hand_on(w, "a_pair", "on_pair")
    n2s[4]()
    cot[4]()
    for w in large:
        weight_in(w)
    for w in weights:
        weight_out(w)
    n1_move.wait()
    bias_move.wait()


def tokens_rows(tokens, tok_all, at):
    return tok_all[slot(*place()), at, :].astype(F32)


def forward(spans, tokens, cotangent, weights, keep, gain1, gain2, vec, seg, hd, number):
    rows, width = tokens.shape
    heads, length = vec.shape[0], seg.shape[1]
    total = weights[0].shape[0] * 4 * spans
    hc, fc = weights[0].shape[1] // 8, weights[4].shape[1] // 8
    dma = pltpu.SemaphoreType.DMA
    shape = jax.ShapeDtypeStruct
    outs = pl.pallas_call(
        functools.partial(forward_kernel, spans, heads, hd),
        out_shape=[
            shape((8, rows, width), BF16),
            shape((8, rows, width), BF16),
            shape((8 * rows, width), BF16),
            shape((heads, length, length), F32),
            shape((total, 3 * hc), BF16),
            shape((total, hc), BF16),
            shape((total, 2 * fc), BF16),
            shape((total, fc), BF16),
            shape((8 * rows, 3 * hc), BF16),
            shape((8 * rows, hc), BF16),
            shape((8 * rows, heads), F32),
            shape((rows, width), F32),
        ],
        in_specs=[any_space] * 9 + [in_vmem] * 6,
        out_specs=[any_space] * 8 + [in_vmem] * 4,
        scratch_shapes=[
            pltpu.VMEM((8, rows, width), BF16),
            pltpu.VMEM((8 * rows, width), BF16),
            pltpu.VMEM((total, 3 * hc), BF16),
            pltpu.VMEM((total, hc), BF16),
            pltpu.VMEM((heads, length, length), F32),
            pltpu.VMEM((8, rows, width), BF16),
            pltpu.VMEM((rows, width), F32),
            pltpu.VMEM((rows, width), BF16),
            dma((7, 4 * spans - 1)),
            dma((7, 4 * spans - 1)),
            dma((7,)),
            dma((4,)),
        ]
        + [dma((9,)), dma((9,)), dma] * 3
        + scatter_scratch(rows, width, False),
        compiler_params=pltpu.CompilerParams(collective_id=number, has_side_effects=True, vmem_limit_bytes=56 * MIB),
    )(tokens, cotangent, *weights, keep, gain1[None, :], gain2[None, :], vec, seg[:, :, None], seg[:, None, :])
    return (outs[0].reshape(8 * rows, width), outs[1].reshape(8 * rows, width), *outs[2:])


def return_steps(spans, part, start, n, at, out, got_y, here, to_a, got_a, total, got_b, sends, recvs, local):
    a, y = lax.axis_index("a"), lax.axis_index("y")
    b, x, c = place()
    me, pair, x_me, x_pair = slot(b, x, c), slot(1 - b, x, c), slot(b, 1 - x, c), slot(1 - b, 1 - x, c)
    cols = pl.ds(start, n)
    count = here.shape[2]
    far = [lax.rem(a + k, spans) for k in range(1, spans)] + [a]

    def copy(src, dst, k, axis, to):
        return remote_to(src, dst, sends.at[k], recvs.at[k], axis, to)

    def place_in(member):
        return out.at[at, pl.ds(pl.multiple_of(member * n, 128), n)]

    to_y = [copy(part.at[f, :, 1 - y, at, cols], got_y.at[k], k, "y", 1 - y) for k, f in enumerate(far)]
    load = [pltpu.make_async_copy(part.at[f, :, y, at, cols], here.at[k], local.at[k]) for k, f in enumerate(far)]
    over_a = [copy(to_a.at[k], got_a.at[k], spans + k, "a", f) for k, f in enumerate(far[:-1])]
    base = 2 * spans - 1
    over_b = copy(total.at[1 - b], got_b, base, "b", 1 - b)
    x_own = copy(total.at[b], place_in(me), base + 1, "x", 1 - x)
    x_other = copy(got_b, place_in(pair), base + 2, "x", 1 - x)
    c_own = copy(total.at[b], place_in(me), base + 3, "c", 1 - c)
    c_other = copy(got_b, place_in(pair), base + 4, "c", 1 - c)
    c_x_own = copy(place_in(x_me), place_in(x_me), base + 5, "c", 1 - c)
    c_x_other = copy(place_in(x_pair), place_in(x_pair), base + 6, "c", 1 - c)
    keep_own = pltpu.make_async_copy(total.at[b], place_in(me), local.at[spans])
    keep_other = pltpu.make_async_copy(got_b, place_in(pair), local.at[spans + 1])

    def each(body):
        for half in range(2):
            in_rows(0, count, functools.partial(body, half))

    def begin():
        for send, item in zip(to_y, load):
            send.start()
            item.start()

    def across():
        for k in range(spans - 1):
            to_y[k].wait_recv()
            load[k].wait()

            def body(half, r, k=k):
                to_a[k, half, r, :] = (here[k, half, r, :].astype(F32) + got_y[k, half, r, :].astype(F32)).astype(BF16)

            each(body)
            over_a[k].start()

    def finish():
        to_y[spans - 1].wait_recv()
        load[spans - 1].wait()
        for item in over_a:
            item.wait_recv()

        def body(half, r):
            value = here[spans - 1, half, r, :].astype(F32) + got_y[spans - 1, half, r, :].astype(F32)
            for k in range(spans - 1):
                value = value + got_a[k, half, r, :].astype(F32)
            total[half, r, :] = value.astype(BF16)

        each(body)
        for item in (over_b, x_own, c_own, keep_own):
            item.start()

    def pass_on():
        over_b.wait_recv()
        for item in (x_other, c_other, keep_other):
            item.start()

    def share():
        x_own.wait_recv()
        c_x_own.start()
        x_other.wait_recv()
        c_x_other.start()

    def end():
        for item in (c_own, c_other, c_x_own, c_x_other):
            item.wait_recv()
        for item in (*to_y, *over_a, over_b, x_own, x_other, c_own, c_other, c_x_own, c_x_other):
            item.wait_send()
        keep_own.wait()
        keep_other.wait()

    return [begin, across, finish, pass_on, share, end]


def return_scratch(spans, count, n):
    dma = pltpu.SemaphoreType.DMA
    return [
        pltpu.VMEM((spans, 2, count, n), BF16),
        pltpu.VMEM((spans, 2, count, n), BF16),
        pltpu.VMEM((max(spans - 1, 1), 2, count, n), BF16),
        pltpu.VMEM((max(spans - 1, 1), 2, count, n), BF16),
        pltpu.VMEM((2, count, n), BF16),
        pltpu.VMEM((count, n), BF16),
        dma((2 * spans + 6,)),
        dma((2 * spans + 6,)),
        dma((spans + 2,)),
    ]


def return_kernel(spans, plan, n_in, n_out, *refs):
    parts, outs, scratch = refs[:n_in], refs[n_in : n_in + n_out], refs[n_in + n_out :]
    meet_all(spans)
    pieces = []
    for i, (part, start, n, out, first, count) in enumerate(plan):
        pieces.append(return_steps(spans, parts[part], start, n, pl.ds(first, count), outs[out], *scratch[9 * i : 9 * i + 9]))
    depth, total = len(pieces[0]), len(pieces)
    for wave in range(total + depth - 1):
        for stage in range(depth):
            if 0 <= wave - stage < total:
                pieces[wave - stage][stage]()


def return_gradients(spans, parts, plan, out_widths, number):
    count = parts[0].shape[0] // (4 * spans)
    shaped = [part.reshape(spans, 2, 2, count, part.shape[1]) for part in parts]
    scratch = []
    for _, _, n, _, _, r in plan:
        scratch += return_scratch(spans, r, n)
    return pl.pallas_call(
        functools.partial(return_kernel, spans, plan, len(parts), len(out_widths)),
        out_shape=[jax.ShapeDtypeStruct((count, n), BF16) for n in out_widths],
        in_specs=[any_space] * len(parts),
        out_specs=[any_space] * len(out_widths),
        scratch_shapes=scratch,
        compiler_params=pltpu.CompilerParams(collective_id=number, has_side_effects=True, vmem_limit_bytes=56 * MIB),
    )(*shaped)


def sum_kernel(spans, src, out, got, sends, recvs):
    meet_all(spans)
    a, y = lax.axis_index("a"), lax.axis_index("y")
    b, x, c = place()
    out[...] = src[...]
    step = 0
    for axis, other in (("c", 1 - c), ("x", 1 - x), ("b", 1 - b), ("y", 1 - y)):
        copy = remote_to(out, got.at[step], sends.at[step], recvs.at[step], axis, other)
        copy.start()
        copy.wait()
        out[...] += got[step]
        step += 1
    copies = []
    for k in range(1, spans):
        copies.append(remote_to(out, got.at[step], sends.at[step], recvs.at[step], "a", lax.rem(a + k, spans)))
        copies[-1].start()
        step += 1
    for copy in copies:
        copy.wait()
    out[...] += functools.reduce(jnp.add, [got[4 + k] for k in range(spans - 1)])


def sum_everywhere(spans, values, number):
    flat = jnp.concatenate([value.reshape(-1) for value in values])
    rows = -(-flat.shape[0] // 1024) * 8
    flat = jnp.pad(flat, (0, rows * 128 - flat.shape[0])).reshape(rows, 128)
    dma = pltpu.SemaphoreType.DMA
    summed = pl.pallas_call(
        functools.partial(sum_kernel, spans),
        out_shape=jax.ShapeDtypeStruct(flat.shape, F32),
        in_specs=[in_vmem],
        out_specs=in_vmem,
        scratch_shapes=[pltpu.VMEM((3 + spans, rows, 128), F32), dma((3 + spans,)), dma((3 + spans,))],
        compiler_params=pltpu.CompilerParams(collective_id=number, has_side_effects=True),
    )(flat).reshape(-1)
    out, at = [], 0
    for value in values:
        out.append(summed[at : at + value.size].reshape(value.shape))
        at += value.size
    return out


def per_device(
    tokens,
    w_query,
    w_key,
    w_value,
    w_attn_out,
    w_gate,
    w_up,
    w_ff_out,
    gain_attn,
    gain_ffn,
    rel_table,
    doc_lengths,
    cotangent,
):
    rows, width = tokens.shape
    n_buckets, heads_all = rel_table.shape
    heads = heads_all // 8
    hc = w_query.shape[1] // 8
    fc = w_gate.shape[1] // 8
    hd = hc // heads
    length = 4 * rows
    b, x, c = place()
    me = slot(b, x, c)

    other_docs = lax.ppermute(doc_lengths, "b", swap)
    ends = jnp.cumsum(in_order(b, doc_lengths[0], other_docs[0]), axis=1)
    positions = jnp.arange(length, dtype=jnp.int32)
    seg = jnp.sum((positions[None, :, None] >= ends[:, None, :]).astype(jnp.int32), axis=2)
    own_seg = lax.dynamic_slice(seg, (b, (x * 2 + c) * rows), (1, rows))[0]
    keep = (own_seg < doc_lengths.shape[1]).astype(F32)[:, None]
    offset = jnp.arange(-length, length, dtype=jnp.int32)
    distance = jnp.abs(offset)
    far = 8 + jnp.sum((distance[:, None] >= jnp.array(thresholds, jnp.int32)).astype(jnp.int32), axis=1)
    bucket = jnp.where(offset > 0, 16, 0) + jnp.where(distance < 8, distance, far)
    onehot = (jnp.arange(n_buckets, dtype=jnp.int32)[:, None] == bucket[None, :]).astype(F32)
    table = lax.dynamic_slice_in_dim(rel_table, me * heads, heads, 1)
    vec = lax.dot_general(table, onehot, (((0,), (0,)), ((), ())), precision=highest, preferred_element_type=F32)

    spans = lax.axis_size("a")
    weights = (w_query, w_key, w_value, w_attn_out, w_gate, w_up, w_ff_out)
    cot_all, n2, n1, bias, wqkv, wo, wgu, wf, qkv, ctx, lse, resid = forward(
        spans, tokens, cotangent, weights, keep, gain_attn, gain_ffn, vec, seg, hd, 0
    )
    gate_up = flat_dot(n2, wgu)
    gate, up = gate_up[:, :fc], gate_up[:, fc:]
    activ, activ_back = jax.vjp(gelu_tanh, gate)
    hidden = (activ * up).astype(BF16)
    out_part = dot_last(hidden, wf).astype(BF16)
    out_f = resid + scatter_group(out_part, 3)

    dhidden = flat_dot(cot_all, wf)
    dgate = activ_back(dhidden * up)[0].astype(BF16)
    dup = (dhidden * activ).astype(BF16)
    dgu = jnp.concatenate([dgate, dup], axis=1)
    dn2_part = dot_last(dgu, wgu).astype(BF16)
    dresid, dattn, dgain_ffn = middle_back(dn2_part, resid, cotangent, keep, gain_ffn, 4)
    count = w_gate.shape[0]
    pieces = [(0, 0, fc, 0), (1, 0, fc, 1), (1, fc, fc, 2)]
    plan = [piece + (first, count // 2) for piece in pieces for first in (0, count // 2)]
    grad_f, grad_g, grad_u = return_gradients(
        spans, [dot_first(cot_all, hidden).astype(BF16), dot_first(n2, dgu).astype(BF16)], plan, [8 * fc] * 3, 6
    )
    dctx = flat_dot(dattn, wo).astype(BF16)
    part_o = dot_first(dattn, ctx).astype(BF16)
    dq, dk, dv, diag = attend_back(qkv, dctx, lse, bias, seg, heads, hd)
    dqkv = jnp.concatenate([dq, dk, dv], axis=1)
    dn1 = scatter_group(dot_last(dqkv, wqkv).astype(BF16), 5)
    plan = [(0, 0, hc, 0, 0, count)] + [(1, k * hc, hc, 1 + k, 0, count) for k in range(3)]
    grad_o, grad_q, grad_k, grad_v = return_gradients(
        spans, [part_o, dot_first(n1, dqkv).astype(BF16)], plan, [8 * hc] * 4, 7
    )

    xf = tokens.astype(F32)
    inv1 = lax.rsqrt(jnp.mean(xf * xf, axis=-1, keepdims=True) + eps)
    inner1 = dn1 * gain_attn
    grad_input = dresid + inv1 * inner1 - xf * inv1**3 * jnp.mean(inner1 * xf, axis=-1, keepdims=True)
    dgain_attn = jnp.sum(dn1 * xf * inv1, axis=0)

    order = jnp.roll(diag, length, axis=1)
    dtable_own = lax.dot_general(onehot, order, (((1,), (1,)), ((), ())), precision=highest, preferred_element_type=F32)
    dtable = lax.dynamic_update_slice(jnp.zeros((n_buckets, heads_all), F32), dtable_own, (0, me * heads))
    squares = jnp.stack([jnp.sum(resid * resid), jnp.sum(out_f * out_f)])
    dgain_attn, dgain_ffn, dtable, squares = sum_everywhere(spans, (dgain_attn, dgain_ffn, dtable, squares), 8)
    entries = rows * width * 16 * spans
    norms = jnp.sqrt(squares / entries)
    return (
        out_f.astype(BF16),
        grad_input,
        grad_q.astype(F32),
        grad_k.astype(F32),
        grad_v.astype(F32),
        grad_o.astype(F32),
        grad_g.astype(F32),
        grad_u.astype(F32),
        grad_f.astype(F32),
        dgain_attn,
        dgain_ffn,
        dtable,
        norms,
    )


def solution(mesh):
    owners, copies = mesh.shape["fsdp"], mesh.shape["rep"]
    finer = Mesh(mesh.devices.reshape(owners // 4, 2, 2, copies // 2, 2), ("a", "b", "y", "x", "c"))
    owner = ("a", "b", "y")
    piece = P(owner + ("x", "c"), None)
    shard = P(owner, None)
    return jax.shard_map(
        per_device,
        mesh=finer,
        in_specs=(piece,) + (shard,) * 7 + (P(), P(), P(), shard, piece),
        out_specs=(piece, piece) + (shard,) * 7 + (P(), P(), P(), P()),
        check_vma=False,
    )
```

```python
import functools

import jax
import jax.numpy as jnp
from jax import lax
from jax.experimental import pallas as pl
from jax.experimental.pallas import tpu as pltpu
from jax.sharding import Mesh
from jax.sharding import PartitionSpec as P

eps = 1e-06
thresholds = (12, 16, 23, 32, 46, 64, 91)
highest = lax.Precision.HIGHEST
F32 = jnp.float32
BF16 = jnp.bfloat16
far_below = -1e30
MESH = pl.DeviceIdType.MESH
swap = ((0, 1), (1, 0))
MIB = 1 << 20


def gelu_tanh(v):
    return jax.nn.gelu(v, approximate=True)


def flat_dot(left, right):
    return jnp.dot(left, right, preferred_element_type=F32)


def dot_last(left, right):
    return lax.dot_general(left, right, (((1,), (1,)), ((), ())), preferred_element_type=F32)


def dot_first(left, right):
    return lax.dot_general(left, right, (((0,), (0,)), ((), ())), preferred_element_type=F32)


def shear_bias(row, length):
    wide = jnp.broadcast_to(row, (length, 2 * length))
    return pltpu.roll(wide, length, 1, stride=1, stride_axis=0)[:, :length]


def place():
    return lax.axis_index("b"), lax.axis_index("x"), lax.axis_index("c")


def slot(b, x, c):
    return b * 4 + x * 2 + c


def meet():
    b, x, c = place()
    barrier = pltpu.get_barrier_semaphore()
    for axis, other in (("b", 1 - b), ("x", 1 - x), ("c", 1 - c)):
        pl.semaphore_signal(barrier, inc=1, device_id={axis: other}, device_id_type=MESH)
    pl.semaphore_wait(barrier, 3)


def remote(src, dst, sends, recvs, n, axis):
    return pltpu.make_async_remote_copy(
        src_ref=src,
        dst_ref=dst,
        send_sem=sends.at[n],
        recv_sem=recvs.at[n],
        device_id={axis: 1 - lax.axis_index(axis)},
        device_id_type=MESH,
    )


def gather_parts(src, out, sends, recvs, local):
    b, x, c = place()
    own, at_x, at_b, at_d = slot(b, x, c), slot(b, 1 - x, c), slot(1 - b, x, c), slot(1 - b, 1 - x, c)
    over_x = remote(src, out.at[own], sends, recvs, 0, "x")
    over_b = remote(src, out.at[own], sends, recvs, 1, "b")
    on_x = remote(out.at[at_b], out.at[at_b], sends, recvs, 2, "x")
    over_c = remote(src, out.at[own], sends, recvs, 3, "c")
    x_on_c = remote(out.at[at_x], out.at[at_x], sends, recvs, 4, "c")
    b_on_c = remote(out.at[at_b], out.at[at_b], sends, recvs, 5, "c")
    d_on_c = remote(out.at[at_d], out.at[at_d], sends, recvs, 6, "c")
    keep = pltpu.make_async_copy(src, out.at[own], local)

    def begin():
        for copy in (over_b, over_x, over_c, keep):
            copy.start()

    def from_x():
        over_x.wait_recv()
        x_on_c.start()

    def from_b():
        over_b.wait_recv()
        on_x.start()
        b_on_c.start()

    def from_both():
        on_x.wait_recv()
        d_on_c.start()

    def end():
        for copy in (over_c, x_on_c, b_on_c, d_on_c):
            copy.wait_recv()
        for copy in (over_x, over_b, on_x, over_c, x_on_c, b_on_c, d_on_c):
            copy.wait_send()
        keep.wait()

    return [begin, from_x, from_b, from_both, end]


def in_rows(first, count, body, chunk=16):
    def step(i, _):
        body(pl.ds(pl.multiple_of(first + i * chunk, chunk), chunk))
        return 0

    lax.fori_loop(0, count // chunk, step, 0)


def scatter_parts(parts, acc, sib, out, diag, last, sends, recvs, mine=None, local=None):
    b, x, c = place()
    rows = parts.shape[1]
    seats = [(b, x), (b, 1 - x), (1 - b, x), (1 - b, 1 - x)]
    to_core = [remote(parts.at[slot(*seats[q], 1 - c)], sib.at[q], sends, recvs, q, "c") for q in range(4)]
    here = []
    if mine is not None:
        here = [pltpu.make_async_copy(parts.at[slot(*seats[q], c)], mine.at[q], local.at[q]) for q in range(4)]
    over_d = remote(out.at[2], diag, sends, recvs, 4, "x")
    over_x = remote(out.at[0], last.at[0], sends, recvs, 5, "x")
    over_b = remote(out.at[1], last.at[1], sends, recvs, 6, "b")

    def ready(q):
        to_core[q].wait_recv()
        for copy in here[q : q + 1]:
            copy.wait()

    def both(q, at):
        held = parts[slot(*seats[q], c), at, :] if mine is None else mine[q, at, :]
        return held.astype(F32) + sib[q, at, :].astype(F32)

    def begin():
        for q in (3, 1, 2, 0):
            to_core[q].start()
            for copy in here[q : q + 1]:
                copy.start()

    def to_x():
        for n, q, copy in ((2, 3, over_d), (0, 1, over_x)):
            ready(q)

            def put(at, n=n, q=q):
                out[n, at, :] = both(q, at).astype(BF16)

            in_rows(0, rows, put)
            copy.start()
        ready(2)
        ready(0)

        def own(at):
            acc[at, :] = both(0, at)

        in_rows(0, rows, own)

    def to_b():
        over_d.wait_recv()

        def put(at):
            out[1, at, :] = (both(2, at) + diag[at, :].astype(F32)).astype(BF16)

        in_rows(0, rows, put)
        over_b.start()

    def end():
        for copy in (over_x, over_b):
            copy.wait_recv()
        for copy in to_core + [over_d, over_x, over_b]:
            copy.wait_send()

        def finish(at):
            acc[at, :] += last[0, at, :].astype(F32) + last[1, at, :].astype(F32)

        in_rows(0, rows, finish)

    return [begin, to_x, to_b, end]


def scatter_scratch(rows, width, copied=True):
    scratch = [
        pltpu.VMEM((4, rows, width), BF16),
        pltpu.VMEM((3, rows, width), BF16),
        pltpu.VMEM((rows, width), BF16),
        pltpu.VMEM((2, rows, width), BF16),
        pltpu.SemaphoreType.DMA((7,)),
        pltpu.SemaphoreType.DMA((7,)),
    ]
    if copied:
        scratch += [pltpu.VMEM((4, rows, width), BF16), pltpu.SemaphoreType.DMA((4,))]
    return scratch


any_space = pl.BlockSpec(memory_space=pl.ANY)
in_vmem = pl.BlockSpec(memory_space=pltpu.VMEM)


def in_order(index, own, other):
    first = index == 0
    return jnp.stack([jnp.where(first, own, other), jnp.where(first, other, own)])


def remote_to(src, dst, send, recv, axis, to):
    return pltpu.make_async_remote_copy(
        src_ref=src, dst_ref=dst, send_sem=send, recv_sem=recv, device_id={axis: to}, device_id_type=MESH
    )


def meet_all(spans):
    a, y = lax.axis_index("a"), lax.axis_index("y")
    b, x, c = place()
    barrier = pltpu.get_barrier_semaphore()
    others = [("b", 1 - b), ("x", 1 - x), ("c", 1 - c), ("y", 1 - y)] + [("a", lax.rem(a + k, spans)) for k in range(1, spans)]
    for axis, other in others:
        pl.semaphore_signal(barrier, inc=1, device_id={axis: other}, device_id_type=MESH)
    pl.semaphore_wait(barrier, len(others))


def fetch_parts(spans, shards, fulls, sends, recvs, local):
    a, y = lax.axis_index("a"), lax.axis_index("y")
    b, x, c = place()
    me, pair = slot(b, x, c), slot(1 - b, x, c)
    count = shards[0].shape[0]

    def rows(at_a, at_b, at_y):
        return pl.ds(pl.multiple_of((at_a * 4 + at_b * 2 + at_y) * count, count), count)

    weights = []
    for i, (shard, (full, start)) in enumerate(zip(shards, fulls)):
        n = shard.shape[1] // 8
        cols = pl.ds(start, n)
        mine = shard.at[:, pl.ds(pl.multiple_of(me * n, 128), n)]
        theirs = shard.at[:, pl.ds(pl.multiple_of(pair * n, 128), n)]
        own, other = rows(a, b, y), rows(a, 1 - b, y)

        def block(at, full=full, cols=cols):
            return full.at[at, cols]

        def copy(src, dst, k, axis, to, i=i):
            return remote_to(src, dst, sends.at[i, k], recvs.at[i, k], axis, to)

        copies = {
            "keep": pltpu.make_async_copy(mine, block(own), local.at[i]),
            "b": copy(theirs, block(own), 0, "b", 1 - b),
            "y": copy(mine, block(own), 1, "y", 1 - y),
            "y_pair": copy(block(other), block(other), 2, "y", 1 - y),
            "a": [],
            "a_pair": [],
            "on": [],
            "on_pair": [],
        }
        for k in range(1, spans):
            to, source = lax.rem(a + k, spans), lax.rem(a + spans - k, spans)
            copies["a"].append(copy(mine, block(own), 4 * k - 1, "a", to))
            copies["a_pair"].append(copy(block(other), block(other), 4 * k, "a", to))
            far, far_pair = block(rows(source, b, y)), block(rows(source, 1 - b, y))
            copies["on"].append(copy(far, far, 4 * k + 1, "y", 1 - y))
            copies["on_pair"].append(copy(far_pair, far_pair, 4 * k + 2, "y", 1 - y))
        weights.append(copies)
    return weights


def start_all(copies):
    for copy in copies:
        copy.start()


def pair_in(copies):
    copies["b"].wait_recv()
    start_all([*copies["a_pair"], copies["y_pair"]])


def hand_on(copies, came, on):
    for got, copy in zip(copies[came], copies[on]):
        got.wait_recv()
        copy.start()


def weight_in(copies):
    copies["keep"].wait()
    for copy in (copies["y"], copies["y_pair"], *copies["on"], *copies["on_pair"]):
        copy.wait_recv()


def weight_out(copies):
    for copy in (copies["b"], copies["y"], copies["y_pair"]):
        copy.wait_send()
    for kind in ("a", "a_pair", "on", "on_pair"):
        for copy in copies[kind]:
            copy.wait_send()


def forward_kernel(
    spans, heads, hd, tokens, cotangent, wq, wk, wv, wo, wg, wu, wf, keep, gain1, gain2, vec, segc, segr,
    cot_all, n2_all, n1_out, bias_out, fqkv, fo, fgu, ff, qkv, ctx, lse, resid,
    tok_all, n1, vqkv, vo, bias, parts, acc, n2, sends, recvs, local, moves, *scratch
):
    hc, fc = wq.shape[1] // 8, wg.shape[1] // 8
    rows, width = tok_all.shape[1:]
    length = segr.shape[2]
    meet_all(spans)
    fulls = [(fqkv, 0), (fqkv, hc), (fqkv, 2 * hc), (fo, 0), (fgu, 0), (fgu, fc), (ff, 0)]
    weights = fetch_parts(spans, [wq, wk, wv, wo, wg, wu, wf], fulls, sends, recvs, local)
    small, large = weights[:4], weights[4:]
    tok = gather_parts(tokens, tok_all, *scratch[0:3])
    cot = gather_parts(cotangent, cot_all, *scratch[3:6])
    n2s = gather_parts(n2, n2_all, *scratch[6:9])

    proj, out_w = small[:3], small[3]
    for w in proj:
        start_all([w["b"], *w["a"], w["y"], w["keep"]])
    tok[0]()
    start_all([out_w["b"], out_w["y"], out_w["keep"]])
    large[0]["y"].start()
    for w in large:
        w["keep"].start()
    for h in range(heads):
        bias[h] = shear_bias(vec[h : h + 1, :], length)
    bias_move = pltpu.make_async_copy(bias, bias_out, moves.at[0])
    bias_move.start()
    for w in proj:
        pair_in(w)
    start_all(out_w["a"])
    for w in proj:
        hand_on(w, "a", "on")
    tok[1]()
    hand_on(proj[0], "a_pair", "on_pair")
    tok[2]()
    pair_in(out_w)
    for w in large:
        start_all(w["a"])
    for w in large[1:]:
        w["y"].start()
    cot[0]()
    for w in proj[1:]:
        hand_on(w, "a_pair", "on_pair")
    for w in large:
        w["b"].start()
    tok[3]()
    tok[4]()

    def norm(i, _):
        m = i // (rows // 16)
        at = pl.multiple_of(lax.rem(i, rows // 16) * 16, 16)
        value = tok_all[m, pl.ds(at, 16), :].astype(F32)
        inv = lax.rsqrt(jnp.mean(value * value, axis=-1, keepdims=True) + eps)
        n1[pl.ds(pl.multiple_of(i * 16, 16), 16), :] = (value * inv * gain1[...]).astype(BF16)
        return 0

    lax.fori_loop(0, 8 * rows // 16, norm, 0)
    n1_move = pltpu.make_async_copy(n1, n1_out, moves.at[1])
    n1_move.start()
    hand_on(out_w, "a", "on")
    for w in proj:
        weight_in(w)
    load = pltpu.make_async_copy(fqkv, vqkv, moves.at[2])
    load.start()
    load.wait()

    def project(i, _):
        at = pl.ds(pl.multiple_of(i * 128, 128), 128)
        qkv[at, :] = flat_dot(n1[at, :], vqkv[...]).astype(BF16)
        return 0

    lax.fori_loop(0, 8 * rows // 128, project, 0)
    hand_on(out_w, "a_pair", "on_pair")
    for s in range(2):
        at = slice(s * length, (s + 1) * length)
        same = segc[s] == segr[s]
        for h in range(heads):
            q_cols, k_cols, v_cols = (slice(k * hc + h * hd, k * hc + (h + 1) * hd) for k in range(3))
            scores = jnp.where(same, dot_last(qkv[at, q_cols], qkv[at, k_cols]) + bias[h], far_below)
            top = jnp.max(scores, axis=1, keepdims=True)
            expo = jnp.exp(scores - top)
            total = jnp.sum(expo, axis=1, keepdims=True)
            probs = (expo * (1.0 / total)).astype(BF16)
            ctx[at, q_cols] = flat_dot(probs, qkv[at, v_cols]).astype(BF16)
            lse[at, h : h + 1] = top + jnp.log(total)
        if s == 0:
            cot[1]()
            cot[2]()
            pair_in(large[0])
            hand_on(large[0], "a", "on")
    weight_in(out_w)
    load = pltpu.make_async_copy(fo, vo, moves.at[3])
    load.start()
    load.wait()

    def spread(m, _):
        at = pl.ds(pl.multiple_of(m * rows, rows), rows)
        parts[m] = dot_last(ctx[at, :], vo[...]).astype(BF16)
        return 0

    lax.fori_loop(0, 8, spread, 0)
    summed = scatter_parts(parts, acc, *scratch[9:])
    summed[0]()
    summed[1]()
    for w in large[1:]:
        pair_in(w)
    hand_on(large[1], "a", "on")
    summed[2]()
    hand_on(large[2], "a", "on")
    summed[3]()

    def residual(at):
        value = tokens_rows(tokens, tok_all, at) + keep[at, :] * acc[at, :]
        resid[at, :] = value
        inv = lax.rsqrt(jnp.mean(value * value, axis=-1, keepdims=True) + eps)
        n2[at, :] = (value * inv * gain2[...]).astype(BF16)

    in_rows(0, rows, residual)
    n2s[0]()
    hand_on(large[0], "a_pair", "on_pair")
    n2s[1]()
    n2s[2]()
    cot[3]()
    hand_on(large[1], "a_pair", "on_pair")
    n2s[3]()
    hand_on(large[2], "a_pair", "on_pair")
    n2s[4]()
    cot[4]()
    for w in large:
        weight_in(w)
    for w in weights:
        weight_out(w)
    n1_move.wait()
    bias_move.wait()


def tokens_rows(tokens, tok_all, at):
    return tok_all[slot(*place()), at, :].astype(F32)


def forward(spans, tokens, cotangent, weights, keep, gain1, gain2, vec, seg, hd, number):
    rows, width = tokens.shape
    heads, length = vec.shape[0], seg.shape[1]
    total = weights[0].shape[0] * 4 * spans
    hc, fc = weights[0].shape[1] // 8, weights[4].shape[1] // 8
    dma = pltpu.SemaphoreType.DMA
    shape = jax.ShapeDtypeStruct
    outs = pl.pallas_call(
        functools.partial(forward_kernel, spans, heads, hd),
        out_shape=[
            shape((8, rows, width), BF16),
            shape((8, rows, width), BF16),
            shape((8 * rows, width), BF16),
            shape((heads, length, length), F32),
            shape((total, 3 * hc), BF16),
            shape((total, hc), BF16),
            shape((total, 2 * fc), BF16),
            shape((total, fc), BF16),
            shape((8 * rows, 3 * hc), BF16),
            shape((8 * rows, hc), BF16),
            shape((8 * rows, heads), F32),
            shape((rows, width), F32),
        ],
        in_specs=[any_space] * 9 + [in_vmem] * 6,
        out_specs=[any_space] * 8 + [in_vmem] * 4,
        scratch_shapes=[
            pltpu.VMEM((8, rows, width), BF16),
            pltpu.VMEM((8 * rows, width), BF16),
            pltpu.VMEM((total, 3 * hc), BF16),
            pltpu.VMEM((total, hc), BF16),
            pltpu.VMEM((heads, length, length), F32),
            pltpu.VMEM((8, rows, width), BF16),
            pltpu.VMEM((rows, width), F32),
            pltpu.VMEM((rows, width), BF16),
            dma((7, 4 * spans - 1)),
            dma((7, 4 * spans - 1)),
            dma((7,)),
            dma((4,)),
        ]
        + [dma((7,)), dma((7,)), dma] * 3
        + scatter_scratch(rows, width, False),
        compiler_params=pltpu.CompilerParams(collective_id=number, has_side_effects=True, vmem_limit_bytes=56 * MIB),
    )(tokens, cotangent, *weights, keep, gain1[None, :], gain2[None, :], vec, seg[:, :, None], seg[:, None, :])
    return (outs[0].reshape(8 * rows, width), outs[1].reshape(8 * rows, width), *outs[2:])


def return_parts(spans, part, start, n, at, out, got_y, here, got_a, got_b, sends, recvs, local):
    a, y = lax.axis_index("a"), lax.axis_index("y")
    b, x, c = place()
    me, pair, x_me, x_pair = slot(b, x, c), slot(1 - b, x, c), slot(b, 1 - x, c), slot(1 - b, 1 - x, c)
    cols = pl.ds(start, n)
    count = got_b.shape[0]
    far = [lax.rem(a + k, spans) for k in range(1, spans)] + [a]
    held = [part.at[f, :, y] if here is None else here.at[k] for k, f in enumerate(far)]

    def copy(src, dst, k, axis, to):
        return remote_to(src, dst, sends.at[k], recvs.at[k], axis, to)

    def place_in(member):
        return out.at[at, pl.ds(pl.multiple_of(member * n, 128), n)]

    to_y = [copy(part.at[f, :, 1 - y, at, cols], got_y.at[k], k, "y", 1 - y) for k, f in enumerate(far)]
    load = []
    if here is not None:
        load = [pltpu.make_async_copy(part.at[f, :, y, at, cols], here.at[k], local.at[k]) for k, f in enumerate(far)]
    over_a = [copy(held[k], got_a.at[k], spans + k, "a", f) for k, f in enumerate(far[:-1])]
    base = 2 * spans - 1
    last = held[-1]
    over_b = copy(last.at[1 - b], got_b, base, "b", 1 - b)
    x_own = copy(last.at[b], place_in(me), base + 1, "x", 1 - x)
    x_other = copy(got_b, place_in(pair), base + 2, "x", 1 - x)
    c_own = copy(last.at[b], place_in(me), base + 3, "c", 1 - c)
    c_other = copy(got_b, place_in(pair), base + 4, "c", 1 - c)
    c_x_own = copy(place_in(x_me), place_in(x_me), base + 5, "c", 1 - c)
    c_x_other = copy(place_in(x_pair), place_in(x_pair), base + 6, "c", 1 - c)
    keep_own = pltpu.make_async_copy(last.at[b], place_in(me), local.at[spans])
    keep_other = pltpu.make_async_copy(got_b, place_in(pair), local.at[spans + 1])

    def add(k, others):
        for half in range(2):

            def body(r, half=half):
                if here is None:
                    value = part[far[k], half, y, r, :].astype(F32)
                else:
                    value = here[k, half, r, :].astype(F32)
                for other in others:
                    value = value + other[half, r, :].astype(F32)
                if here is None:
                    part[far[k], half, y, r, :] = value.astype(BF16)
                else:
                    here[k, half, r, :] = value.astype(BF16)

            in_rows(0, count, body)

    def ready(k):
        to_y[k].wait_recv()
        for item in load[k : k + 1]:
            item.wait()

    def begin():
        start_all(to_y + load)

    def across():
        for k in range(spans - 1):
            ready(k)
            add(k, [got_y.at[k]])
            over_a[k].start()

    def finish():
        ready(spans - 1)
        for item in over_a:
            item.wait_recv()
        add(spans - 1, [got_y.at[spans - 1]] + [got_a.at[k] for k in range(spans - 1)])
        start_all([over_b, x_own, c_own, keep_own])

    def pass_on():
        over_b.wait_recv()
        start_all([x_other, c_other, keep_other])

    def share():
        x_own.wait_recv()
        c_x_own.start()
        x_other.wait_recv()
        c_x_other.start()

    def end():
        for item in (c_own, c_other, c_x_own, c_x_other):
            item.wait_recv()
        for item in (*to_y, *over_a, over_b, x_own, x_other, c_own, c_other, c_x_own, c_x_other):
            item.wait_send()
        keep_own.wait()
        keep_other.wait()

    return [begin, across, finish, pass_on, share, end]


def return_scratch(spans, count, n, copied):
    dma = pltpu.SemaphoreType.DMA
    one = pltpu.VMEM((spans, 2, count, n), BF16)
    return [
        one,
        *([one] if copied else []),
        pltpu.VMEM((max(spans - 1, 1), 2, count, n), BF16),
        pltpu.VMEM((count, n), BF16),
        dma((2 * spans + 6,)),
        dma((2 * spans + 6,)),
        dma((spans + 2,)),
    ]


def sum_parts(spans, bufs, gots, sends, recvs):
    a, y = lax.axis_index("a"), lax.axis_index("y")
    b, x, c = place()
    steps = []

    def hop(step, targets):
        copies = [
            remote_to(buf, got.at[step + k], sends.at[i, step + k], recvs.at[i, step + k], axis, other)
            for k, (axis, other) in enumerate(targets)
            for i, (buf, got) in enumerate(zip(bufs, gots))
        ]

        def begin():
            start_all(copies)

        def end():
            for copy in copies:
                copy.wait()
            for buf, got in zip(bufs, gots):
                buf[...] = functools.reduce(jnp.add, [buf[...]] + [got[step + k] for k in range(len(targets))])

        steps.extend([begin, end])

    for step, target in enumerate((("c", 1 - c), ("x", 1 - x), ("b", 1 - b), ("y", 1 - y))):
        hop(step, [target])
    if spans > 1:
        hop(4, [("a", lax.rem(a + k, spans)) for k in range(1, spans)])
    return steps


def backward_kernel(
    spans, heads, hd, dn2_parts, out_parts, gf, ggu, wqkv, wo, n1, resid, tokens, cotangent, keep, gain1, gain2, qkv, ctx, lse, vec, segc, segr, onehot,
    dattn_all, o_f, o_g, o_u, o_o, o_q, o_k, o_v, out, grad_input, sums, table,
    sib, mid, diag, last, mine, sib2, mid2, diag2, last2, acc, dattn, dresid, held, v_qkv, v_o, dctx, dqkv, parts, gatt, shear, diags,
    got_sums, got_table, moves, *scratch
):
    total, hc = wo.shape
    fc = gf.shape[4]
    rows, width = resid.shape
    count = gf.shape[3]
    length = segr.shape[2]
    scratch = list(scratch)

    def take(n):
        out = scratch[:n]
        del scratch[:n]
        return out

    meet_all(spans)
    dn2_sum = scatter_parts(dn2_parts, acc, sib, mid, diag, last, *take(2), mine, *take(1))
    dn1_sum = scatter_parts(parts, acc, sib, mid, diag, last, *take(2))
    out_sum = scatter_parts(out_parts, acc, sib2, mid2, diag2, last2, *take(2), mine, *take(1))
    dattn_in = gather_parts(dattn, dattn_all, *take(3))
    summed = sum_parts(spans, [sums, table], [got_sums, got_table], *take(2))
    ffn = []
    for part, start, result in ((gf, 0, o_f), (ggu, 0, o_g), (ggu, fc, o_u)):
        for first in (0, count // 2):
            ffn.append(return_parts(spans, part, start, fc, pl.ds(first, count // 2), result, *take(7)))
    att = []
    for i, result in enumerate((o_o, o_q, o_k, o_v)):
        got_y, got_a, got_b, *sems = take(6)
        att.append(return_parts(spans, gatt.at[i], 0, hc, pl.ds(0, count), result, got_y, None, got_a, got_b, *sems))
    begin, across, finish, pass_on, share, end = range(6)

    loads = [
        pltpu.make_async_copy(wqkv, v_qkv, moves.at[0]),
        pltpu.make_async_copy(wo, v_o, moves.at[1]),
    ]
    dn2_sum[0]()
    for piece in ffn:
        piece[begin]()
    start_all(loads)
    sums[...] = jnp.zeros_like(sums)
    table[...] = jnp.zeros_like(table)
    dn2_sum[1]()
    ffn[0][across]()
    dn2_sum[2]()
    ffn[1][across]()
    dn2_sum[3]()

    def second_norm(at):
        value, dn2 = resid[at, :], acc[at, :]
        inv = lax.rsqrt(jnp.mean(value * value, axis=-1, keepdims=True) + eps)
        inner = dn2 * gain2[...]
        grad = (
            cotangent[at, :].astype(F32)
            + inv * inner
            - value * (inv * inv * inv * jnp.mean(inner * value, axis=-1, keepdims=True))
        )
        dresid[at, :] = grad
        sums[1:2, :] += jnp.sum(dn2 * value * inv, axis=0, keepdims=True)
        sums[2:3, :] += jnp.sum(value * value, axis=0, keepdims=True)
        dattn[at, :] = (keep[at, :] * grad).astype(BF16)

    in_rows(0, rows, second_norm)
    dattn_in[0]()
    ffn[0][finish]()
    dattn_in[1]()
    ffn[2][across]()
    dattn_in[2]()
    ffn[0][pass_on]()
    ffn[1][finish]()
    ffn[0][share]()
    dattn_in[3]()
    ffn[3][across]()
    dattn_in[4]()
    for m in range(8):
        pltpu.make_async_copy(dattn_all.at[m], held.at[pl.ds(m * rows, rows)], moves.at[2 + m]).start()
    for load in loads:
        load.wait()
    for m in range(8):
        pltpu.make_async_copy(dattn_all.at[m], held.at[pl.ds(m * rows, rows)], moves.at[2 + m]).wait()

    def to_ctx(m, _):
        at = pl.ds(pl.multiple_of(m * rows, rows), rows)
        dctx[at, :] = flat_dot(held[at, :], v_o[...]).astype(BF16)
        return 0

    lax.fori_loop(0, 8, to_ctx, 0)
    wide = max(count, 256)

    def weight_grad(i, factor):
        for first in range(0, total, wide):
            value = dot_first(held[:, first : first + wide], factor).astype(BF16)
            for owner in range(first // count, (first + wide) // count):
                at = owner * count - first
                gatt[i, owner // 4, owner // 2 % 2, owner % 2] = value[at : at + count]

    weight_grad(0, ctx[...])
    att[0][begin]()
    n1_load = pltpu.make_async_copy(n1, held, moves.at[10])
    n1_load.start()
    ffn[2][finish]()
    ffn[1][pass_on]()
    ffn[1][share]()
    between = [
        [ffn[4][across], ffn[3][finish]],
        [ffn[2][pass_on], ffn[2][share]],
        [ffn[5][across], ffn[4][finish]],
        [ffn[3][pass_on], ffn[3][share]],
    ]
    for h in range(heads):
        bias = shear_bias(vec[h : h + 1, :], length)
        q_cols, k_cols, v_cols = (slice(k * hc + h * hd, k * hc + (h + 1) * hd) for k in range(3))
        for s in range(2):
            at = slice(s * length, (s + 1) * length)
            same = segc[s] == segr[s]
            q, k, v, d = qkv[at, q_cols], qkv[at, k_cols], qkv[at, v_cols], dctx[at, q_cols]
            scores = jnp.where(same, dot_last(q, k) + bias, far_below)
            probs = jnp.exp(scores - lse[at, h : h + 1])
            dprobs = dot_last(d, v)
            dqkv[at, v_cols] = dot_first(probs.astype(BF16), d).astype(BF16)
            product = probs * dprobs
            dscores = product - probs * jnp.sum(product, axis=1, keepdims=True)
            if s == 0:
                shear[...] = dscores
            else:
                shear[...] += dscores
            dlogits = dscores.astype(BF16)
            dqkv[at, q_cols] = flat_dot(dlogits, k).astype(BF16)
            dqkv[at, k_cols] = dot_first(dlogits, q).astype(BF16)

        def shift(g, carry):
            group = shear[pl.ds(pl.multiple_of(g * 8, 8), 8), :]
            group = jnp.concatenate([group, jnp.zeros_like(group)], axis=1)
            return carry + pltpu.roll(group, 2 * length - g * 8, 1)

        shifted = lax.fori_loop(0, length // 8, shift, jnp.zeros((8, 2 * length), F32), unroll=8)
        line = shifted[0:1, :]
        for r in range(1, 8):
            line = line + pltpu.roll(shifted[r : r + 1, :], 2 * length - r, 1)
        diags[h : h + 1, :] = line
        for step in between[h]:
            step()

    def to_n1(m, _):
        at = pl.ds(pl.multiple_of(m * rows, rows), rows)
        parts[m] = dot_last(dqkv[at, :], v_qkv[...]).astype(BF16)
        return 0

    lax.fori_loop(0, 8, to_n1, 0)
    dn1_sum[0]()
    dn1_sum[1]()
    n1_load.wait()
    for i in range(3):
        weight_grad(1 + i, dqkv[:, i * hc : (i + 1) * hc])
        att[1 + i][begin]()
    ffn[5][finish]()
    ffn[4][pass_on]()
    ffn[4][share]()
    dn1_sum[2]()
    att[0][across]()
    out_sum[0]()
    dn1_sum[3]()

    def first_norm(at):
        value, dn1 = tokens[at, :].astype(F32), acc[at, :]
        inv = lax.rsqrt(jnp.mean(value * value, axis=-1, keepdims=True) + eps)
        inner = dn1 * gain1[...]
        grad_input[at, :] = (
            dresid[at, :]
            + inv * inner
            - value * (inv * inv * inv * jnp.mean(inner * value, axis=-1, keepdims=True))
        )
        sums[0:1, :] += jnp.sum(dn1 * value * inv, axis=0, keepdims=True)

    in_rows(0, rows, first_norm)
    out_sum[1]()
    att[1][across]()
    ffn[5][pass_on]()
    ffn[5][share]()
    att[0][finish]()
    out_sum[2]()
    att[2][across]()
    att[1][finish]()
    att[0][pass_on]()
    att[0][share]()
    att[3][across]()
    out_sum[3]()

    def final(at):
        value = resid[at, :] + acc[at, :]
        out[at, :] = value.astype(BF16)
        sums[3:4, :] += jnp.sum(value * value, axis=0, keepdims=True)

    in_rows(0, rows, final)
    buckets = lax.dot_general(
        diags[...], onehot[...], (((1,), (0,)), ((), ())), precision=highest, preferred_element_type=F32
    )
    table[slot(*place()), 0:heads, 0 : buckets.shape[1]] = buckets
    summed[0]()
    att[2][finish]()
    summed[1]()
    summed[2]()
    att[1][pass_on]()
    att[1][share]()
    summed[3]()
    summed[4]()
    att[3][finish]()
    att[2][pass_on]()
    att[2][share]()
    for step in summed[5:]:
        step()
    att[3][pass_on]()
    att[3][share]()
    for piece in ffn + att:
        piece[end]()


def backward(spans, dn2_part, out_part, grads, wqkv, wo, n1, resid, tokens, cotangent, keep, gain1, gain2, qkv, ctx, lse, vec, seg, onehot, hd, number):
    rows, width = tokens.shape
    heads, length = vec.shape[0], seg.shape[1]
    total, hc = wo.shape
    fc = grads[0].shape[1]
    count = total // (4 * spans)
    dma, shape, vmem = pltpu.SemaphoreType.DMA, jax.ShapeDtypeStruct, pltpu.VMEM
    scratch = [*scatter_scratch(rows, width)[:4], scatter_scratch(rows, width)[6], *scatter_scratch(rows, width)[:4]]
    scratch += [
        vmem((rows, width), F32),
        vmem((rows, width), BF16),
        vmem((rows, width), F32),
        vmem((8 * rows, width), BF16),
        vmem((total, 3 * hc), BF16),
        vmem((total, hc), BF16),
        vmem((8 * rows, hc), BF16),
        vmem((8 * rows, 3 * hc), BF16),
        vmem((8, rows, width), BF16),
        vmem((4, spans, 2, 2, count, hc), BF16),
        vmem((length, length), F32),
        vmem((heads, 2 * length), F32),
        vmem((3 + spans, 8, width), F32),
        vmem((3 + spans, 8, 8, 128), F32),
        dma((11,)),
    ]
    scratch += [dma((7,)), dma((7,)), dma((4,)), dma((7,)), dma((7,)), dma((7,)), dma((7,)), dma((4,))]
    scratch += [dma((7,)), dma((7,)), dma, dma((2, 3 + spans)), dma((2, 3 + spans))]
    for _ in range(6):
        scratch += return_scratch(spans, count // 2, fc, True)
    for _ in range(4):
        scratch += return_scratch(spans, count, hc, False)
    shaped = [grad.reshape(spans, 2, 2, count, grad.shape[1]) for grad in grads]
    outs = pl.pallas_call(
        functools.partial(backward_kernel, spans, heads, hd),
        out_shape=[shape((8, rows, width), BF16)]
        + [shape((count, 8 * fc), BF16)] * 3
        + [shape((count, 8 * hc), BF16)] * 4
        + [shape((rows, width), BF16), shape((rows, width), F32), shape((8, width), F32), shape((8, 8, 128), F32)],
        in_specs=[any_space] * 7 + [in_vmem] * 13,
        out_specs=[any_space] * 8 + [in_vmem] * 4,
        scratch_shapes=scratch,
        compiler_params=pltpu.CompilerParams(collective_id=number, has_side_effects=True, vmem_limit_bytes=62 * MIB),
    )(
        dn2_part.reshape(8, rows, width),
        out_part.reshape(8, rows, width),
        *shaped,
        wqkv,
        wo,
        n1,
        resid,
        tokens,
        cotangent,
        keep,
        gain1[None, :],
        gain2[None, :],
        qkv,
        ctx,
        lse,
        vec,
        seg[:, :, None],
        seg[:, None, :],
        onehot,
    )
    return outs[1:]


def per_device(
    tokens,
    w_query,
    w_key,
    w_value,
    w_attn_out,
    w_gate,
    w_up,
    w_ff_out,
    gain_attn,
    gain_ffn,
    rel_table,
    doc_lengths,
    cotangent,
):
    rows, width = tokens.shape
    n_buckets, heads_all = rel_table.shape
    heads = heads_all // 8
    hc = w_query.shape[1] // 8
    fc = w_gate.shape[1] // 8
    hd = hc // heads
    length = 4 * rows
    b, x, c = place()
    me = slot(b, x, c)

    other_docs = lax.ppermute(doc_lengths, "b", swap)
    ends = jnp.cumsum(in_order(b, doc_lengths[0], other_docs[0]), axis=1)
    positions = jnp.arange(length, dtype=jnp.int32)
    seg = jnp.sum((positions[None, :, None] >= ends[:, None, :]).astype(jnp.int32), axis=2)
    own_seg = lax.dynamic_slice(seg, (b, (x * 2 + c) * rows), (1, rows))[0]
    keep = (own_seg < doc_lengths.shape[1]).astype(F32)[:, None]
    offset = jnp.arange(-length, length, dtype=jnp.int32)
    distance = jnp.abs(offset)
    far = 8 + jnp.sum((distance[:, None] >= jnp.array(thresholds, jnp.int32)).astype(jnp.int32), axis=1)
    bucket = jnp.where(offset > 0, 16, 0) + jnp.where(distance < 8, distance, far)
    onehot = (jnp.arange(n_buckets, dtype=jnp.int32)[:, None] == bucket[None, :]).astype(F32)
    table = lax.dynamic_slice_in_dim(rel_table, me * heads, heads, 1)
    vec = lax.dot_general(table, onehot, (((0,), (0,)), ((), ())), precision=highest, preferred_element_type=F32)

    spans = lax.axis_size("a")
    weights = (w_query, w_key, w_value, w_attn_out, w_gate, w_up, w_ff_out)
    cot_all, n2, n1, bias, wqkv, wo, wgu, wf, qkv, ctx, lse, resid = forward(
        spans, tokens, cotangent, weights, keep, gain_attn, gain_ffn, vec, seg, hd, 0
    )
    gate_up = flat_dot(n2, wgu)
    gate, up = gate_up[:, :fc], gate_up[:, fc:]
    activ, activ_back = jax.vjp(gelu_tanh, gate)
    hidden = (activ * up).astype(BF16)
    out_part = dot_last(hidden, wf).astype(BF16)

    dhidden = flat_dot(cot_all, wf)
    dgate = activ_back(dhidden * up)[0].astype(BF16)
    dup = (dhidden * activ).astype(BF16)
    dgu = jnp.concatenate([dgate, dup], axis=1)
    dn2_part = dot_last(dgu, wgu).astype(BF16)
    grads = [dot_first(cot_all, hidden).astype(BF16), dot_first(n2, dgu).astype(BF16)]
    order = jnp.roll(onehot, length, axis=1).T
    grad_f, grad_g, grad_u, grad_o, grad_q, grad_k, grad_v, out, grad_input, sums, table_sums = backward(
        spans, dn2_part, out_part, grads, wqkv, wo, n1, resid, tokens, cotangent, keep, gain_attn, gain_ffn, qkv, ctx, lse, vec, seg, order, hd, 1
    )
    dtable = table_sums[:, :heads, :n_buckets].reshape(heads_all, n_buckets).T
    entries = rows * width * 16 * spans
    norms = jnp.sqrt(jnp.sum(sums[2:4], axis=1) / entries)
    return (
        out,
        grad_input,
        grad_q.astype(F32),
        grad_k.astype(F32),
        grad_v.astype(F32),
        grad_o.astype(F32),
        grad_g.astype(F32),
        grad_u.astype(F32),
        grad_f.astype(F32),
        sums[0],
        sums[1],
        dtable,
        norms,
    )


def solution(mesh):
    owners, copies = mesh.shape["fsdp"], mesh.shape["rep"]
    finer = Mesh(mesh.devices.reshape(owners // 4, 2, 2, copies // 2, 2), ("a", "b", "y", "x", "c"))
    owner = ("a", "b", "y")
    piece = P(owner + ("x", "c"), None)
    shard = P(owner, None)
    return jax.shard_map(
        per_device,
        mesh=finer,
        in_specs=(piece,) + (shard,) * 7 + (P(), P(), P(), shard, piece),
        out_specs=(piece, piece) + (shard,) * 7 + (P(), P(), P(), P()),
        check_vma=False,
    )
```

```python
import functools
import types

import jax
import jax.numpy as jnp
import numpy as np
from jax import lax
from jax.experimental import pallas as pl
from jax.experimental.pallas import tpu as pltpu
from jax.sharding import Mesh
from jax.sharding import PartitionSpec as P

eps = 1e-06
thresholds = (12, 16, 23, 32, 46, 64, 91)
highest = lax.Precision.HIGHEST
F32 = jnp.float32
BF16 = jnp.bfloat16
far_below = -1e30
MESH = pl.DeviceIdType.MESH
swap = ((0, 1), (1, 0))
MIB = 1 << 20


def gelu_tanh(v):
    return jax.nn.gelu(v, approximate=True)


def flat_dot(left, right):
    return jnp.dot(left, right, preferred_element_type=F32)


def dot_last(left, right):
    return lax.dot_general(left, right, (((1,), (1,)), ((), ())), preferred_element_type=F32)


def dot_first(left, right):
    return lax.dot_general(left, right, (((0,), (0,)), ((), ())), preferred_element_type=F32)


def shear_bias(row, length):
    wide = jnp.broadcast_to(row, (length, 2 * length))
    return pltpu.roll(wide, length, 1, stride=1, stride_axis=0)[:, :length]


def place():
    return lax.axis_index("b"), lax.axis_index("x"), lax.axis_index("c")


def slot(b, x, c):
    return b * 4 + x * 2 + c


def meet():
    b, x, c = place()
    barrier = pltpu.get_barrier_semaphore()
    for axis, other in (("b", 1 - b), ("x", 1 - x), ("c", 1 - c)):
        pl.semaphore_signal(barrier, inc=1, device_id={axis: other}, device_id_type=MESH)
    pl.semaphore_wait(barrier, 3)


def start_all(copies):
    for copy in copies:
        copy.start()


def remote(src, dst, sends, recvs, n, axis):
    return pltpu.make_async_remote_copy(
        src_ref=src,
        dst_ref=dst,
        send_sem=sends.at[n],
        recv_sem=recvs.at[n],
        device_id={axis: 1 - lax.axis_index(axis)},
        device_id_type=MESH,
    )


def gather_parts(share, src, out, sends, recvs, local):
    b, x, c = place()
    rows = src.shape[0]
    by_x = int(rows * share) // 16 * 16
    first, rest = pl.ds(0, by_x), pl.ds(by_x, rows - by_x)
    own, at_x, at_b, at_d = slot(b, x, c), slot(b, 1 - x, c), slot(1 - b, x, c), slot(1 - b, 1 - x, c)
    over_x = remote(src, out.at[own], sends, recvs, 0, "x")
    over_b = remote(src, out.at[own], sends, recvs, 1, "b")
    on_x = remote(out.at[at_b, first], out.at[at_b, first], sends, recvs, 2, "x")
    over_c = remote(src, out.at[own], sends, recvs, 3, "c")
    x_on_c = remote(out.at[at_x], out.at[at_x], sends, recvs, 4, "c")
    b_on_c = remote(out.at[at_b], out.at[at_b], sends, recvs, 5, "c")
    d_on_c = [remote(out.at[at_d, first], out.at[at_d, first], sends, recvs, 6, "c")]
    on_b = []
    if by_x < rows:
        on_b = [remote(out.at[at_x, rest], out.at[at_x, rest], sends, recvs, 7, "b")]
        d_on_c.append(remote(out.at[at_d, rest], out.at[at_d, rest], sends, recvs, 8, "c"))
    keep = pltpu.make_async_copy(src, out.at[own], local)

    def begin():
        for copy in (over_b, over_x, over_c, keep):
            copy.start()

    def from_x():
        over_x.wait_recv()
        for copy in (*on_b, x_on_c):
            copy.start()

    def from_b():
        over_b.wait_recv()
        on_x.start()
        b_on_c.start()

    def from_both():
        for came, on in zip([on_x, *on_b], d_on_c):
            came.wait_recv()
            on.start()

    def end():
        for copy in (over_c, x_on_c, b_on_c, *d_on_c):
            copy.wait_recv()
        for copy in (over_x, over_b, on_x, *on_b, over_c, x_on_c, b_on_c, *d_on_c):
            copy.wait_send()
        keep.wait()

    return [begin, from_x, from_b, from_both, end]


def in_rows(first, count, body, chunk=16):
    def step(i, _):
        body(pl.ds(pl.multiple_of(first + i * chunk, chunk), chunk))
        return 0

    lax.fori_loop(0, count // chunk, step, 0)


def scatter_parts(share, source, acc, sib, out, diag, last, sends, recvs):
    b, x, c = place()
    rows = sib.shape[1]
    by_x = int(rows * share) // 16 * 16
    seats = [(b, x), (b, 1 - x), (1 - b, x), (1 - b, 1 - x)]
    here, there = [slot(*seat, c) for seat in seats], [slot(*seat, 1 - c) for seat in seats]
    to_core = [remote(sib.at[q], sib.at[q], sends, recvs, q, "c") for q in range(4)]

    def over(n, to, first, count, k, axis):
        at = pl.ds(first, count)
        return remote(out.at[n, at], to.at[at], sends, recvs, k, axis)

    rest = rows - by_x
    d_x = over(2, diag, 0, by_x, 4, "x")
    x_first, b_last = over(0, last.at[0], 0, by_x, 5, "x"), over(1, last.at[1], 0, by_x, 6, "b")
    d_b, x_last, b_first = [], [], []
    if rest:
        d_b = [over(2, diag, by_x, rest, 7, "b")]
        x_last, b_first = [over(0, last.at[0], by_x, rest, 8, "x")], [over(1, last.at[1], by_x, rest, 9, "b")]

    def both(q, at):
        return source.parts[here[q], at, :].astype(F32) + sib[q, at, :].astype(F32)

    def put(n, q, first, count, more=False):
        def body(at):
            value = both(q, at)
            if more:
                value = value + diag[at, :].astype(F32)
            out[n, at, :] = value.astype(BF16)

        if count:
            in_rows(first, count, body)

    def begin(q):
        source.make(there[q])
        remote(source.parts.at[there[q]], sib.at[q], sends, recvs, q, "c").start()
        source.make(here[q])

    def to_diagonal():
        to_core[3].wait_recv()
        put(2, 3, 0, by_x)
        d_x.start()
        put(2, 3, by_x, rest)
        start_all(d_b)

    def to_x():
        to_core[1].wait_recv()
        put(0, 1, 0, by_x)
        x_first.start()

    def to_b():
        to_core[2].wait_recv()
        put(1, 2, by_x, rest)
        start_all(b_first)

    def keep():
        to_core[0].wait_recv()

        def own(at):
            acc[at, :] = both(0, at)

        in_rows(0, rows, own)

    def on_x():
        for copy in d_b:
            copy.wait_recv()
        put(0, 1, by_x, rest, True)
        start_all(x_last)

    def on_b():
        d_x.wait_recv()
        put(1, 2, 0, by_x, True)
        b_last.start()
        for copy in to_core:
            copy.wait_send()

    def end():
        for copy in (x_first, *b_first, *x_last, b_last):
            copy.wait_recv()
        for copy in (d_x, *d_b, x_first, *b_first, *x_last, b_last):
            copy.wait_send()

        def finish(at):
            acc[at, :] += last[0, at, :].astype(F32) + last[1, at, :].astype(F32)

        in_rows(0, rows, finish)

    makes = [functools.partial(begin, q) for q in (3, 1, 2, 0)]
    return [*makes, to_diagonal, to_x, to_b, keep, on_x, on_b, end]


def scatter_scratch(rows, width):
    return [
        pltpu.VMEM((4, rows, width), BF16),
        pltpu.VMEM((3, rows, width), BF16),
        pltpu.VMEM((rows, width), BF16),
        pltpu.VMEM((2, rows, width), BF16),
        pltpu.SemaphoreType.DMA((10,)),
        pltpu.SemaphoreType.DMA((10,)),
    ]


any_space = pl.BlockSpec(memory_space=pl.ANY)
in_vmem = pl.BlockSpec(memory_space=pltpu.VMEM)


def remote_to(src, dst, send, recv, axis, to):
    return pltpu.make_async_remote_copy(
        src_ref=src, dst_ref=dst, send_sem=send, recv_sem=recv, device_id={axis: to}, device_id_type=MESH
    )


def meet_all(spans):
    a, y = lax.axis_index("a"), lax.axis_index("y")
    b, x, c = place()
    barrier = pltpu.get_barrier_semaphore()
    others = [("b", 1 - b), ("x", 1 - x), ("c", 1 - c), ("y", 1 - y)] + [("a", lax.rem(a + k, spans)) for k in range(1, spans)]
    for axis, other in others:
        pl.semaphore_signal(barrier, inc=1, device_id={axis: other}, device_id_type=MESH)
    pl.semaphore_wait(barrier, len(others))


def fetch_parts(spans, shards, fulls, stages, sends, recvs, local):
    a, y = lax.axis_index("a"), lax.axis_index("y")
    b, x, c = place()
    me, pair = slot(b, x, c), slot(1 - b, x, c)
    count = shards[0].shape[0]

    def rows(at_a, at_b, at_y):
        return pl.ds(pl.multiple_of((at_a * 4 + at_b * 2 + at_y) * count, count), count)

    weights = []
    for i, (shard, (full, start)) in enumerate(zip(shards, fulls)):
        n = shard.shape[1] // 8
        cols = pl.ds(start, n)
        mine = shard.at[:, pl.ds(pl.multiple_of(me * n, 128), n)]
        theirs = shard.at[:, pl.ds(pl.multiple_of(pair * n, 128), n)]
        own, other = rows(a, b, y), rows(a, 1 - b, y)

        def block(at, full=full, cols=cols):
            return full.at[at, cols]

        def copy(src, dst, k, axis, to, i=i):
            return remote_to(src, dst, sends.at[i, k], recvs.at[i, k], axis, to)

        copies = {
            "load": pltpu.make_async_copy(mine, stages[i], local.at[i]),
            "keep": pltpu.make_async_copy(stages[i], block(own), local.at[i]),
            "b": copy(theirs, block(own), 0, "b", 1 - b),
            "y": copy(mine, block(own), 1, "y", 1 - y),
            "y_pair": copy(block(other), block(other), 2, "y", 1 - y),
            "a": [],
            "a_pair": [],
            "on": [],
            "on_pair": [],
        }
        for k in range(1, spans):
            to, source = lax.rem(a + k, spans), lax.rem(a + spans - k, spans)
            copies["a"].append(copy(mine, block(own), 4 * k - 1, "a", to))
            copies["a_pair"].append(copy(block(other), block(other), 4 * k, "a", to))
            far, far_pair = block(rows(source, b, y)), block(rows(source, 1 - b, y))
            copies["on"].append(copy(far, far, 4 * k + 1, "y", 1 - y))
            copies["on_pair"].append(copy(far_pair, far_pair, 4 * k + 2, "y", 1 - y))
        weights.append(copies)
    return weights


def pair_in(copies):
    copies["b"].wait_recv()
    start_all([*copies["a_pair"], copies["y_pair"]])


def hand_on(copies, came, on):
    for got, copy in zip(copies[came], copies[on]):
        got.wait_recv()
        copy.start()


def own_in(copies):
    copies["load"].wait()
    copies["keep"].start()


def weight_in(copies):
    copies["keep"].wait()
    for copy in (copies["y"], copies["y_pair"], *copies["on"], *copies["on_pair"]):
        copy.wait_recv()


def weight_out(copies):
    for copy in (copies["b"], copies["y"], copies["y_pair"]):
        copy.wait_send()
    for kind in ("a", "a_pair", "on", "on_pair"):
        for copy in copies[kind]:
            copy.wait_send()


def forward_kernel(
    spans, heads, hd, tokens, cotangent, wq, wk, wv, wo, wg, wu, wf, ends, gain1, gain2, rel_table, onehot,
    cot_out, n2_out, n1_out, fqkv, fo, fgu, ff, gu_out, hidden_out, gf_out, qkv, ctx, lse, resid, segc, segr, keep, vec,
    tok_all, cot_all, n2_all, n1, vqkv, vo, vgu, gu, hidden, gf, bias, parts, pair_ends, vecs, acc, n2, mine_small, mine_large, cot_own, sends, recvs, local, moves, *scratch
):
    hc, fc = wq.shape[1] // 8, wg.shape[1] // 8
    rows, width = tok_all.shape[1:]
    length = segr.shape[2]
    b, x, c = place()
    meet_all(spans)
    fulls = [(fqkv, 0), (fqkv, hc), (fqkv, 2 * hc), (fo, 0), (fgu, 0), (fgu, fc), (ff, 0)]
    stages = [mine_small.at[i] for i in range(4)] + [mine_large.at[i] for i in range(3)]
    weights = fetch_parts(spans, [wq, wk, wv, wo, wg, wu, wf], fulls, stages, sends, recvs, local)
    tok = gather_parts(tok_share, tokens, tok_all, *scratch[0:3])
    cot = gather_parts(cot_share, cot_own, cot_all, *scratch[3:6])
    n2s = gather_parts(n2_share, n2, n2_all, *scratch[6:9])

    def make_part(m):
        at = pl.ds(pl.multiple_of(m * rows, rows), rows)
        parts[m] = dot_last(ctx[at, :], vo[...]).astype(BF16)

    summed = scatter_parts(attn_share, types.SimpleNamespace(make=make_part, parts=parts), acc, *scratch[9:])
    cot_load = pltpu.make_async_copy(cotangent, cot_own, moves.at[4])
    cot_load.start()
    start_cot = cot[0]

    def cot_begin():
        cot_load.wait()
        start_cot()

    cot[0] = cot_begin
    pair_docs = remote_to(ends, pair_ends, moves.at[5], moves.at[6], "b", 1 - b)
    gu_load = pltpu.make_async_copy(fgu, vgu, moves.at[0])
    last_moves = [
        pltpu.make_async_copy(n2_all, n2_out, moves.at[7]),
        pltpu.make_async_copy(cot_all, cot_out, moves.at[8]),
        pltpu.make_async_copy(gu, gu_out, moves.at[9]),
        pltpu.make_async_copy(hidden, hidden_out, moves.at[10]),
        pltpu.make_async_copy(gf, gf_out, moves.at[11]),
    ]
    n1_move = pltpu.make_async_copy(n1, n1_out, moves.at[1])
    names = ("q", "k", "v", "o", "g", "u", "f")
    steps = {}
    for name, w in zip(names, weights):
        steps["b" + name] = w["b"].start
        steps["y" + name] = w["y"].start
        steps["load" + name] = w["load"].start
        steps["keep" + name] = functools.partial(own_in, w)
        steps["a" + name] = functools.partial(start_all, w["a"])
        steps["pair" + name] = functools.partial(pair_in, w)
        steps["on" + name] = functools.partial(hand_on, w, "a", "on")
        steps["onp" + name] = functools.partial(hand_on, w, "a_pair", "on_pair")
        steps["in" + name] = functools.partial(weight_in, w)
    for name, parts_of in (("t", tok), ("c", cot), ("n", n2s), ("s", summed)):
        for k, step in enumerate(parts_of):
            steps[name + str(k)] = step

    def step(function):
        steps[function.__name__] = function
        return function

    steps["docs"] = pair_docs.start
    steps["load_gu"] = gu_load.start

    @step
    def make_bias():
        every = lax.dot_general(
            rel_table[...], onehot[...], (((0,), (0,)), ((), ())), precision=highest, preferred_element_type=F32
        )
        for m in range(8):
            vecs[m] = every[m * heads : (m + 1) * heads]
        vec[...] = vecs[slot(*place())]
        for h in range(heads):
            bias[h] = shear_bias(vec[h : h + 1, :], length)

    def documents(position, last):
        out = jnp.zeros(position.shape, jnp.int32)
        for k in range(docs_per_sequence):
            out = out + (position >= last[0:1, k : k + 1]).astype(jnp.int32)
        return out

    @step
    def segments():
        pair_docs.wait()
        column = lax.broadcasted_iota(jnp.int32, (length, 1), 0)
        line = lax.broadcasted_iota(jnp.int32, (1, length), 1)
        for s in range(2):
            last = jnp.where(b == s, ends[...], pair_ends[...])
            segc[s] = documents(column, last)
            segr[s] = documents(line, last)
        own = (x * 2 + c) * rows + lax.broadcasted_iota(jnp.int32, (rows, 1), 0)
        keep[...] = (documents(own, ends[...]) < docs_per_sequence).astype(F32)

    @step
    def norm():
        def body(i, _):
            m = i // (rows // 16)
            at = pl.multiple_of(lax.rem(i, rows // 16) * 16, 16)
            value = tok_all[m, pl.ds(at, 16), :].astype(F32)
            inv = lax.rsqrt(jnp.mean(value * value, axis=-1, keepdims=True) + eps)
            n1[pl.ds(pl.multiple_of(i * 16, 16), 16), :] = (value * inv * gain1[...]).astype(BF16)
            return 0

        lax.fori_loop(0, 8 * rows // 16, body, 0)
        n1_move.start()

    @step
    def project():
        load = pltpu.make_async_copy(fqkv, vqkv, moves.at[2])
        load.start()
        load.wait()

        def body(i, _):
            at = pl.ds(pl.multiple_of(i * 128, 128), 128)
            qkv[at, :] = flat_dot(n1[at, :], vqkv[...]).astype(BF16)
            return 0

        lax.fori_loop(0, 8 * rows // 128, body, 0)

    def attend(s, h):
        at = slice(s * length, (s + 1) * length)
        same = segc[s] == segr[s]
        q_cols, k_cols, v_cols = (slice(k * hc + h * hd, k * hc + (h + 1) * hd) for k in range(3))
        scores = jnp.where(same, dot_last(qkv[at, q_cols], qkv[at, k_cols]) + bias[h], far_below)
        top = jnp.max(scores, axis=1, keepdims=True)
        expo = jnp.exp(scores - top)
        total = jnp.sum(expo, axis=1, keepdims=True)
        probs = (expo * (1.0 / total)).astype(BF16)
        ctx[at, q_cols] = flat_dot(probs, qkv[at, v_cols]).astype(BF16)
        lse[at, h : h + 1] = top + jnp.log(total)

    for s in range(2):
        for h in range(heads):
            steps["h" + str(s * heads + h)] = functools.partial(attend, s, h)

    @step
    def load_o():
        load = pltpu.make_async_copy(fo, vo, moves.at[3])
        load.start()
        load.wait()

    @step
    def residual():
        def body(at):
            value = tok_all[slot(*place()), at, :].astype(F32) + keep[at, :] * acc[at, :]
            resid[at, :] = value
            inv = lax.rsqrt(jnp.mean(value * value, axis=-1, keepdims=True) + eps)
            n2[at, :] = (value * inv * gain2[...]).astype(BF16)

        in_rows(0, rows, body)

    @step
    def gate_up():
        gu_load.wait()

        def body(m, _):
            at = pl.ds(pl.multiple_of(m * rows, rows), rows)
            value = flat_dot(n2_all[m], vgu[...])
            gu[at, :] = value
            hidden[at, :] = (gelu_tanh(value[:, :fc]) * value[:, fc:]).astype(BF16)
            return 0

        lax.fori_loop(0, 8, body, 0)
        start_all([last_moves[0], last_moves[2], last_moves[3]])

    @step
    def grad_f():
        last_moves[1].start()
        wide = 256
        for first in range(0, width, wide):
            left = cot_all[:, :, first : first + wide].reshape(8 * rows, wide)
            gf[first : first + wide, :] = dot_first(left, hidden[...]).astype(BF16)
        last_moves[4].start()

    for item in forward_order(types.SimpleNamespace(**steps)):
        item()
    for w in weights:
        weight_out(w)
    n1_move.wait()
    for move in last_moves:
        move.wait()


docs_per_sequence = 8
tok_share, cot_share, n2_share, attn_share = (1.0, 1.0, 0.375, 0.75)


def forward_order(n):
    return (
        n.bv, n.loadf, n.bk, n.yk, n.bo, n.ao, n.docs, n.t0, n.loadu, n.loadk,
        n.pairk, n.loadq, n.loado, n.yo, n.bq, n.pairv, n.ak, n.loadv, n.av, n.loadg,
        n.make_bias, n.t1, n.keepo, n.keepk, n.yv, n.keepq, n.onk, n.onpk, n.keepv, n.pairo,
        n.ono, n.bu, n.t2, n.pairq, n.onpv, n.c0, n.yq, n.aq, n.t3, n.onv,
        n.t4, n.keepu, n.onpo, n.onq, n.au, n.bf, n.onpq, n.norm, n.segments, n.inv,
        n.ink, n.inq, n.c1, n.pairu, n.project, n.ino, n.yf, n.h0, n.h1, n.h2,
        n.c2, n.h3, n.onu, n.bg, n.h4, n.ag, n.h5, n.h6, n.h7, n.load_o,
        n.yu, n.s0, n.s1, n.s2, n.s3, n.s4, n.s5, n.s6, n.s7, n.keepf,
        n.yg, n.pairg, n.c3, n.s8, n.s9, n.onpu, n.ong, n.onpg, n.pairf, n.keepg,
        n.s10, n.residual, n.n0, n.n1, n.ing, n.inu, n.af, n.onpf, n.n2, n.n3,
        n.onf, n.c4, n.n4, n.load_gu, n.gate_up, n.grad_f, n.inf,
    )


def forward(spans, tokens, cotangent, weights, ends, gain1, gain2, rel_table, onehot, hd, number):
    rows, width = tokens.shape
    length = 4 * rows
    total = weights[0].shape[0] * 4 * spans
    hc, fc = weights[0].shape[1] // 8, weights[4].shape[1] // 8
    heads = hc // hd
    dma, shape, vmem = pltpu.SemaphoreType.DMA, jax.ShapeDtypeStruct, pltpu.VMEM
    outs = pl.pallas_call(
        functools.partial(forward_kernel, spans, heads, hd),
        out_shape=[
            shape((8, rows, width), BF16),
            shape((8, rows, width), BF16),
            shape((8 * rows, width), BF16),
            shape((total, 3 * hc), BF16),
            shape((total, hc), BF16),
            shape((total, 2 * fc), BF16),
            shape((total, fc), BF16),
            shape((8 * rows, 2 * fc), F32),
            shape((8 * rows, fc), BF16),
            shape((total, fc), BF16),
            shape((8 * rows, 3 * hc), BF16),
            shape((8 * rows, hc), BF16),
            shape((8 * rows, heads), F32),
            shape((rows, width), F32),
            shape((2, length, 1), jnp.int32),
            shape((2, 1, length), jnp.int32),
            shape((rows, 1), F32),
            shape((heads, 2 * length), F32),
        ],
        in_specs=[any_space] * 9 + [in_vmem] * 5,
        out_specs=[any_space] * 10 + [in_vmem] * 8,
        scratch_shapes=[
            vmem((8, rows, width), BF16),
            vmem((8, rows, width), BF16),
            vmem((8, rows, width), BF16),
            vmem((8 * rows, width), BF16),
            vmem((total, 3 * hc), BF16),
            vmem((total, hc), BF16),
            vmem((total, 2 * fc), BF16),
            vmem((8 * rows, 2 * fc), F32),
            vmem((8 * rows, fc), BF16),
            vmem((total, fc), BF16),
            vmem((heads, length, length), F32),
            vmem((8, rows, width), BF16),
            vmem(ends.shape, jnp.int32),
            vmem((8, heads, 2 * length), F32),
            vmem((rows, width), F32),
            vmem((rows, width), BF16),
            vmem((4, weights[0].shape[0], hc), BF16),
            vmem((3, weights[4].shape[0], fc), BF16),
            vmem((rows, width), BF16),
            dma((7, 4 * spans - 1)),
            dma((7, 4 * spans - 1)),
            dma((7,)),
            dma((13,)),
        ]
        + [dma((9,)), dma((9,)), dma] * 3
        + scatter_scratch(rows, width),
        compiler_params=pltpu.CompilerParams(collective_id=number, has_side_effects=True, vmem_limit_bytes=62 * MIB),
    )(tokens, cotangent, *weights, ends, gain1[None, :], gain2[None, :], rel_table, onehot)
    return (outs[0].reshape(8 * rows, width), outs[1].reshape(8 * rows, width), *outs[2:])


def return_parts(spans, part, start, n, at, out, got_y, here, got_a, got_b, sends, recvs, local):
    a, y = lax.axis_index("a"), lax.axis_index("y")
    b, x, c = place()
    me, pair, x_me, x_pair = slot(b, x, c), slot(1 - b, x, c), slot(b, 1 - x, c), slot(1 - b, 1 - x, c)
    cols = pl.ds(start, n)
    count = got_b.shape[0]
    far = [lax.rem(a + k, spans) for k in range(1, spans)] + [a]
    held = [part.at[f, :, y, at, cols] if here is None else here.at[k] for k, f in enumerate(far)]

    def copy(src, dst, k, axis, to):
        return remote_to(src, dst, sends.at[k], recvs.at[k], axis, to)

    def place_in(member):
        return out.at[at, pl.ds(pl.multiple_of(member * n, 128), n)]

    to_y = [copy(part.at[f, :, 1 - y, at, cols], got_y.at[k], k, "y", 1 - y) for k, f in enumerate(far)]
    load = []
    if here is not None:
        load = [pltpu.make_async_copy(part.at[f, :, y, at, cols], here.at[k], local.at[k]) for k, f in enumerate(far)]
    over_a = [copy(held[k], got_a.at[k], spans + k, "a", f) for k, f in enumerate(far[:-1])]
    base = 2 * spans - 1
    last = held[-1]
    over_b = copy(last.at[1 - b], got_b, base, "b", 1 - b)
    x_own = copy(last.at[b], place_in(me), base + 1, "x", 1 - x)
    x_other = copy(got_b, place_in(pair), base + 2, "x", 1 - x)
    c_own = copy(last.at[b], place_in(me), base + 3, "c", 1 - c)
    c_other = copy(got_b, place_in(pair), base + 4, "c", 1 - c)
    c_x_own = copy(place_in(x_me), place_in(x_me), base + 5, "c", 1 - c)
    c_x_other = copy(place_in(x_pair), place_in(x_pair), base + 6, "c", 1 - c)
    keep_own = pltpu.make_async_copy(last.at[b], place_in(me), local.at[spans])
    keep_other = pltpu.make_async_copy(got_b, place_in(pair), local.at[spans + 1])

    def add(k, others):
        for half in range(2):

            def body(r, half=half):
                value = held[k][half, r, :].astype(F32)
                for other in others:
                    value = value + other[half, r, :].astype(F32)
                held[k][half, r, :] = value.astype(BF16)

            in_rows(0, count, body)

    def ready(k):
        to_y[k].wait_recv()
        for item in load[k : k + 1]:
            item.wait()

    def begin():
        start_all(to_y + load)

    def across():
        for k in range(spans - 1):
            ready(k)
            add(k, [got_y.at[k]])
            over_a[k].start()

    def finish():
        ready(spans - 1)
        for item in over_a:
            item.wait_recv()
        add(spans - 1, [got_y.at[spans - 1]] + [got_a.at[k] for k in range(spans - 1)])
        start_all([over_b, x_own, c_own, keep_own])

    def pass_on():
        over_b.wait_recv()
        start_all([x_other, c_other, keep_other])

    def share():
        x_own.wait_recv()
        c_x_own.start()
        x_other.wait_recv()
        c_x_other.start()

    def end():
        for item in (c_own, c_other, c_x_own, c_x_other):
            item.wait_recv()
        for item in (*to_y, *over_a, over_b, x_own, x_other, c_own, c_other, c_x_own, c_x_other):
            item.wait_send()
        keep_own.wait()
        keep_other.wait()

    return [begin, across, finish, pass_on, share, end]


def return_scratch(spans, count, n, copied):
    dma = pltpu.SemaphoreType.DMA
    one = pltpu.VMEM((spans, 2, count, n), BF16)
    return [
        one,
        *([one] if copied else []),
        pltpu.VMEM((max(spans - 1, 1), 2, count, n), BF16),
        pltpu.VMEM((count, n), BF16),
        dma((2 * spans + 6,)),
        dma((2 * spans + 6,)),
        dma((spans + 2,)),
    ]


def sum_parts(spans, bufs, gots, sends, recvs):
    a, y = lax.axis_index("a"), lax.axis_index("y")
    b, x, c = place()
    steps = []

    def hop(step, targets):
        copies = [
            remote_to(buf, got.at[step + k], sends.at[i, step + k], recvs.at[i, step + k], axis, other)
            for k, (axis, other) in enumerate(targets)
            for i, (buf, got) in enumerate(zip(bufs, gots))
        ]

        def begin():
            start_all(copies)

        def end():
            for copy in copies:
                copy.wait()
            for buf, got in zip(bufs, gots):
                buf[...] = functools.reduce(jnp.add, [buf[...]] + [got[step + k] for k in range(len(targets))])

        steps.extend([begin, end])

    for step, target in enumerate((("c", 1 - c), ("x", 1 - x), ("b", 1 - b), ("y", 1 - y))):
        hop(step, [target])
    if spans > 1:
        hop(4, [("a", lax.rem(a + k, spans)) for k in range(1, spans)])
    return steps


def gelu_both(v):
    inner = 0.7978845608028654 * (v + 0.044715 * (v * v * v))
    t = jnp.tanh(inner)
    slope = 0.7978845608028654 * (1.0 + 0.134145 * (v * v))
    return 0.5 * v * (1.0 + t), 0.5 * (1.0 + t) + 0.5 * v * (1.0 - t * t) * slope


def backward_kernel(
    spans, heads, hd, hidden, gf, n2, cot_all, gu, wgu, wf, wqkv, wo, n1, qkv_all, ctx_all, lse_all,
    resid, tokens, cotangent, keep, gain1, gain2, vec, segc, segr, onehot,
    dattn_all, o_f, o_g, o_u, o_o, o_q, o_k, o_v, out, grad_input, sums, table,
    sib, mid, diag, last, sib2, mid2, diag2, last2, acc, acc2, dattn, dresid, held, parts, ggu, gatt, diags,
    got_sums, got_table, moves, *scratch
):
    total, hc = wo.shape
    fc = gf.shape[4]
    rows, width = resid.shape
    count = gf.shape[3]
    length = segr.shape[2]
    scratch = list(scratch)

    def take(n):
        out = scratch[:n]
        del scratch[:n]
        return out

    meet_all(spans)
    dn2_source, dn1_source, out_source = (types.SimpleNamespace(parts=parts) for _ in range(3))
    dn2_sum = scatter_parts(dn2_share, dn2_source, acc, sib, mid, diag, last, *take(2))
    dn1_sum = scatter_parts(dn1_share, dn1_source, acc, sib, mid, diag, last, *take(2))
    out_sum = scatter_parts(out_share, out_source, acc2, sib2, mid2, diag2, last2, *take(2))
    dattn_in = gather_parts(dattn_share, dattn, dattn_all, *take(3))
    summed = sum_parts(spans, [sums, table], [got_sums, got_table], *take(2))
    pieces = []
    for part, result in ((gf, o_f), (ggu.at[0], o_g), (ggu.at[1], o_u)):
        for first in (0, count // 2):
            at = pl.ds(first, count // 2)
            if part is gf:
                pieces.append(return_parts(spans, part, 0, fc, at, result, *take(7)))
            else:
                got_y, got_a, got_b, *sems = take(6)
                pieces.append(return_parts(spans, part, 0, fc, at, result, got_y, None, got_a, got_b, *sems))
    for i, result in enumerate((o_o, o_q, o_k, o_v)):
        got_y, got_a, got_b, *sems = take(6)
        pieces.append(return_parts(spans, gatt.at[i], 0, hc, pl.ds(0, count), result, got_y, None, got_a, got_b, *sems))
    steps = {}
    for name, piece in zip(("f", "F", "g", "G", "u", "U", "o", "q", "k", "v"), pieces):
        for k, item in enumerate(piece):
            steps[name + str(k)] = item
    for name, parts_of in (("d", dn2_sum), ("e", dn1_sum), ("x", out_sum), ("n", dattn_in), ("s", summed)):
        for k, item in enumerate(parts_of):
            steps[name + "_" + str(k)] = item

    def step(function):
        steps[function.__name__] = function
        return function

    cot_load = pltpu.make_async_copy(cot_all, held, moves.at[1])
    n2_load = pltpu.make_async_copy(n2, held, moves.at[11])
    n1_load = pltpu.make_async_copy(n1, held, moves.at[10])

    @step
    def setup():
        sums[...] = jnp.zeros_like(sums)
        table[...] = jnp.zeros_like(table)

    @step
    def second_norm():
        def body(at):
            value, dn2 = resid[at, :], acc[at, :]
            inv = lax.rsqrt(jnp.mean(value * value, axis=-1, keepdims=True) + eps)
            inner = dn2 * gain2[...]
            grad = (
                cotangent[at, :].astype(F32)
                + inv * inner
                - value * (inv * inv * inv * jnp.mean(inner * value, axis=-1, keepdims=True))
            )
            dresid[at, :] = grad
            sums[1:2, :] += jnp.sum(dn2 * value * inv, axis=0, keepdims=True)
            sums[2:3, :] += jnp.sum(value * value, axis=0, keepdims=True)
            dattn[at, :] = (keep[at, :] * grad).astype(BF16)

        in_rows(0, rows, body)

    wide = max(count, 256)

    def weight_grad(store, factor):
        for first in range(0, total, wide):
            value = dot_first(held[:, first : first + wide], factor).astype(BF16)
            for owner in range(first // count, (first + wide) // count):
                at = owner * count - first
                store[owner // 4, owner // 2 % 2, owner % 2] = value[at : at + count]

    @step
    def first_norm():
        def body(at):
            value, dn1 = tokens[at, :].astype(F32), acc[at, :]
            inv = lax.rsqrt(jnp.mean(value * value, axis=-1, keepdims=True) + eps)
            inner = dn1 * gain1[...]
            grad_input[at, :] = (
                dresid[at, :]
                + inv * inner
                - value * (inv * inv * inv * jnp.mean(inner * value, axis=-1, keepdims=True))
            )
            sums[0:1, :] += jnp.sum(dn1 * value * inv, axis=0, keepdims=True)

        in_rows(0, rows, body)

    @step
    def final():
        def body(at):
            value = resid[at, :] + acc2[at, :]
            out[at, :] = value.astype(BF16)
            sums[3:4, :] += jnp.sum(value * value, axis=0, keepdims=True)

        in_rows(0, rows, body)

    @step
    def tables():
        buckets = lax.dot_general(
            diags[...], onehot[...], (((1,), (1,)), ((), ())), precision=highest, preferred_element_type=F32
        )
        table[slot(*place()), 0:heads, 0 : buckets.shape[1]] = buckets

    def first_half(v_dgu, v_out):
        out_source.parts = v_out
        @step
        def dhidden():
            def inner(v_wf, v_gu):
                wf_load = pltpu.make_async_copy(wf, v_wf, moves.at[0])

                def fetch_gu(m):
                    at = pl.ds(pl.multiple_of(m * rows, rows), rows)
                    slot_of = lax.rem(m, 2)
                    return pltpu.make_async_copy(gu.at[at], v_gu.at[slot_of], moves.at[12 + slot_of])

                start_all([cot_load, wf_load, fetch_gu(0)])
                wf_load.wait()
                cot_load.wait()

                def body(m, _):
                    at = pl.ds(pl.multiple_of(m * rows, rows), rows)

                    @pl.when(m < 7)
                    def _():
                        fetch_gu(m + 1).start()

                    grad = flat_dot(held[at, :], v_wf[...])
                    fetch_gu(m).wait()
                    both = v_gu[lax.rem(m, 2)]
                    activ, slope = gelu_both(both[:, :fc])
                    v_dgu[at, :fc] = (grad * both[:, fc:] * slope).astype(BF16)
                    v_dgu[at, fc:] = (grad * activ).astype(BF16)
                    return 0

                lax.fori_loop(0, 8, body, 0)
                n2_load.start()

            pl.run_scoped(inner, pltpu.VMEM(wf.shape, BF16), pltpu.VMEM((2, rows, 2 * fc), F32))

        def with_out(v_wf, v_hidden):
            loads = [pltpu.make_async_copy(wf, v_wf, moves.at[0]), pltpu.make_async_copy(hidden, v_hidden, moves.at[12])]

            def make(m):
                at = pl.ds(pl.multiple_of(m * rows, rows), rows)
                v_out[m] = dot_last(v_hidden[at, :], v_wf[...]).astype(BF16)

            out_source.make = make
            start_all(loads)
            for load in loads:
                load.wait()
            for item in backward_out(types.SimpleNamespace(**steps)):
                item()

        def with_dn2(v_wgu):
            load = pltpu.make_async_copy(wgu, v_wgu, moves.at[0])

            def make(m):
                at = pl.ds(pl.multiple_of(m * rows, rows), rows)
                parts[m] = dot_last(v_dgu[at, :], v_wgu[...]).astype(BF16)

            dn2_source.make = make
            load.start()
            load.wait()
            for item in backward_dn2(types.SimpleNamespace(**steps)):
                item()

        @step
        def grad_g():
            n2_load.wait()
            weight_grad(ggu.at[0], v_dgu[:, :fc])

        @step
        def grad_u():
            weight_grad(ggu.at[1], v_dgu[:, fc:])

        for item in backward_start(types.SimpleNamespace(**steps)):
            item()
        pl.run_scoped(with_dn2, pltpu.VMEM(wgu.shape, BF16))
        pl.run_scoped(with_out, pltpu.VMEM(wf.shape, BF16), pltpu.VMEM(hidden.shape, BF16))
        for item in backward_first(types.SimpleNamespace(**steps)):
            item()

    def second_half(v_qkv, qkv, ctx, lse, dctx, dqkv, shear, v_o):
        loads = [
            pltpu.make_async_copy(src, dst, moves.at[k])
            for src, dst, k in ((wo, v_o, 1), (qkv_all, qkv, 12), (ctx_all, ctx, 13), (lse_all, lse, 14))
        ]
        qkv_load = pltpu.make_async_copy(wqkv, v_qkv, moves.at[0])
        start_all([*loads, qkv_load])
        steps["in_qkv"] = qkv_load.wait

        @step
        def to_ctx():
            copies = [
                pltpu.make_async_copy(dattn_all.at[m], held.at[pl.ds(m * rows, rows)], moves.at[2 + m]) for m in range(8)
            ]
            start_all(copies)
            for copy in (*loads, *copies):
                copy.wait()

            def body(m, _):
                at = pl.ds(pl.multiple_of(m * rows, rows), rows)
                dctx[at, :] = flat_dot(held[at, :], v_o[...]).astype(BF16)
                return 0

            lax.fori_loop(0, 8, body, 0)

        @step
        def grad_o():
            weight_grad(gatt.at[0], ctx[...])
            n1_load.start()

        def attend_back(h):
            bias = shear_bias(vec[h : h + 1, :], length)
            q_cols, k_cols, v_cols = (slice(k * hc + h * hd, k * hc + (h + 1) * hd) for k in range(3))
            for s in range(2):
                at = slice(s * length, (s + 1) * length)
                same = segc[s] == segr[s]
                q, k, v, d = qkv[at, q_cols], qkv[at, k_cols], qkv[at, v_cols], dctx[at, q_cols]
                scores = jnp.where(same, dot_last(q, k) + bias, far_below)
                probs = jnp.exp(scores - lse[at, h : h + 1])
                dprobs = dot_last(d, v)
                dqkv[at, v_cols] = dot_first(probs.astype(BF16), d).astype(BF16)
                product = probs * dprobs
                dscores = product - probs * jnp.sum(product, axis=1, keepdims=True)
                if s == 0:
                    shear[...] = dscores
                else:
                    shear[...] += dscores
                dlogits = dscores.astype(BF16)
                dqkv[at, q_cols] = flat_dot(dlogits, k).astype(BF16)
                dqkv[at, k_cols] = dot_first(dlogits, q).astype(BF16)

            def shift(g, carry):
                group = shear[pl.ds(pl.multiple_of(g * 8, 8), 8), :]
                group = jnp.concatenate([group, jnp.zeros_like(group)], axis=1)
                return carry + pltpu.roll(group, 2 * length - g * 8, 1)

            shifted = lax.fori_loop(0, length // 8, shift, jnp.zeros((8, 2 * length), F32), unroll=8)
            line = shifted[0:1, :]
            for r in range(1, 8):
                line = line + pltpu.roll(shifted[r : r + 1, :], 2 * length - r, 1)
            diags[h : h + 1, :] = line

        for h in range(heads):
            steps["h" + str(h)] = functools.partial(attend_back, h)

        for i, name in enumerate(("q", "k", "v")):

            def grad_of(i=i):
                if i == 0:
                    n1_load.wait()
                weight_grad(gatt.at[1 + i], dqkv[:, i * hc : (i + 1) * hc])

            steps["grad_" + name] = grad_of

        def make(m):
            at = pl.ds(pl.multiple_of(m * rows, rows), rows)
            parts[m] = dot_last(dqkv[at, :], v_qkv[...]).astype(BF16)

        dn1_source.make = make

        for item in backward_second(types.SimpleNamespace(**steps)):
            item()

    pl.run_scoped(first_half, pltpu.VMEM((8 * rows, 2 * fc), BF16), pltpu.VMEM((8, rows, width), BF16))
    pl.run_scoped(
        second_half,
        pltpu.VMEM((total, 3 * hc), BF16),
        pltpu.VMEM((8 * rows, 3 * hc), BF16),
        pltpu.VMEM((8 * rows, hc), BF16),
        pltpu.VMEM((8 * rows, heads), F32),
        pltpu.VMEM((8 * rows, hc), BF16),
        pltpu.VMEM((8 * rows, 3 * hc), BF16),
        pltpu.VMEM((length, length), F32),
        pltpu.VMEM((total, hc), BF16),
    )
    for name in ("f", "F", "g", "G", "u", "U", "o", "q", "k", "v"):
        steps[name + "5"]()


dn2_share, dattn_share, dn1_share, out_share = (0.625, 0.75, 0.75, 0.75)


def backward_start(n):
    return (
        n.F0, n.dhidden, n.F1,
    )


def backward_dn2(n):
    return (
        n.d_0, n.d_4, n.f0, n.d_1, n.d_2, n.d_6, n.d_5, n.d_3,
    )


def backward_out(n):
    return (
        n.d_9, n.d_8, n.d_7, n.F2, n.grad_g, n.g0, n.f1, n.setup, n.G0, n.d_10,
        n.second_norm, n.n_0, n.grad_u, n.x_0, n.u0, n.x_1, n.x_2, n.x_4, n.n_1, n.x_3,
        n.x_6, n.g1, n.n_2, n.U0, n.x_5, n.x_8, n.x_7, n.f2, n.x_9, n.G1,
    )


def backward_first(n):
    return (
    )


def backward_second(n):
    return (
        n.F3, n.n_3, n.n_4, n.u1, n.to_ctx, n.h0, n.grad_o, n.h1, n.U1, n.f3,
        n.g2, n.h2, n.o0, n.G2, n.h3, n.u2, n.in_qkv, n.o1, n.e_0, n.e_1,
        n.e_4, n.e_2, n.grad_q, n.x_10, n.q0, n.final, n.e_3, n.e_6, n.u3, n.tables,
        n.grad_k, n.e_5, n.e_9, n.G3, n.e_8, n.k0, n.U2, n.g3, n.q1, n.k1,
        n.grad_v, n.v0, n.q2, n.e_7, n.e_10, n.first_norm, n.s_0, n.s_1, n.s_2, n.g4,
        n.o2, n.U3, n.v1, n.q3, n.s_3, n.f4, n.G4, n.F4, n.s_4, n.k2,
        n.o3, n.s_5, n.s_6, n.v2, n.U4, n.s_7, n.s_8, n.k3, n.o4, n.v3,
        n.u4, n.k4, n.q4, n.s_9, n.v4,
    )


def backward(
    spans, hidden, grad_f, n2, cot_all, gu, wgu, wf, wqkv, wo, n1, qkv, ctx, lse, resid, tokens, cotangent, keep, gain1, gain2, vec, segc, segr, onehot, hd, number
):
    rows, width = tokens.shape
    heads, length = vec.shape[0], segr.shape[2]
    total, hc = wo.shape
    fc = grad_f.shape[1]
    count = total // (4 * spans)
    dma, shape, vmem = pltpu.SemaphoreType.DMA, jax.ShapeDtypeStruct, pltpu.VMEM
    scratch = scatter_scratch(rows, width)[:4] + scatter_scratch(rows, width)[:4]
    scratch += [
        vmem((rows, width), F32),
        vmem((rows, width), F32),
        vmem((rows, width), BF16),
        vmem((rows, width), F32),
        vmem((8 * rows, width), BF16),
        vmem((8, rows, width), BF16),
        vmem((2, spans, 2, 2, count, fc), BF16),
        vmem((4, spans, 2, 2, count, hc), BF16),
        vmem((heads, 2 * length), F32),
        vmem((3 + spans, 8, width), F32),
        vmem((3 + spans, 8, 8, 128), F32),
        dma((15,)),
    ]
    scratch += [dma((10,))] * 6
    scratch += [dma((9,)), dma((9,)), dma, dma((2, 3 + spans)), dma((2, 3 + spans))]
    for i in range(6):
        scratch += return_scratch(spans, count // 2, fc, i < 2)
    for _ in range(4):
        scratch += return_scratch(spans, count, hc, False)
    outs = pl.pallas_call(
        functools.partial(backward_kernel, spans, heads, hd),
        out_shape=[shape((8, rows, width), BF16)]
        + [shape((count, 8 * fc), BF16)] * 3
        + [shape((count, 8 * hc), BF16)] * 4
        + [shape((rows, width), BF16), shape((rows, width), F32), shape((8, width), F32), shape((8, 8, 128), F32)],
        in_specs=[any_space] * 13 + [in_vmem] * 10,
        out_specs=[any_space] * 8 + [in_vmem] * 4,
        scratch_shapes=scratch,
        compiler_params=pltpu.CompilerParams(collective_id=number, has_side_effects=True, vmem_limit_bytes=62 * MIB),
    )(
        hidden,
        grad_f.reshape(spans, 2, 2, count, fc),
        n2,
        cot_all,
        gu,
        wgu,
        wf,
        wqkv,
        wo,
        n1,
        qkv,
        ctx,
        lse,
        resid,
        tokens,
        cotangent,
        keep,
        gain1[None, :],
        gain2[None, :],
        vec,
        segc,
        segr,
        onehot,
    )
    return outs[1:]


def per_device(
    tokens,
    w_query,
    w_key,
    w_value,
    w_attn_out,
    w_gate,
    w_up,
    w_ff_out,
    gain_attn,
    gain_ffn,
    rel_table,
    doc_lengths,
    cotangent,
):
    rows, width = tokens.shape
    n_buckets, heads_all = rel_table.shape
    heads = heads_all // 8
    hc = w_query.shape[1] // 8
    fc = w_gate.shape[1] // 8
    hd = hc // heads
    length = 4 * rows

    ends = jnp.cumsum(doc_lengths, axis=1).astype(jnp.int32)
    offset = np.arange(-length, length)
    distance = np.abs(offset)
    far = 8 + np.sum(distance[:, None] >= np.array(thresholds), axis=1)
    bucket = np.where(offset > 0, 16, 0) + np.where(distance < 8, distance, far)
    onehot = (np.arange(n_buckets)[:, None] == bucket[None, :]).astype(np.float32)
    order = np.roll(onehot, length, axis=1)

    spans = lax.axis_size("a")
    weights = (w_query, w_key, w_value, w_attn_out, w_gate, w_up, w_ff_out)
    (cot_all, n2, n1, wqkv, wo, wgu, wf, gate_up, hidden, grad_f, qkv, ctx, lse, resid, segc, segr, keep, vec) = forward(
        spans, tokens, cotangent, weights, ends, gain_attn, gain_ffn, rel_table, jnp.asarray(onehot), hd, 0
    )
    grad_f, grad_g, grad_u, grad_o, grad_q, grad_k, grad_v, out, grad_input, sums, table_sums = backward(
        spans, hidden, grad_f, n2, cot_all, gate_up, wgu, wf, wqkv, wo, n1, qkv, ctx, lse, resid, tokens, cotangent, keep, gain_attn, gain_ffn,
        vec, segc, segr, jnp.asarray(order), hd, 1
    )
    dtable = table_sums[:, :heads, :n_buckets].reshape(heads_all, n_buckets).T
    entries = rows * width * 16 * spans
    norms = jnp.sqrt(jnp.sum(sums[2:4], axis=1) / entries)
    return (
        out,
        grad_input,
        grad_q.astype(F32),
        grad_k.astype(F32),
        grad_v.astype(F32),
        grad_o.astype(F32),
        grad_g.astype(F32),
        grad_u.astype(F32),
        grad_f.astype(F32),
        sums[0],
        sums[1],
        dtable,
        norms,
    )


def solution(mesh):
    owners, copies = mesh.shape["fsdp"], mesh.shape["rep"]
    finer = Mesh(mesh.devices.reshape(owners // 4, 2, 2, copies // 2, 2), ("a", "b", "y", "x", "c"))
    owner = ("a", "b", "y")
    piece = P(owner + ("x", "c"), None)
    shard = P(owner, None)
    return jax.shard_map(
        per_device,
        mesh=finer,
        in_specs=(piece,) + (shard,) * 7 + (P(), P(), P(), shard, piece),
        out_specs=(piece, piece) + (shard,) * 7 + (P(), P(), P(), P()),
        check_vma=False,
    )
```

```python
import functools
import types

import jax
import jax.numpy as jnp
import numpy as np
from jax import lax
from jax.experimental import pallas as pl
from jax.experimental.pallas import tpu as pltpu
from jax.sharding import Mesh
from jax.sharding import PartitionSpec as P

eps = 1e-06
thresholds = (12, 16, 23, 32, 46, 64, 91)
highest = lax.Precision.HIGHEST
F32 = jnp.float32
BF16 = jnp.bfloat16
far_below = -1e30
MESH = pl.DeviceIdType.MESH
swap = ((0, 1), (1, 0))
MIB = 1 << 20


def gelu_tanh(v):
    return jax.nn.gelu(v, approximate=True)


def flat_dot(left, right):
    return jnp.dot(left, right, preferred_element_type=F32)


def dot_last(left, right):
    return lax.dot_general(left, right, (((1,), (1,)), ((), ())), preferred_element_type=F32)


def dot_first(left, right):
    return lax.dot_general(left, right, (((0,), (0,)), ((), ())), preferred_element_type=F32)


def shear_bias(row, length):
    wide = jnp.broadcast_to(row, (length, 2 * length))
    return pltpu.roll(wide, length, 1, stride=1, stride_axis=0)[:, :length]


def place():
    return lax.axis_index("b"), lax.axis_index("x"), lax.axis_index("c")


def slot(b, x, c):
    return b * 4 + x * 2 + c


def meet():
    b, x, c = place()
    barrier = pltpu.get_barrier_semaphore()
    for axis, other in (("b", 1 - b), ("x", 1 - x), ("c", 1 - c)):
        pl.semaphore_signal(barrier, inc=1, device_id={axis: other}, device_id_type=MESH)
    pl.semaphore_wait(barrier, 3)


def start_all(copies):
    for copy in copies:
        copy.start()


def remote(src, dst, sends, recvs, n, axis):
    return pltpu.make_async_remote_copy(
        src_ref=src,
        dst_ref=dst,
        send_sem=sends.at[n],
        recv_sem=recvs.at[n],
        device_id={axis: 1 - lax.axis_index(axis)},
        device_id_type=MESH,
    )


def gather_parts(share, src, out, sends, recvs, local):
    b, x, c = place()
    rows = src.shape[0]
    by_x = int(rows * share) // 16 * 16
    first, rest = pl.ds(0, by_x), pl.ds(by_x, rows - by_x)
    own, at_x, at_b, at_d = slot(b, x, c), slot(b, 1 - x, c), slot(1 - b, x, c), slot(1 - b, 1 - x, c)
    over_x = remote(src, out.at[own], sends, recvs, 0, "x")
    over_b = remote(src, out.at[own], sends, recvs, 1, "b")
    on_x = remote(out.at[at_b, first], out.at[at_b, first], sends, recvs, 2, "x")
    over_c = remote(src, out.at[own], sends, recvs, 3, "c")
    x_on_c = remote(out.at[at_x], out.at[at_x], sends, recvs, 4, "c")
    b_on_c = remote(out.at[at_b], out.at[at_b], sends, recvs, 5, "c")
    d_on_c = [remote(out.at[at_d, first], out.at[at_d, first], sends, recvs, 6, "c")]
    on_b = []
    if by_x < rows:
        on_b = [remote(out.at[at_x, rest], out.at[at_x, rest], sends, recvs, 7, "b")]
        d_on_c.append(remote(out.at[at_d, rest], out.at[at_d, rest], sends, recvs, 8, "c"))
    keep = pltpu.make_async_copy(src, out.at[own], local)

    def begin():
        for copy in (over_b, over_x, over_c, keep):
            copy.start()

    def from_x():
        over_x.wait_recv()
        for copy in (*on_b, x_on_c):
            copy.start()

    def from_b():
        over_b.wait_recv()
        on_x.start()
        b_on_c.start()

    def from_both():
        for came, on in zip([on_x, *on_b], d_on_c):
            came.wait_recv()
            on.start()

    def end():
        for copy in d_on_c:
            copy.wait_recv()
        for copy in (over_x, over_b, on_x, *on_b, over_c, x_on_c, b_on_c, *d_on_c):
            copy.wait_send()

    def from_c():
        over_c.wait_recv()
        keep.wait()

    return [begin, from_x, from_b, from_both, from_c, x_on_c.wait_recv, b_on_c.wait_recv, end]


def in_rows(first, count, body, chunk=16):
    def step(i, _):
        body(pl.ds(pl.multiple_of(first + i * chunk, chunk), chunk))
        return 0

    lax.fori_loop(0, count // chunk, step, 0)


def scatter_parts(share, source, acc, sib, out, diag, last, sends, recvs):
    b, x, c = place()
    rows = sib.shape[1]
    by_x = int(rows * share) // 16 * 16
    seats = [(b, x), (b, 1 - x), (1 - b, x), (1 - b, 1 - x)]
    here, there = [slot(*seat, c) for seat in seats], [slot(*seat, 1 - c) for seat in seats]
    to_core = [remote(sib.at[q], sib.at[q], sends, recvs, q, "c") for q in range(4)]

    def over(n, to, first, count, k, axis):
        at = pl.ds(first, count)
        return remote(out.at[n, at], to.at[at], sends, recvs, k, axis)

    rest = rows - by_x
    d_x = over(2, diag, 0, by_x, 4, "x")
    x_first, b_last = over(0, last.at[0], 0, by_x, 5, "x"), over(1, last.at[1], 0, by_x, 6, "b")
    d_b, x_last, b_first = [], [], []
    if rest:
        d_b = [over(2, diag, by_x, rest, 7, "b")]
        x_last, b_first = [over(0, last.at[0], by_x, rest, 8, "x")], [over(1, last.at[1], by_x, rest, 9, "b")]

    def both(q, at):
        return source.parts[here[q], at, :].astype(F32) + sib[q, at, :].astype(F32)

    def put(n, q, first, count, more=False):
        def body(at):
            value = both(q, at)
            if more:
                value = value + diag[at, :].astype(F32)
            out[n, at, :] = value.astype(BF16)

        if count:
            in_rows(first, count, body)

    def begin(q):
        source.make(there[q])
        remote(source.parts.at[there[q]], sib.at[q], sends, recvs, q, "c").start()
        source.make(here[q])

    def to_diagonal():
        to_core[3].wait_recv()
        put(2, 3, 0, by_x)
        d_x.start()
        put(2, 3, by_x, rest)
        start_all(d_b)

    def to_x():
        to_core[1].wait_recv()
        put(0, 1, 0, by_x)
        x_first.start()

    def to_b():
        to_core[2].wait_recv()
        put(1, 2, by_x, rest)
        start_all(b_first)

    def keep():
        to_core[0].wait_recv()

        def own(at):
            acc[at, :] = both(0, at)

        in_rows(0, rows, own)

    def on_x():
        for copy in d_b:
            copy.wait_recv()
        put(0, 1, by_x, rest, True)
        start_all(x_last)

    def on_b():
        d_x.wait_recv()
        put(1, 2, 0, by_x, True)
        b_last.start()
        for copy in to_core:
            copy.wait_send()

    def end():
        for copy in (x_first, *b_first, *x_last, b_last):
            copy.wait_recv()
        for copy in (d_x, *d_b, x_first, *b_first, *x_last, b_last):
            copy.wait_send()

        def finish(at):
            acc[at, :] += last[0, at, :].astype(F32) + last[1, at, :].astype(F32)

        in_rows(0, rows, finish)

    makes = [functools.partial(begin, q) for q in (3, 1, 2, 0)]
    return [*makes, to_diagonal, to_x, to_b, keep, on_x, on_b, end]


def scatter_scratch(rows, width):
    return [
        pltpu.VMEM((4, rows, width), BF16),
        pltpu.VMEM((3, rows, width), BF16),
        pltpu.VMEM((rows, width), BF16),
        pltpu.VMEM((2, rows, width), BF16),
        pltpu.SemaphoreType.DMA((10,)),
        pltpu.SemaphoreType.DMA((10,)),
    ]


any_space = pl.BlockSpec(memory_space=pl.ANY)
in_vmem = pl.BlockSpec(memory_space=pltpu.VMEM)


def remote_to(src, dst, send, recv, axis, to):
    return pltpu.make_async_remote_copy(
        src_ref=src, dst_ref=dst, send_sem=send, recv_sem=recv, device_id={axis: to}, device_id_type=MESH
    )


def meet_all(spans):
    a, y = lax.axis_index("a"), lax.axis_index("y")
    b, x, c = place()
    barrier = pltpu.get_barrier_semaphore()
    others = [("b", 1 - b), ("x", 1 - x), ("c", 1 - c), ("y", 1 - y)] + [("a", lax.rem(a + k, spans)) for k in range(1, spans)]
    for axis, other in others:
        pl.semaphore_signal(barrier, inc=1, device_id={axis: other}, device_id_type=MESH)
    pl.semaphore_wait(barrier, len(others))


def fetch_parts(spans, shards, fulls, stages, sends, recvs, local):
    a, y = lax.axis_index("a"), lax.axis_index("y")
    b, x, c = place()
    me, pair = slot(b, x, c), slot(1 - b, x, c)
    count = shards[0].shape[0]

    def rows(at_a, at_b, at_y):
        return pl.ds(pl.multiple_of((at_a * 4 + at_b * 2 + at_y) * count, count), count)

    weights = []
    for i, (shard, (full, start)) in enumerate(zip(shards, fulls)):
        n = shard.shape[1] // 8
        cols = pl.ds(start, n)
        mine = shard.at[:, pl.ds(pl.multiple_of(me * n, 128), n)]
        theirs = shard.at[:, pl.ds(pl.multiple_of(pair * n, 128), n)]
        own, other = rows(a, b, y), rows(a, 1 - b, y)

        def block(at, full=full, cols=cols):
            return full.at[at, cols]

        def copy(src, dst, k, axis, to, i=i):
            return remote_to(src, dst, sends.at[i, k], recvs.at[i, k], axis, to)

        copies = {
            "load": pltpu.make_async_copy(mine, stages[i], local.at[i]),
            "keep": pltpu.make_async_copy(stages[i], block(own), local.at[i]),
            "b": copy(theirs, block(own), 0, "b", 1 - b),
            "y": copy(mine, block(own), 1, "y", 1 - y),
            "y_pair": copy(block(other), block(other), 2, "y", 1 - y),
            "a": [],
            "a_pair": [],
            "on": [],
            "on_pair": [],
        }
        for k in range(1, spans):
            to, source = lax.rem(a + k, spans), lax.rem(a + spans - k, spans)
            copies["a"].append(copy(mine, block(own), 4 * k - 1, "a", to))
            copies["a_pair"].append(copy(block(other), block(other), 4 * k, "a", to))
            far, far_pair = block(rows(source, b, y)), block(rows(source, 1 - b, y))
            copies["on"].append(copy(far, far, 4 * k + 1, "y", 1 - y))
            copies["on_pair"].append(copy(far_pair, far_pair, 4 * k + 2, "y", 1 - y))
        weights.append(copies)
    return weights


def pair_in(copies):
    copies["b"].wait_recv()
    start_all([*copies["a_pair"], copies["y_pair"]])


def hand_on(copies, came, on):
    for got, copy in zip(copies[came], copies[on]):
        got.wait_recv()
        copy.start()


def own_in(copies):
    copies["load"].wait()
    copies["keep"].start()


def weight_in(copies):
    copies["keep"].wait()
    for copy in (copies["y"], copies["y_pair"], *copies["on"], *copies["on_pair"]):
        copy.wait_recv()


def weight_out(copies):
    for copy in (copies["b"], copies["y"], copies["y_pair"]):
        copy.wait_send()
    for kind in ("a", "a_pair", "on", "on_pair"):
        for copy in copies[kind]:
            copy.wait_send()


def forward_kernel(
    spans, heads, hd, tokens, cotangent, wq, wk, wv, wo, wg, wu, wf, ends, gain1, gain2, rel_table, onehot,
    cot_out, n2_out, n1_out, fqkv, fo, fgu, ff, gu_out, hidden_out, gf_out, qkv, ctx, lse, resid, segc, segr, keep, vec,
    tok_all, cot_all, n2_all, n1, vqkv, vo, vgu, gu, hidden, gf, bias, parts, pair_ends, vecs, acc, n2, mine_small, mine_large, cot_own, sends, recvs, local, moves, *scratch
):
    hc, fc = wq.shape[1] // 8, wg.shape[1] // 8
    rows, width = tok_all.shape[1:]
    length = segr.shape[2]
    b, x, c = place()
    meet_all(spans)
    fulls = [(fqkv, 0), (fqkv, hc), (fqkv, 2 * hc), (fo, 0), (fgu, 0), (fgu, fc), (ff, 0)]
    stages = [mine_small.at[i] for i in range(4)] + [mine_large.at[i] for i in range(3)]
    weights = fetch_parts(spans, [wq, wk, wv, wo, wg, wu, wf], fulls, stages, sends, recvs, local)
    tok = gather_parts(tok_share, tokens, tok_all, *scratch[0:3])
    cot = gather_parts(cot_share, cot_own, cot_all, *scratch[3:6])
    n2s = gather_parts(n2_share, n2, n2_all, *scratch[6:9])

    def make_part(m):
        at = pl.ds(pl.multiple_of(m * rows, rows), rows)
        parts[m] = dot_last(ctx[at, :], vo[...]).astype(BF16)

    summed = scatter_parts(attn_share, types.SimpleNamespace(make=make_part, parts=parts), acc, *scratch[9:])
    cot_load = pltpu.make_async_copy(cotangent, cot_own, moves.at[4])
    cot_load.start()
    start_cot = cot[0]

    def cot_begin():
        cot_load.wait()
        start_cot()

    cot[0] = cot_begin
    pair_docs = remote_to(ends, pair_ends, moves.at[5], moves.at[6], "b", 1 - b)
    gu_load = pltpu.make_async_copy(fgu, vgu, moves.at[0])
    last_moves = [
        pltpu.make_async_copy(n2_all, n2_out, moves.at[7]),
        pltpu.make_async_copy(cot_all, cot_out, moves.at[8]),
        pltpu.make_async_copy(gu, gu_out, moves.at[9]),
        pltpu.make_async_copy(hidden, hidden_out, moves.at[10]),
        pltpu.make_async_copy(gf, gf_out, moves.at[11]),
    ]
    n1_move = pltpu.make_async_copy(n1, n1_out, moves.at[1])
    names = ("q", "k", "v", "o", "g", "u", "f")
    steps = {}
    for name, w in zip(names, weights):
        steps["b" + name] = w["b"].start
        steps["y" + name] = w["y"].start
        steps["load" + name] = w["load"].start
        steps["keep" + name] = functools.partial(own_in, w)
        steps["a" + name] = functools.partial(start_all, w["a"])
        steps["pair" + name] = functools.partial(pair_in, w)
        steps["on" + name] = functools.partial(hand_on, w, "a", "on")
        steps["onp" + name] = functools.partial(hand_on, w, "a_pair", "on_pair")
        steps["in" + name] = functools.partial(weight_in, w)
    for name, parts_of in (("t", tok), ("c", cot), ("n", n2s), ("s", summed)):
        for k, step in enumerate(parts_of):
            steps[name + str(k)] = step

    def step(function):
        steps[function.__name__] = function
        return function

    steps["docs"] = pair_docs.start
    steps["load_gu"] = gu_load.start

    @step
    def make_bias():
        every = lax.dot_general(
            rel_table[...], onehot[...], (((0,), (0,)), ((), ())), precision=highest, preferred_element_type=F32
        )
        for m in range(8):
            vecs[m] = every[m * heads : (m + 1) * heads]
        vec[...] = vecs[slot(*place())]
        for h in range(heads):
            bias[h] = shear_bias(vec[h : h + 1, :], length)

    def documents(position, last):
        out = jnp.zeros(position.shape, jnp.int32)
        for k in range(docs_per_sequence):
            out = out + (position >= last[0:1, k : k + 1]).astype(jnp.int32)
        return out

    @step
    def segments():
        pair_docs.wait()
        column = lax.broadcasted_iota(jnp.int32, (length, 1), 0)
        line = lax.broadcasted_iota(jnp.int32, (1, length), 1)
        for s in range(2):
            last = jnp.where(b == s, ends[...], pair_ends[...])
            segc[s] = documents(column, last)
            segr[s] = documents(line, last)
        own = (x * 2 + c) * rows + lax.broadcasted_iota(jnp.int32, (rows, 1), 0)
        keep[...] = (documents(own, ends[...]) < docs_per_sequence).astype(F32)

    @step
    def norm():
        def body(i, _):
            m = i // (rows // 16)
            at = pl.multiple_of(lax.rem(i, rows // 16) * 16, 16)
            value = tok_all[m, pl.ds(at, 16), :].astype(F32)
            inv = lax.rsqrt(jnp.mean(value * value, axis=-1, keepdims=True) + eps)
            n1[pl.ds(pl.multiple_of(i * 16, 16), 16), :] = (value * inv * gain1[...]).astype(BF16)
            return 0

        lax.fori_loop(0, 8 * rows // 16, body, 0)
        n1_move.start()

    @step
    def project():
        load = pltpu.make_async_copy(fqkv, vqkv, moves.at[2])
        load.start()
        load.wait()

        def body(i, _):
            at = pl.ds(pl.multiple_of(i * 128, 128), 128)
            qkv[at, :] = flat_dot(n1[at, :], vqkv[...]).astype(BF16)
            return 0

        lax.fori_loop(0, 8 * rows // 128, body, 0)

    def attend(s, h):
        at = slice(s * length, (s + 1) * length)
        same = segc[s] == segr[s]
        q_cols, k_cols, v_cols = (slice(k * hc + h * hd, k * hc + (h + 1) * hd) for k in range(3))
        scores = jnp.where(same, dot_last(qkv[at, q_cols], qkv[at, k_cols]) + bias[h], far_below)
        top = jnp.max(scores, axis=1, keepdims=True)
        expo = jnp.exp(scores - top)
        total = jnp.sum(expo, axis=1, keepdims=True)
        probs = (expo * (1.0 / total)).astype(BF16)
        ctx[at, q_cols] = flat_dot(probs, qkv[at, v_cols]).astype(BF16)
        lse[at, h : h + 1] = top + jnp.log(total)

    for s in range(2):
        for h in range(heads):
            steps["h" + str(s * heads + h)] = functools.partial(attend, s, h)

    @step
    def load_o():
        load = pltpu.make_async_copy(fo, vo, moves.at[3])
        load.start()
        load.wait()

    @step
    def residual():
        def body(at):
            value = tok_all[slot(*place()), at, :].astype(F32) + keep[at, :] * acc[at, :]
            resid[at, :] = value
            inv = lax.rsqrt(jnp.mean(value * value, axis=-1, keepdims=True) + eps)
            n2[at, :] = (value * inv * gain2[...]).astype(BF16)

        in_rows(0, rows, body)

    def gate_up(at_b, at_x):
        def body(k, _):
            m = slot(at_b, at_x, k)
            at = pl.ds(pl.multiple_of(m * rows, rows), rows)
            value = flat_dot(n2_all[m], vgu[...])
            gu[at, :] = value
            hidden[at, :] = (gelu_tanh(value[:, :fc]) * value[:, fc:]).astype(BF16)
            return 0

        lax.fori_loop(0, 2, body, 0)

    for k, (at_b, at_x) in enumerate(((b, x), (b, 1 - x), (1 - b, x), (1 - b, 1 - x))):
        steps["gate_up" + str(k)] = functools.partial(gate_up, at_b, at_x)
    steps["wait_gu"] = gu_load.wait

    @step
    def save():
        start_all([last_moves[0], last_moves[2], last_moves[3]])

    @step
    def grad_f():
        last_moves[1].start()
        wide = 256
        for first in range(0, width, wide):
            left = cot_all[:, :, first : first + wide].reshape(8 * rows, wide)
            gf[first : first + wide, :] = dot_first(left, hidden[...]).astype(BF16)
        last_moves[4].start()

    for item in forward_order(types.SimpleNamespace(**steps)):
        item()
    for w in weights:
        weight_out(w)
    n1_move.wait()
    for move in last_moves:
        move.wait()


docs_per_sequence = 8
tok_share, cot_share, n2_share, attn_share = (1.0, 1.0, 0.375, 0.75)


def forward_order(n):
    return (
        n.bq, n.yq, n.bv, n.bk, n.yk, n.au, n.loadu, n.t0, n.av, n.loadk,
        n.yu, n.loadv, n.ak, n.c0, n.pairq, n.bo, n.pairv, n.loadq, n.t1, n.c1,
        n.onv, n.aq, n.pairk, n.loado, n.docs, n.yg, n.loadg, n.t2, n.yf, n.onpq,
        n.ao, n.loadf, n.onq, n.onpv, n.make_bias, n.keepv, n.onpk, n.t3, n.onk, n.yv,
        n.t4, n.bg, n.t5, n.keepk, n.ono, n.t6, n.keepu, n.pairo, n.keepq, n.segments,
        n.inq, n.bu, n.c2, n.t7, n.yo, n.ink, n.ag, n.keepo, n.norm, n.onpo,
        n.inv, n.project, n.c3, n.pairg, n.ino, n.h0, n.c4, n.h1, n.bf, n.keepg,
        n.h2, n.onu, n.h3, n.load_o, n.h4, n.h5, n.af, n.h6, n.ong, n.h7,
        n.s0, n.s1, n.c5, n.s4, n.s2, n.s3, n.s6, n.onpg, n.s9, n.keepf,
        n.s7, n.ing, n.s5, n.pairu, n.onf, n.s8, n.pairf, n.s10, n.residual, n.n0,
        n.n4, n.onpu, n.onpf, n.n1, n.inu, n.c6, n.load_gu, n.wait_gu, n.gate_up0, n.n2,
        n.n5, n.gate_up1, n.n6, n.gate_up2, n.c7, n.n3, n.inf, n.n7, n.gate_up3, n.save,
        n.grad_f,
    )


def forward(spans, tokens, cotangent, weights, ends, gain1, gain2, rel_table, onehot, hd, number):
    rows, width = tokens.shape
    length = 4 * rows
    total = weights[0].shape[0] * 4 * spans
    hc, fc = weights[0].shape[1] // 8, weights[4].shape[1] // 8
    heads = hc // hd
    dma, shape, vmem = pltpu.SemaphoreType.DMA, jax.ShapeDtypeStruct, pltpu.VMEM
    outs = pl.pallas_call(
        functools.partial(forward_kernel, spans, heads, hd),
        out_shape=[
            shape((8, rows, width), BF16),
            shape((8, rows, width), BF16),
            shape((8 * rows, width), BF16),
            shape((total, 3 * hc), BF16),
            shape((total, hc), BF16),
            shape((total, 2 * fc), BF16),
            shape((total, fc), BF16),
            shape((8 * rows, 2 * fc), F32),
            shape((8 * rows, fc), BF16),
            shape((total, fc), BF16),
            shape((8 * rows, 3 * hc), BF16),
            shape((8 * rows, hc), BF16),
            shape((8 * rows, heads), F32),
            shape((rows, width), F32),
            shape((2, length, 1), jnp.int32),
            shape((2, 1, length), jnp.int32),
            shape((rows, 1), F32),
            shape((heads, 2 * length), F32),
        ],
        in_specs=[any_space] * 9 + [in_vmem] * 5,
        out_specs=[any_space] * 10 + [in_vmem] * 8,
        scratch_shapes=[
            vmem((8, rows, width), BF16),
            vmem((8, rows, width), BF16),
            vmem((8, rows, width), BF16),
            vmem((8 * rows, width), BF16),
            vmem((total, 3 * hc), BF16),
            vmem((total, hc), BF16),
            vmem((total, 2 * fc), BF16),
            vmem((8 * rows, 2 * fc), F32),
            vmem((8 * rows, fc), BF16),
            vmem((total, fc), BF16),
            vmem((heads, length, length), F32),
            vmem((8, rows, width), BF16),
            vmem(ends.shape, jnp.int32),
            vmem((8, heads, 2 * length), F32),
            vmem((rows, width), F32),
            vmem((rows, width), BF16),
            vmem((4, weights[0].shape[0], hc), BF16),
            vmem((3, weights[4].shape[0], fc), BF16),
            vmem((rows, width), BF16),
            dma((7, 4 * spans - 1)),
            dma((7, 4 * spans - 1)),
            dma((7,)),
            dma((13,)),
        ]
        + [dma((9,)), dma((9,)), dma] * 3
        + scatter_scratch(rows, width),
        compiler_params=pltpu.CompilerParams(collective_id=number, has_side_effects=True, vmem_limit_bytes=62 * MIB),
    )(tokens, cotangent, *weights, ends, gain1[None, :], gain2[None, :], rel_table, onehot)
    return (outs[0].reshape(8 * rows, width), outs[1].reshape(8 * rows, width), *outs[2:])


def return_parts(spans, part, start, n, at, out, got_y, here, got_a, got_b, sends, recvs, local):
    a, y = lax.axis_index("a"), lax.axis_index("y")
    b, x, c = place()
    me, pair, x_me, x_pair = slot(b, x, c), slot(1 - b, x, c), slot(b, 1 - x, c), slot(1 - b, 1 - x, c)
    cols = pl.ds(start, n)
    count = got_b.shape[0]
    far = [lax.rem(a + k, spans) for k in range(1, spans)] + [a]
    held = [part.at[f, :, y, at, cols] if here is None else here.at[k] for k, f in enumerate(far)]

    def copy(src, dst, k, axis, to):
        return remote_to(src, dst, sends.at[k], recvs.at[k], axis, to)

    def place_in(member):
        return out.at[at, pl.ds(pl.multiple_of(member * n, 128), n)]

    to_y = [copy(part.at[f, :, 1 - y, at, cols], got_y.at[k], k, "y", 1 - y) for k, f in enumerate(far)]
    load = []
    if here is not None:
        load = [pltpu.make_async_copy(part.at[f, :, y, at, cols], here.at[k], local.at[k]) for k, f in enumerate(far)]
    over_a = [copy(held[k], got_a.at[k], spans + k, "a", f) for k, f in enumerate(far[:-1])]
    base = 2 * spans - 1
    last = held[-1]
    over_b = copy(last.at[1 - b], got_b, base, "b", 1 - b)
    x_own = copy(last.at[b], place_in(me), base + 1, "x", 1 - x)
    x_other = copy(got_b, place_in(pair), base + 2, "x", 1 - x)
    c_own = copy(last.at[b], place_in(me), base + 3, "c", 1 - c)
    c_other = copy(got_b, place_in(pair), base + 4, "c", 1 - c)
    c_x_own = copy(place_in(x_me), place_in(x_me), base + 5, "c", 1 - c)
    c_x_other = copy(place_in(x_pair), place_in(x_pair), base + 6, "c", 1 - c)
    keep_own = pltpu.make_async_copy(last.at[b], place_in(me), local.at[spans])
    keep_other = pltpu.make_async_copy(got_b, place_in(pair), local.at[spans + 1])

    def add(k, others):
        for half in range(2):

            def body(r, half=half):
                value = held[k][half, r, :].astype(F32)
                for other in others:
                    value = value + other[half, r, :].astype(F32)
                held[k][half, r, :] = value.astype(BF16)

            in_rows(0, count, body)

    def ready(k):
        to_y[k].wait_recv()
        for item in load[k : k + 1]:
            item.wait()

    def begin():
        start_all(to_y + load)

    def across():
        for k in range(spans - 1):
            ready(k)
            add(k, [got_y.at[k]])
            over_a[k].start()

    def finish():
        ready(spans - 1)
        for item in over_a:
            item.wait_recv()
        add(spans - 1, [got_y.at[spans - 1]] + [got_a.at[k] for k in range(spans - 1)])
        start_all([over_b, x_own, c_own, keep_own])

    def pass_on():
        over_b.wait_recv()
        start_all([x_other, c_other, keep_other])

    def share():
        x_own.wait_recv()
        c_x_own.start()
        x_other.wait_recv()
        c_x_other.start()

    def end():
        for item in (c_own, c_other, c_x_own, c_x_other):
            item.wait_recv()
        for item in (*to_y, *over_a, over_b, x_own, x_other, c_own, c_other, c_x_own, c_x_other):
            item.wait_send()
        keep_own.wait()
        keep_other.wait()

    return [begin, across, finish, pass_on, share, end]


def return_scratch(spans, count, n, copied):
    dma = pltpu.SemaphoreType.DMA
    one = pltpu.VMEM((spans, 2, count, n), BF16)
    return [
        one,
        *([one] if copied else []),
        pltpu.VMEM((max(spans - 1, 1), 2, count, n), BF16),
        pltpu.VMEM((count, n), BF16),
        dma((2 * spans + 6,)),
        dma((2 * spans + 6,)),
        dma((spans + 2,)),
    ]


def sum_parts(spans, bufs, gots, sends, recvs):
    a, y = lax.axis_index("a"), lax.axis_index("y")
    b, x, c = place()
    steps = []

    def hop(step, targets):
        copies = [
            remote_to(buf, got.at[step + k], sends.at[i, step + k], recvs.at[i, step + k], axis, other)
            for k, (axis, other) in enumerate(targets)
            for i, (buf, got) in enumerate(zip(bufs, gots))
        ]

        def begin():
            start_all(copies)

        def end():
            for copy in copies:
                copy.wait()
            for buf, got in zip(bufs, gots):
                buf[...] = functools.reduce(jnp.add, [buf[...]] + [got[step + k] for k in range(len(targets))])

        steps.extend([begin, end])

    for step, target in enumerate((("c", 1 - c), ("x", 1 - x), ("b", 1 - b), ("y", 1 - y))):
        hop(step, [target])
    if spans > 1:
        hop(4, [("a", lax.rem(a + k, spans)) for k in range(1, spans)])
    return steps


def gelu_both(v):
    inner = 0.7978845608028654 * (v + 0.044715 * (v * v * v))
    t = jnp.tanh(inner)
    slope = 0.7978845608028654 * (1.0 + 0.134145 * (v * v))
    return 0.5 * v * (1.0 + t), 0.5 * (1.0 + t) + 0.5 * v * (1.0 - t * t) * slope


def backward_kernel(
    spans, heads, hd, hidden, gf, n2, cot_all, gu, wgu, wf, wqkv, wo, n1, qkv_all, ctx_all, lse_all,
    resid, tokens, cotangent, keep, gain1, gain2, vec, segc, segr, onehot,
    dattn_all, o_f, o_g, o_u, o_o, o_q, o_k, o_v, out, grad_input, sums, table,
    sib, mid, diag, last, sib2, mid2, diag2, last2, acc, acc2, dattn, dresid, held, parts, ggu, gatt, diags,
    got_sums, got_table, moves, *scratch
):
    total, hc = wo.shape
    fc = gf.shape[4]
    rows, width = resid.shape
    count = gf.shape[3]
    length = segr.shape[2]
    scratch = list(scratch)

    def take(n):
        out = scratch[:n]
        del scratch[:n]
        return out

    cot_load = pltpu.make_async_copy(cot_all, held, moves.at[1])
    cot_load.start()
    meet_all(spans)
    dn2_source, dn1_source, out_source = (types.SimpleNamespace(parts=parts) for _ in range(3))
    dn2_sum = scatter_parts(dn2_share, dn2_source, acc, sib, mid, diag, last, *take(2))
    dn1_sum = scatter_parts(dn1_share, dn1_source, acc, sib, mid, diag, last, *take(2))
    out_sum = scatter_parts(out_share, out_source, acc2, sib2, mid2, diag2, last2, *take(2))
    dattn_in = gather_parts(dattn_share, dattn, dattn_all, *take(3))
    summed = sum_parts(spans, [sums, table], [got_sums, got_table], *take(2))
    pieces = []
    for part, result in ((gf, o_f), (ggu.at[0], o_g), (ggu.at[1], o_u)):
        for first in (0, count // 2):
            at = pl.ds(first, count // 2)
            if part is gf:
                pieces.append(return_parts(spans, part, 0, fc, at, result, *take(7)))
            else:
                got_y, got_a, got_b, *sems = take(6)
                pieces.append(return_parts(spans, part, 0, fc, at, result, got_y, None, got_a, got_b, *sems))
    for i, result in enumerate((o_o, o_q, o_k, o_v)):
        got_y, got_a, got_b, *sems = take(6)
        pieces.append(return_parts(spans, gatt.at[i], 0, hc, pl.ds(0, count), result, got_y, None, got_a, got_b, *sems))
    steps = {}
    for name, piece in zip(("f", "F", "g", "G", "u", "U", "o", "q", "k", "v"), pieces):
        for k, item in enumerate(piece):
            steps[name + str(k)] = item
    for name, parts_of in (("d", dn2_sum), ("e", dn1_sum), ("x", out_sum), ("n", dattn_in), ("s", summed)):
        for k, item in enumerate(parts_of):
            steps[name + "_" + str(k)] = item

    def step(function):
        steps[function.__name__] = function
        return function

    n2_load = pltpu.make_async_copy(n2, held, moves.at[11])
    n1_load = pltpu.make_async_copy(n1, held, moves.at[10])

    @step
    def setup():
        sums[...] = jnp.zeros_like(sums)
        table[...] = jnp.zeros_like(table)

    @step
    def second_norm():
        def body(at):
            value, dn2 = resid[at, :], acc[at, :]
            inv = lax.rsqrt(jnp.mean(value * value, axis=-1, keepdims=True) + eps)
            inner = dn2 * gain2[...]
            grad = (
                cotangent[at, :].astype(F32)
                + inv * inner
                - value * (inv * inv * inv * jnp.mean(inner * value, axis=-1, keepdims=True))
            )
            dresid[at, :] = grad
            sums[1:2, :] += jnp.sum(dn2 * value * inv, axis=0, keepdims=True)
            sums[2:3, :] += jnp.sum(value * value, axis=0, keepdims=True)
            dattn[at, :] = (keep[at, :] * grad).astype(BF16)

        in_rows(0, rows, body)

    wide = max(count, 256)

    def weight_grad(store, factor):
        for first in range(0, total, wide):
            value = dot_first(held[:, first : first + wide], factor).astype(BF16)
            for owner in range(first // count, (first + wide) // count):
                at = owner * count - first
                store[owner // 4, owner // 2 % 2, owner % 2] = value[at : at + count]

    @step
    def first_norm():
        def body(at):
            value, dn1 = tokens[at, :].astype(F32), acc[at, :]
            inv = lax.rsqrt(jnp.mean(value * value, axis=-1, keepdims=True) + eps)
            inner = dn1 * gain1[...]
            grad_input[at, :] = (
                dresid[at, :]
                + inv * inner
                - value * (inv * inv * inv * jnp.mean(inner * value, axis=-1, keepdims=True))
            )
            sums[0:1, :] += jnp.sum(dn1 * value * inv, axis=0, keepdims=True)

        in_rows(0, rows, body)

    @step
    def final():
        def body(at):
            value = resid[at, :] + acc2[at, :]
            out[at, :] = value.astype(BF16)
            sums[3:4, :] += jnp.sum(value * value, axis=0, keepdims=True)

        in_rows(0, rows, body)

    @step
    def tables():
        buckets = lax.dot_general(
            diags[...], onehot[...], (((1,), (1,)), ((), ())), precision=highest, preferred_element_type=F32
        )
        table[slot(*place()), 0:heads, 0 : buckets.shape[1]] = buckets

    def first_half(v_dgu, v_out):
        out_source.parts = v_out
        @step
        def dhidden():
            def inner(v_wf, v_gu):
                wf_load = pltpu.make_async_copy(wf, v_wf, moves.at[0])

                def fetch_gu(m):
                    at = pl.ds(pl.multiple_of(m * rows, rows), rows)
                    slot_of = lax.rem(m, 2)
                    return pltpu.make_async_copy(gu.at[at], v_gu.at[slot_of], moves.at[12 + slot_of])

                start_all([wf_load, fetch_gu(0)])
                wf_load.wait()
                cot_load.wait()

                def body(m, _):
                    at = pl.ds(pl.multiple_of(m * rows, rows), rows)

                    @pl.when(m < 7)
                    def _():
                        fetch_gu(m + 1).start()

                    grad = flat_dot(held[at, :], v_wf[...])
                    fetch_gu(m).wait()
                    both = v_gu[lax.rem(m, 2)]
                    activ, slope = gelu_both(both[:, :fc])
                    v_dgu[at, :fc] = (grad * both[:, fc:] * slope).astype(BF16)
                    v_dgu[at, fc:] = (grad * activ).astype(BF16)
                    return 0

                lax.fori_loop(0, 8, body, 0)
                n2_load.start()

            pl.run_scoped(inner, pltpu.VMEM(wf.shape, BF16), pltpu.VMEM((2, rows, 2 * fc), F32))

        def with_out(v_wf, v_hidden):
            loads = [pltpu.make_async_copy(wf, v_wf, moves.at[0]), pltpu.make_async_copy(hidden, v_hidden, moves.at[12])]

            def make(m):
                at = pl.ds(pl.multiple_of(m * rows, rows), rows)
                v_out[m] = dot_last(v_hidden[at, :], v_wf[...]).astype(BF16)

            out_source.make = make
            start_all(loads)
            for load in loads:
                load.wait()
            for item in backward_out(types.SimpleNamespace(**steps)):
                item()

        def with_dn2(v_wgu):
            load = pltpu.make_async_copy(wgu, v_wgu, moves.at[0])

            def make(m):
                at = pl.ds(pl.multiple_of(m * rows, rows), rows)
                parts[m] = dot_last(v_dgu[at, :], v_wgu[...]).astype(BF16)

            dn2_source.make = make
            load.start()
            load.wait()
            for item in backward_dn2(types.SimpleNamespace(**steps)):
                item()

        @step
        def grad_g():
            n2_load.wait()
            weight_grad(ggu.at[0], v_dgu[:, :fc])

        @step
        def grad_u():
            weight_grad(ggu.at[1], v_dgu[:, fc:])

        for item in backward_start(types.SimpleNamespace(**steps)):
            item()
        pl.run_scoped(with_dn2, pltpu.VMEM(wgu.shape, BF16))
        pl.run_scoped(with_out, pltpu.VMEM(wf.shape, BF16), pltpu.VMEM(hidden.shape, BF16))
        for item in backward_first(types.SimpleNamespace(**steps)):
            item()

    def second_half(v_qkv, qkv, ctx, lse, dctx, dqkv, shear, v_o):
        loads = [
            pltpu.make_async_copy(src, dst, moves.at[k])
            for src, dst, k in ((wo, v_o, 1), (qkv_all, qkv, 12), (ctx_all, ctx, 13), (lse_all, lse, 14))
        ]
        qkv_load = pltpu.make_async_copy(wqkv, v_qkv, moves.at[0])
        start_all([*loads, qkv_load])
        steps["in_qkv"] = qkv_load.wait

        @step
        def to_ctx():
            copies = [
                pltpu.make_async_copy(dattn_all.at[m], held.at[pl.ds(m * rows, rows)], moves.at[2 + m]) for m in range(8)
            ]
            start_all(copies)
            for copy in (*loads, *copies):
                copy.wait()

            def body(m, _):
                at = pl.ds(pl.multiple_of(m * rows, rows), rows)
                dctx[at, :] = flat_dot(held[at, :], v_o[...]).astype(BF16)
                return 0

            lax.fori_loop(0, 8, body, 0)

        @step
        def grad_o():
            weight_grad(gatt.at[0], ctx[...])
            n1_load.start()

        def attend_back(h):
            bias = shear_bias(vec[h : h + 1, :], length)
            q_cols, k_cols, v_cols = (slice(k * hc + h * hd, k * hc + (h + 1) * hd) for k in range(3))
            for s in range(2):
                at = slice(s * length, (s + 1) * length)
                same = segc[s] == segr[s]
                q, k, v, d = qkv[at, q_cols], qkv[at, k_cols], qkv[at, v_cols], dctx[at, q_cols]
                scores = jnp.where(same, dot_last(q, k) + bias, far_below)
                probs = jnp.exp(scores - lse[at, h : h + 1])
                dprobs = dot_last(d, v)
                dqkv[at, v_cols] = dot_first(probs.astype(BF16), d).astype(BF16)
                product = probs * dprobs
                dscores = product - probs * jnp.sum(product, axis=1, keepdims=True)
                if s == 0:
                    shear[...] = dscores
                else:
                    shear[...] += dscores
                dlogits = dscores.astype(BF16)
                dqkv[at, q_cols] = flat_dot(dlogits, k).astype(BF16)
                dqkv[at, k_cols] = dot_first(dlogits, q).astype(BF16)

            def shift(g, carry):
                group = shear[pl.ds(pl.multiple_of(g * 8, 8), 8), :]
                group = jnp.concatenate([group, jnp.zeros_like(group)], axis=1)
                return carry + pltpu.roll(group, 2 * length - g * 8, 1)

            shifted = lax.fori_loop(0, length // 8, shift, jnp.zeros((8, 2 * length), F32), unroll=8)
            line = shifted[0:1, :]
            for r in range(1, 8):
                line = line + pltpu.roll(shifted[r : r + 1, :], 2 * length - r, 1)
            diags[h : h + 1, :] = line

        for h in range(heads):
            steps["h" + str(h)] = functools.partial(attend_back, h)

        for i, name in enumerate(("q", "k", "v")):

            def grad_of(i=i):
                if i == 0:
                    n1_load.wait()
                weight_grad(gatt.at[1 + i], dqkv[:, i * hc : (i + 1) * hc])

            steps["grad_" + name] = grad_of

        def make(m):
            at = pl.ds(pl.multiple_of(m * rows, rows), rows)
            parts[m] = dot_last(dqkv[at, :], v_qkv[...]).astype(BF16)

        dn1_source.make = make

        for item in backward_second(types.SimpleNamespace(**steps)):
            item()

    pl.run_scoped(first_half, pltpu.VMEM((8 * rows, 2 * fc), BF16), pltpu.VMEM((8, rows, width), BF16))
    pl.run_scoped(
        second_half,
        pltpu.VMEM((total, 3 * hc), BF16),
        pltpu.VMEM((8 * rows, 3 * hc), BF16),
        pltpu.VMEM((8 * rows, hc), BF16),
        pltpu.VMEM((8 * rows, heads), F32),
        pltpu.VMEM((8 * rows, hc), BF16),
        pltpu.VMEM((8 * rows, 3 * hc), BF16),
        pltpu.VMEM((length, length), F32),
        pltpu.VMEM((total, hc), BF16),
    )
    for name in ("f", "F", "g", "G", "u", "U", "o", "q", "k", "v"):
        steps[name + "5"]()


dn2_share, dattn_share, dn1_share, out_share = (0.625, 0.75, 0.75, 0.75)


def backward_start(n):
    return (
        n.F0, n.dhidden, n.F1,
    )


def backward_dn2(n):
    return (
        n.d_0, n.d_4, n.f0, n.d_1, n.d_2, n.d_6, n.d_5, n.d_3,
    )


def backward_out(n):
    return (
        n.d_9, n.d_8, n.d_7, n.F2, n.grad_g, n.g0, n.f1, n.setup, n.G0, n.d_10,
        n.second_norm, n.n_0, n.grad_u, n.x_0, n.u0, n.x_1, n.x_2, n.x_4, n.n_1, n.x_3,
        n.x_6, n.g1, n.n_2, n.U0, n.x_5, n.x_8, n.x_7, n.f2, n.x_9, n.G1,
    )


def backward_first(n):
    return (
    )


def backward_second(n):
    return (
        n.F3, n.n_3, n.n_4, n.n_5, n.n_6, n.n_7, n.u1, n.to_ctx, n.h0, n.grad_o,
        n.h1, n.U1, n.f3, n.g2, n.h2, n.o0, n.G2, n.h3, n.u2, n.in_qkv,
        n.o1, n.e_0, n.e_1, n.e_4, n.e_2, n.grad_q, n.x_10, n.q0, n.final, n.e_3,
        n.e_6, n.u3, n.tables, n.grad_k, n.e_5, n.e_9, n.G3, n.e_8, n.k0, n.U2,
        n.g3, n.q1, n.k1, n.grad_v, n.v0, n.q2, n.e_7, n.e_10, n.first_norm, n.s_0,
        n.s_1, n.s_2, n.g4, n.o2, n.U3, n.v1, n.q3, n.s_3, n.f4, n.G4,
        n.F4, n.s_4, n.k2, n.o3, n.s_5, n.s_6, n.v2, n.U4, n.s_7, n.s_8,
        n.k3, n.o4, n.v3, n.u4, n.k4, n.q4, n.s_9, n.v4,
    )


def backward(
    spans, hidden, grad_f, n2, cot_all, gu, wgu, wf, wqkv, wo, n1, qkv, ctx, lse, resid, tokens, cotangent, keep, gain1, gain2, vec, segc, segr, onehot, hd, number
):
    rows, width = tokens.shape
    heads, length = vec.shape[0], segr.shape[2]
    total, hc = wo.shape
    fc = grad_f.shape[1]
    count = total // (4 * spans)
    dma, shape, vmem = pltpu.SemaphoreType.DMA, jax.ShapeDtypeStruct, pltpu.VMEM
    scratch = scatter_scratch(rows, width)[:4] + scatter_scratch(rows, width)[:4]
    scratch += [
        vmem((rows, width), F32),
        vmem((rows, width), F32),
        vmem((rows, width), BF16),
        vmem((rows, width), F32),
        vmem((8 * rows, width), BF16),
        vmem((8, rows, width), BF16),
        vmem((2, spans, 2, 2, count, fc), BF16),
        vmem((4, spans, 2, 2, count, hc), BF16),
        vmem((heads, 2 * length), F32),
        vmem((3 + spans, 8, width), F32),
        vmem((3 + spans, 8, 8, 128), F32),
        dma((15,)),
    ]
    scratch += [dma((10,))] * 6
    scratch += [dma((9,)), dma((9,)), dma, dma((2, 3 + spans)), dma((2, 3 + spans))]
    for i in range(6):
        scratch += return_scratch(spans, count // 2, fc, i < 2)
    for _ in range(4):
        scratch += return_scratch(spans, count, hc, False)
    outs = pl.pallas_call(
        functools.partial(backward_kernel, spans, heads, hd),
        out_shape=[shape((8, rows, width), BF16)]
        + [shape((count, 8 * fc), BF16)] * 3
        + [shape((count, 8 * hc), BF16)] * 4
        + [shape((rows, width), BF16), shape((rows, width), F32), shape((8, width), F32), shape((8, 8, 128), F32)],
        in_specs=[any_space] * 13 + [in_vmem] * 10,
        out_specs=[any_space] * 8 + [in_vmem] * 4,
        scratch_shapes=scratch,
        compiler_params=pltpu.CompilerParams(collective_id=number, has_side_effects=True, vmem_limit_bytes=62 * MIB),
    )(
        hidden,
        grad_f.reshape(spans, 2, 2, count, fc),
        n2,
        cot_all,
        gu,
        wgu,
        wf,
        wqkv,
        wo,
        n1,
        qkv,
        ctx,
        lse,
        resid,
        tokens,
        cotangent,
        keep,
        gain1[None, :],
        gain2[None, :],
        vec,
        segc,
        segr,
        onehot,
    )
    return outs[1:]


def widen_kernel(count, *refs):
    for narrow, wide in zip(refs[:count], refs[count:]):
        wide[...] = narrow[...].astype(F32)


def widen(arrays):
    rows = arrays[0].shape[0]
    step = max(rows // 8, 16)
    specs = [pl.BlockSpec((step, array.shape[1]), lambda i: (i, 0)) for array in arrays]
    return pl.pallas_call(
        functools.partial(widen_kernel, len(arrays)),
        grid=(rows // step,),
        in_specs=specs,
        out_specs=specs,
        out_shape=[jax.ShapeDtypeStruct(array.shape, F32) for array in arrays],
        compiler_params=pltpu.CompilerParams(vmem_limit_bytes=62 * MIB),
    )(*arrays)


def per_device(
    tokens,
    w_query,
    w_key,
    w_value,
    w_attn_out,
    w_gate,
    w_up,
    w_ff_out,
    gain_attn,
    gain_ffn,
    rel_table,
    doc_lengths,
    cotangent,
):
    rows, width = tokens.shape
    n_buckets, heads_all = rel_table.shape
    heads = heads_all // 8
    hc = w_query.shape[1] // 8
    fc = w_gate.shape[1] // 8
    hd = hc // heads
    length = 4 * rows

    ends = jnp.cumsum(doc_lengths, axis=1).astype(jnp.int32)
    offset = np.arange(-length, length)
    distance = np.abs(offset)
    far = 8 + np.sum(distance[:, None] >= np.array(thresholds), axis=1)
    bucket = np.where(offset > 0, 16, 0) + np.where(distance < 8, distance, far)
    onehot = (np.arange(n_buckets)[:, None] == bucket[None, :]).astype(np.float32)
    order = np.roll(onehot, length, axis=1)

    spans = lax.axis_size("a")
    weights = (w_query, w_key, w_value, w_attn_out, w_gate, w_up, w_ff_out)
    (cot_all, n2, n1, wqkv, wo, wgu, wf, gate_up, hidden, grad_f, qkv, ctx, lse, resid, segc, segr, keep, vec) = forward(
        spans, tokens, cotangent, weights, ends, gain_attn, gain_ffn, rel_table, jnp.asarray(onehot), hd, 0
    )
    grad_f, grad_g, grad_u, grad_o, grad_q, grad_k, grad_v, out, grad_input, sums, table_sums = backward(
        spans, hidden, grad_f, n2, cot_all, gate_up, wgu, wf, wqkv, wo, n1, qkv, ctx, lse, resid, tokens, cotangent, keep, gain_attn, gain_ffn,
        vec, segc, segr, jnp.asarray(order), hd, 1
    )
    dtable = table_sums[:, :heads, :n_buckets].reshape(heads_all, n_buckets).T
    entries = rows * width * 16 * spans
    norms = jnp.sqrt(jnp.sum(sums[2:4], axis=1) / entries)
    return (
        out,
        grad_input,
        *widen([grad_q, grad_k, grad_v, grad_o, grad_g, grad_u, grad_f]),
        sums[0],
        sums[1],
        dtable,
        norms,
    )


def solution(mesh):
    owners, copies = mesh.shape["fsdp"], mesh.shape["rep"]
    finer = Mesh(mesh.devices.reshape(owners // 4, 2, 2, copies // 2, 2), ("a", "b", "y", "x", "c"))
    owner = ("a", "b", "y")
    piece = P(owner + ("x", "c"), None)
    shard = P(owner, None)
    return jax.shard_map(
        per_device,
        mesh=finer,
        in_specs=(piece,) + (shard,) * 7 + (P(), P(), P(), shard, piece),
        out_specs=(piece, piece) + (shard,) * 7 + (P(), P(), P(), P()),
        check_vma=False,
    )
```

```python
import functools
import types

import jax
import jax.numpy as jnp
import numpy as np
from jax import lax
from jax.experimental import pallas as pl
from jax.experimental.pallas import tpu as pltpu
from jax.sharding import Mesh
from jax.sharding import PartitionSpec as P

eps = 1e-06
thresholds = (12, 16, 23, 32, 46, 64, 91)
highest = lax.Precision.HIGHEST
F32 = jnp.float32
BF16 = jnp.bfloat16
far_below = -1e30
MESH = pl.DeviceIdType.MESH
swap = ((0, 1), (1, 0))
MIB = 1 << 20


def flat_dot(left, right):
    return jnp.dot(left, right, preferred_element_type=F32)


def dot_last(left, right):
    return lax.dot_general(left, right, (((1,), (1,)), ((), ())), preferred_element_type=F32)


def dot_first(left, right):
    return lax.dot_general(left, right, (((0,), (0,)), ((), ())), preferred_element_type=F32)


def shear_bias(row, length):
    wide = jnp.broadcast_to(row, (length, 2 * length))
    return pltpu.roll(wide, length, 1, stride=1, stride_axis=0)[:, :length]


def place():
    return lax.axis_index("b"), lax.axis_index("x"), lax.axis_index("c")


def slot(b, x, c):
    return b * 4 + x * 2 + c


def meet():
    b, x, c = place()
    barrier = pltpu.get_barrier_semaphore()
    for axis, other in (("b", 1 - b), ("x", 1 - x), ("c", 1 - c)):
        pl.semaphore_signal(barrier, inc=1, device_id={axis: other}, device_id_type=MESH)
    pl.semaphore_wait(barrier, 3)


def start_all(copies):
    for copy in copies:
        copy.start()


def remote(src, dst, sends, recvs, n, axis):
    return pltpu.make_async_remote_copy(
        src_ref=src,
        dst_ref=dst,
        send_sem=sends.at[n],
        recv_sem=recvs.at[n],
        device_id={axis: 1 - lax.axis_index(axis)},
        device_id_type=MESH,
    )


def gather_parts(share, src, out, sends, recvs, local):
    b, x, c = place()
    rows = src.shape[0]
    by_x = int(rows * share) // 16 * 16
    first, rest = pl.ds(0, by_x), pl.ds(by_x, rows - by_x)
    own, at_x, at_b, at_d = slot(b, x, c), slot(b, 1 - x, c), slot(1 - b, x, c), slot(1 - b, 1 - x, c)
    over_x = remote(src, out.at[own], sends, recvs, 0, "x")
    over_b = remote(src, out.at[own], sends, recvs, 1, "b")
    on_x = remote(out.at[at_b, first], out.at[at_b, first], sends, recvs, 2, "x")
    over_c = remote(src, out.at[own], sends, recvs, 3, "c")
    x_on_c = remote(out.at[at_x], out.at[at_x], sends, recvs, 4, "c")
    b_on_c = remote(out.at[at_b], out.at[at_b], sends, recvs, 5, "c")
    d_on_c = [remote(out.at[at_d, first], out.at[at_d, first], sends, recvs, 6, "c")]
    on_b = []
    if by_x < rows:
        on_b = [remote(out.at[at_x, rest], out.at[at_x, rest], sends, recvs, 7, "b")]
        d_on_c.append(remote(out.at[at_d, rest], out.at[at_d, rest], sends, recvs, 8, "c"))
    keep = pltpu.make_async_copy(src, out.at[own], local)

    def begin():
        for copy in (over_b, over_x, over_c, keep):
            copy.start()

    def from_x():
        over_x.wait_recv()
        for copy in (*on_b, x_on_c):
            copy.start()

    def from_b():
        over_b.wait_recv()
        on_x.start()
        b_on_c.start()

    def from_both():
        for came, on in zip([on_x, *on_b], d_on_c):
            came.wait_recv()
            on.start()

    def end():
        for copy in d_on_c:
            copy.wait_recv()
        for copy in (over_x, over_b, on_x, *on_b, over_c, x_on_c, b_on_c, *d_on_c):
            copy.wait_send()

    def from_c():
        over_c.wait_recv()
        keep.wait()

    return [begin, from_x, from_b, from_both, from_c, x_on_c.wait_recv, b_on_c.wait_recv, end]


def in_rows(first, count, body, chunk=16):
    def step(i, _):
        body(pl.ds(pl.multiple_of(first + i * chunk, chunk), chunk))
        return 0

    lax.fori_loop(0, count // chunk, step, 0)


def scatter_parts(share, source, acc, sib, out, diag, last, sends, recvs):
    b, x, c = place()
    rows = sib.shape[1]
    by_x = int(rows * share) // 16 * 16
    seats = [(b, x), (b, 1 - x), (1 - b, x), (1 - b, 1 - x)]
    here, there = [slot(*seat, c) for seat in seats], [slot(*seat, 1 - c) for seat in seats]
    to_core = [remote(sib.at[q], sib.at[q], sends, recvs, q, "c") for q in range(4)]

    def over(n, to, first, count, k, axis):
        at = pl.ds(first, count)
        return remote(out.at[n, at], to.at[at], sends, recvs, k, axis)

    rest = rows - by_x
    d_x = over(2, diag, 0, by_x, 4, "x")
    x_first, b_last = over(0, last.at[0], 0, by_x, 5, "x"), over(1, last.at[1], 0, by_x, 6, "b")
    d_b, x_last, b_first = [], [], []
    if rest:
        d_b = [over(2, diag, by_x, rest, 7, "b")]
        x_last, b_first = [over(0, last.at[0], by_x, rest, 8, "x")], [over(1, last.at[1], by_x, rest, 9, "b")]

    def both(q, at):
        return source.parts[here[q], at, :].astype(F32) + sib[q, at, :].astype(F32)

    def put(n, q, first, count, more=False):
        def body(at):
            value = both(q, at)
            if more:
                value = value + diag[at, :].astype(F32)
            out[n, at, :] = value.astype(BF16)

        if count:
            in_rows(first, count, body)

    def begin(q):
        source.make(there[q])
        remote(source.parts.at[there[q]], sib.at[q], sends, recvs, q, "c").start()
        source.make(here[q])

    def to_diagonal():
        to_core[3].wait_recv()
        put(2, 3, 0, by_x)
        d_x.start()
        put(2, 3, by_x, rest)
        start_all(d_b)

    def to_x():
        to_core[1].wait_recv()
        put(0, 1, 0, by_x)
        x_first.start()

    def to_b():
        to_core[2].wait_recv()
        put(1, 2, by_x, rest)
        start_all(b_first)

    def keep():
        to_core[0].wait_recv()

        def own(at):
            acc[at, :] = both(0, at)

        in_rows(0, rows, own)

    def on_x():
        for copy in d_b:
            copy.wait_recv()
        put(0, 1, by_x, rest, True)
        start_all(x_last)

    def on_b():
        d_x.wait_recv()
        put(1, 2, 0, by_x, True)
        b_last.start()
        for copy in to_core:
            copy.wait_send()

    def end():
        for copy in (x_first, *b_first, *x_last, b_last):
            copy.wait_recv()
        for copy in (d_x, *d_b, x_first, *b_first, *x_last, b_last):
            copy.wait_send()

        def finish(at):
            acc[at, :] += last[0, at, :].astype(F32) + last[1, at, :].astype(F32)

        in_rows(0, rows, finish)

    makes = [functools.partial(begin, q) for q in (3, 1, 2, 0)]
    return [*makes, to_diagonal, to_x, to_b, keep, on_x, on_b, end]


def scatter_scratch(rows, width):
    return [
        pltpu.VMEM((4, rows, width), BF16),
        pltpu.VMEM((3, rows, width), BF16),
        pltpu.VMEM((rows, width), BF16),
        pltpu.VMEM((2, rows, width), BF16),
        pltpu.SemaphoreType.DMA((10,)),
        pltpu.SemaphoreType.DMA((10,)),
    ]


any_space = pl.BlockSpec(memory_space=pl.ANY)
in_vmem = pl.BlockSpec(memory_space=pltpu.VMEM)


def remote_to(src, dst, send, recv, axis, to):
    return pltpu.make_async_remote_copy(
        src_ref=src, dst_ref=dst, send_sem=send, recv_sem=recv, device_id={axis: to}, device_id_type=MESH
    )


def meet_all(spans):
    a, y = lax.axis_index("a"), lax.axis_index("y")
    b, x, c = place()
    barrier = pltpu.get_barrier_semaphore()
    others = [("b", 1 - b), ("x", 1 - x), ("c", 1 - c), ("y", 1 - y)] + [("a", lax.rem(a + k, spans)) for k in range(1, spans)]
    for axis, other in others:
        pl.semaphore_signal(barrier, inc=1, device_id={axis: other}, device_id_type=MESH)
    pl.semaphore_wait(barrier, len(others))


def fetch_parts(spans, shards, fulls, stages, sends, recvs, local):
    a, y = lax.axis_index("a"), lax.axis_index("y")
    b, x, c = place()
    me, pair = slot(b, x, c), slot(1 - b, x, c)
    count = shards[0].shape[0]

    def rows(at_a, at_b, at_y):
        return pl.ds(pl.multiple_of((at_a * 4 + at_b * 2 + at_y) * count, count), count)

    weights = []
    for i, (shard, (full, start)) in enumerate(zip(shards, fulls)):
        n = shard.shape[1] // 8
        cols = pl.ds(start, n)
        mine = shard.at[:, pl.ds(pl.multiple_of(me * n, 128), n)]
        theirs = shard.at[:, pl.ds(pl.multiple_of(pair * n, 128), n)]
        own, other = rows(a, b, y), rows(a, 1 - b, y)

        def block(at, full=full, cols=cols):
            return full.at[at, cols]

        def copy(src, dst, k, axis, to, i=i):
            return remote_to(src, dst, sends.at[i, k], recvs.at[i, k], axis, to)

        copies = {
            "load": pltpu.make_async_copy(mine, stages[i], local.at[i]),
            "keep": pltpu.make_async_copy(stages[i], block(own), local.at[i]),
            "b": copy(theirs, block(own), 0, "b", 1 - b),
            "y": copy(mine, block(own), 1, "y", 1 - y),
            "y_pair": copy(block(other), block(other), 2, "y", 1 - y),
            "a": [],
            "a_pair": [],
            "on": [],
            "on_pair": [],
        }
        for k in range(1, spans):
            to, source = lax.rem(a + k, spans), lax.rem(a + spans - k, spans)
            copies["a"].append(copy(mine, block(own), 4 * k - 1, "a", to))
            copies["a_pair"].append(copy(block(other), block(other), 4 * k, "a", to))
            far, far_pair = block(rows(source, b, y)), block(rows(source, 1 - b, y))
            copies["on"].append(copy(far, far, 4 * k + 1, "y", 1 - y))
            copies["on_pair"].append(copy(far_pair, far_pair, 4 * k + 2, "y", 1 - y))
        weights.append(copies)
    return weights


def pair_in(copies):
    copies["b"].wait_recv()
    start_all([*copies["a_pair"], copies["y_pair"]])


def hand_on(copies, came, on):
    for got, copy in zip(copies[came], copies[on]):
        got.wait_recv()
        copy.start()


def own_in(copies):
    copies["load"].wait()
    copies["keep"].start()


def weight_in(copies):
    copies["keep"].wait()
    for copy in (copies["y"], copies["y_pair"], *copies["on"], *copies["on_pair"]):
        copy.wait_recv()


def weight_out(copies):
    for copy in (copies["b"], copies["y"], copies["y_pair"]):
        copy.wait_send()
    for kind in ("a", "a_pair", "on", "on_pair"):
        for copy in copies[kind]:
            copy.wait_send()


def forward_kernel(
    spans, heads, hd, tokens, cotangent, wq, wk, wv, wo, wg, wu, wf, ends, gain1, gain2, rel_table, onehot,
    cot_out, n2_out, n1_out, fqkv, fo, fgu, ff, gu_out, hidden_out, gf_out, qkv, ctx, lse, resid, segc, segr, keep, vec,
    tok_all, cot_all, n2_all, n1, vqkv, vo, vgu, gu, hidden, gf, bias, parts, pair_ends, vecs, acc, n2, mine_small, mine_large, cot_own, sends, recvs, local, moves, *scratch
):
    hc, fc = wq.shape[1] // 8, wg.shape[1] // 8
    rows, width = tok_all.shape[1:]
    length = segr.shape[2]
    b, x, c = place()
    meet_all(spans)
    fulls = [(fqkv, 0), (fqkv, hc), (fqkv, 2 * hc), (fo, 0), (fgu, 0), (fgu, fc), (ff, 0)]
    stages = [mine_small.at[i] for i in range(4)] + [mine_large.at[i] for i in range(3)]
    weights = fetch_parts(spans, [wq, wk, wv, wo, wg, wu, wf], fulls, stages, sends, recvs, local)
    tok = gather_parts(tok_share, tokens, tok_all, *scratch[0:3])
    cot = gather_parts(cot_share, cot_own, cot_all, *scratch[3:6])
    n2s = gather_parts(n2_share, n2, n2_all, *scratch[6:9])

    def make_part(m):
        at = pl.ds(pl.multiple_of(m * rows, rows), rows)
        parts[m] = dot_last(ctx[at, :], vo[...]).astype(BF16)

    summed = scatter_parts(attn_share, types.SimpleNamespace(make=make_part, parts=parts), acc, *scratch[9:])
    cot_load = pltpu.make_async_copy(cotangent, cot_own, moves.at[4])
    cot_load.start()
    start_cot = cot[0]

    def cot_begin():
        cot_load.wait()
        start_cot()

    cot[0] = cot_begin
    pair_docs = remote_to(ends, pair_ends, moves.at[5], moves.at[6], "b", 1 - b)
    gu_load = pltpu.make_async_copy(fgu, vgu, moves.at[0])
    last_moves = [
        pltpu.make_async_copy(n2_all, n2_out, moves.at[7]),
        pltpu.make_async_copy(cot_all, cot_out, moves.at[8]),
        pltpu.make_async_copy(gu, gu_out, moves.at[9]),
        pltpu.make_async_copy(hidden, hidden_out, moves.at[10]),
        pltpu.make_async_copy(gf, gf_out, moves.at[11]),
    ]
    n1_move = pltpu.make_async_copy(n1, n1_out, moves.at[1])
    names = ("q", "k", "v", "o", "g", "u", "f")
    steps = {}
    for name, w in zip(names, weights):
        steps["b" + name] = w["b"].start
        steps["y" + name] = w["y"].start
        steps["load" + name] = w["load"].start
        steps["keep" + name] = functools.partial(own_in, w)
        steps["a" + name] = functools.partial(start_all, w["a"])
        steps["pair" + name] = functools.partial(pair_in, w)
        steps["on" + name] = functools.partial(hand_on, w, "a", "on")
        steps["onp" + name] = functools.partial(hand_on, w, "a_pair", "on_pair")
        steps["in" + name] = functools.partial(weight_in, w)
    for name, parts_of in (("t", tok), ("c", cot), ("n", n2s), ("s", summed)):
        for k, step in enumerate(parts_of):
            steps[name + str(k)] = step

    def step(function):
        steps[function.__name__] = function
        return function

    steps["docs"] = pair_docs.start
    steps["load_gu"] = gu_load.start

    @step
    def make_bias():
        every = lax.dot_general(
            rel_table[...], onehot[...], (((0,), (0,)), ((), ())), precision=highest, preferred_element_type=F32
        )
        for m in range(8):
            vecs[m] = every[m * heads : (m + 1) * heads]
        vec[...] = vecs[slot(*place())]
        for h in range(heads):
            bias[h] = shear_bias(vec[h : h + 1, :], length)

    def documents(position, last):
        out = jnp.zeros(position.shape, jnp.int32)
        for k in range(docs_per_sequence):
            out = out + (position >= last[0:1, k : k + 1]).astype(jnp.int32)
        return out

    @step
    def segments():
        pair_docs.wait()
        column = lax.broadcasted_iota(jnp.int32, (length, 1), 0)
        line = lax.broadcasted_iota(jnp.int32, (1, length), 1)
        for s in range(2):
            last = jnp.where(b == s, ends[...], pair_ends[...])
            segc[s] = documents(column, last)
            segr[s] = documents(line, last)
        own = (x * 2 + c) * rows + lax.broadcasted_iota(jnp.int32, (rows, 1), 0)
        keep[...] = (documents(own, ends[...]) < docs_per_sequence).astype(F32)

    @step
    def norm():
        def body(i, _):
            m = i // (rows // 16)
            at = pl.multiple_of(lax.rem(i, rows // 16) * 16, 16)
            value = tok_all[m, pl.ds(at, 16), :].astype(F32)
            inv = lax.rsqrt(jnp.mean(value * value, axis=-1, keepdims=True) + eps)
            n1[pl.ds(pl.multiple_of(i * 16, 16), 16), :] = (value * inv * gain1[...]).astype(BF16)
            return 0

        lax.fori_loop(0, 8 * rows // 16, body, 0)
        n1_move.start()

    @step
    def project():
        load = pltpu.make_async_copy(fqkv, vqkv, moves.at[2])
        load.start()
        load.wait()

        def body(i, _):
            at = pl.ds(pl.multiple_of(i * 128, 128), 128)
            qkv[at, :] = flat_dot(n1[at, :], vqkv[...]).astype(BF16)
            return 0

        lax.fori_loop(0, 8 * rows // 128, body, 0)

    def attend(s, h):
        at = slice(s * length, (s + 1) * length)
        same = segc[s] == segr[s]
        q_cols, k_cols, v_cols = (slice(k * hc + h * hd, k * hc + (h + 1) * hd) for k in range(3))
        scores = jnp.where(same, dot_last(qkv[at, q_cols], qkv[at, k_cols]) + bias[h], far_below)
        top = jnp.max(scores, axis=1, keepdims=True)
        expo = jnp.exp(scores - top)
        total = jnp.sum(expo, axis=1, keepdims=True)
        probs = (expo * (1.0 / total)).astype(BF16)
        ctx[at, q_cols] = flat_dot(probs, qkv[at, v_cols]).astype(BF16)
        lse[at, h : h + 1] = top + jnp.log(total)

    for s in range(2):
        for h in range(heads):
            steps["h" + str(s * heads + h)] = functools.partial(attend, s, h)

    @step
    def load_o():
        load = pltpu.make_async_copy(fo, vo, moves.at[3])
        load.start()
        load.wait()

    @step
    def residual():
        def body(at):
            value = tok_all[slot(*place()), at, :].astype(F32) + keep[at, :] * acc[at, :]
            resid[at, :] = value
            inv = lax.rsqrt(jnp.mean(value * value, axis=-1, keepdims=True) + eps)
            n2[at, :] = (value * inv * gain2[...]).astype(BF16)

        in_rows(0, rows, body)

    def gate_up(at_b, at_x):
        def body(k, _):
            m = slot(at_b, at_x, k)
            at = pl.ds(pl.multiple_of(m * rows, rows), rows)
            value = flat_dot(n2_all[m], vgu[...])
            activ, slope = gelu_both(value[:, :fc])
            up = value[:, fc:]
            gu[at, :fc] = up * slope
            gu[at, fc:] = activ
            hidden[at, :] = (activ * up).astype(BF16)
            return 0

        lax.fori_loop(0, 2, body, 0)

    for k, (at_b, at_x) in enumerate(((b, x), (b, 1 - x), (1 - b, x), (1 - b, 1 - x))):
        steps["gate_up" + str(k)] = functools.partial(gate_up, at_b, at_x)
    steps["wait_gu"] = gu_load.wait

    @step
    def save():
        start_all([last_moves[0], last_moves[2], last_moves[3]])

    @step
    def grad_f():
        last_moves[1].start()
        wide = 256
        for first in range(0, width, wide):
            left = cot_all[:, :, first : first + wide].reshape(8 * rows, wide)
            gf[first : first + wide, :] = dot_first(left, hidden[...]).astype(BF16)
        last_moves[4].start()

    for item in forward_order(types.SimpleNamespace(**steps)):
        item()
    for w in weights:
        weight_out(w)
    n1_move.wait()
    for move in last_moves:
        move.wait()


docs_per_sequence = 8
tok_share, cot_share, n2_share, attn_share = (1.0, 1.0, 0.375, 1.0)


def forward_order(n):
    return (
        n.bk, n.loadf, n.bq, n.pairk, n.docs, n.t0, n.pairq, n.loadg, n.bv, n.bo,
        n.t1, n.onpk, n.ak, n.yk, n.loado, n.aq, n.onpq, n.av, n.t2, n.bu,
        n.ao, n.pairv, n.onk, n.pairo, n.loadv, n.loadk, n.loadu, n.loadq, n.t3, n.yv,
        n.bg, n.t4, n.yo, n.onq, n.onv, n.ag, n.t5, n.make_bias, n.c0, n.au,
        n.segments, n.t6, n.keepk, n.keepo, n.ink, n.onpv, n.yq, n.keepf, n.t7, n.keepv,
        n.yg, n.keepu, n.ono, n.inv, n.onpo, n.keepq, n.pairu, n.norm, n.keepg, n.yu,
        n.inq, n.project, n.h0, n.ino, n.h1, n.h2, n.h3, n.h4, n.h5, n.h6,
        n.h7, n.load_o, n.s0, n.ong, n.pairg, n.s1, n.bf, n.s2, n.af, n.c1,
        n.s4, n.onu, n.onpu, n.c2, n.s5, n.s6, n.s3, n.s9, n.s7, n.pairf,
        n.s8, n.onpg, n.c3, n.onf, n.s10, n.residual, n.n0, n.ing, n.inu, n.load_gu,
        n.n4, n.wait_gu, n.c4, n.yf, n.gate_up0, n.onpf, n.n1, n.n2, n.n5, n.c5,
        n.gate_up1, n.n6, n.gate_up2, n.inf, n.c6, n.c7, n.n3, n.n7, n.gate_up3, n.save,
        n.grad_f,
    )


def forward(spans, tokens, cotangent, weights, ends, gain1, gain2, rel_table, onehot, hd, number):
    rows, width = tokens.shape
    length = 4 * rows
    total = weights[0].shape[0] * 4 * spans
    hc, fc = weights[0].shape[1] // 8, weights[4].shape[1] // 8
    heads = hc // hd
    dma, shape, vmem = pltpu.SemaphoreType.DMA, jax.ShapeDtypeStruct, pltpu.VMEM
    outs = pl.pallas_call(
        functools.partial(forward_kernel, spans, heads, hd),
        out_shape=[
            shape((8, rows, width), BF16),
            shape((8, rows, width), BF16),
            shape((8 * rows, width), BF16),
            shape((total, 3 * hc), BF16),
            shape((total, hc), BF16),
            shape((total, 2 * fc), BF16),
            shape((total, fc), BF16),
            shape((8 * rows, 2 * fc), F32),
            shape((8 * rows, fc), BF16),
            shape((total, fc), BF16),
            shape((8 * rows, 3 * hc), BF16),
            shape((8 * rows, hc), BF16),
            shape((8 * rows, heads), F32),
            shape((rows, width), F32),
            shape((2, length, 1), jnp.int32),
            shape((2, 1, length), jnp.int32),
            shape((rows, 1), F32),
            shape((heads, 2 * length), F32),
        ],
        in_specs=[any_space] * 9 + [in_vmem] * 5,
        out_specs=[any_space] * 10 + [in_vmem] * 8,
        scratch_shapes=[
            vmem((8, rows, width), BF16),
            vmem((8, rows, width), BF16),
            vmem((8, rows, width), BF16),
            vmem((8 * rows, width), BF16),
            vmem((total, 3 * hc), BF16),
            vmem((total, hc), BF16),
            vmem((total, 2 * fc), BF16),
            vmem((8 * rows, 2 * fc), F32),
            vmem((8 * rows, fc), BF16),
            vmem((total, fc), BF16),
            vmem((heads, length, length), F32),
            vmem((8, rows, width), BF16),
            vmem(ends.shape, jnp.int32),
            vmem((8, heads, 2 * length), F32),
            vmem((rows, width), F32),
            vmem((rows, width), BF16),
            vmem((4, weights[0].shape[0], hc), BF16),
            vmem((3, weights[4].shape[0], fc), BF16),
            vmem((rows, width), BF16),
            dma((7, 4 * spans - 1)),
            dma((7, 4 * spans - 1)),
            dma((7,)),
            dma((13,)),
        ]
        + [dma((9,)), dma((9,)), dma] * 3
        + scatter_scratch(rows, width),
        compiler_params=pltpu.CompilerParams(collective_id=number, has_side_effects=True, vmem_limit_bytes=62 * MIB),
    )(tokens, cotangent, *weights, ends, gain1[None, :], gain2[None, :], rel_table, onehot)
    return (outs[0].reshape(8 * rows, width), outs[1].reshape(8 * rows, width), *outs[2:])


def return_parts(spans, part, start, n, at, out, got_y, here, got_a, got_b, sends, recvs, local):
    a, y = lax.axis_index("a"), lax.axis_index("y")
    b, x, c = place()
    me, pair, x_me, x_pair = slot(b, x, c), slot(1 - b, x, c), slot(b, 1 - x, c), slot(1 - b, 1 - x, c)
    cols = pl.ds(start, n)
    count = got_b.shape[0]
    far = [lax.rem(a + k, spans) for k in range(1, spans)] + [a]
    held = [part.at[f, :, y, at, cols] if here is None else here.at[k] for k, f in enumerate(far)]

    def copy(src, dst, k, axis, to):
        return remote_to(src, dst, sends.at[k], recvs.at[k], axis, to)

    def place_in(member):
        return out.at[at, pl.ds(pl.multiple_of(member * n, 128), n)]

    to_y = [copy(part.at[f, :, 1 - y, at, cols], got_y.at[k], k, "y", 1 - y) for k, f in enumerate(far)]
    load = []
    if here is not None:
        load = [pltpu.make_async_copy(part.at[f, :, y, at, cols], here.at[k], local.at[k]) for k, f in enumerate(far)]
    over_a = [copy(held[k], got_a.at[k], spans + k, "a", f) for k, f in enumerate(far[:-1])]
    base = 2 * spans - 1
    last = held[-1]
    over_b = copy(last.at[1 - b], got_b, base, "b", 1 - b)
    x_own = copy(last.at[b], place_in(me), base + 1, "x", 1 - x)
    x_other = copy(got_b, place_in(pair), base + 2, "x", 1 - x)
    c_own = copy(last.at[b], place_in(me), base + 3, "c", 1 - c)
    c_other = copy(got_b, place_in(pair), base + 4, "c", 1 - c)
    c_x_own = copy(place_in(x_me), place_in(x_me), base + 5, "c", 1 - c)
    c_x_other = copy(place_in(x_pair), place_in(x_pair), base + 6, "c", 1 - c)
    keep_own = pltpu.make_async_copy(last.at[b], place_in(me), local.at[spans])
    keep_other = pltpu.make_async_copy(got_b, place_in(pair), local.at[spans + 1])

    def add(k, others):
        for half in range(2):

            def body(r, half=half):
                value = held[k][half, r, :].astype(F32)
                for other in others:
                    value = value + other[half, r, :].astype(F32)
                held[k][half, r, :] = value.astype(BF16)

            in_rows(0, count, body)

    def ready(k):
        to_y[k].wait_recv()
        for item in load[k : k + 1]:
            item.wait()

    def begin():
        start_all(to_y + load)

    def across():
        for k in range(spans - 1):
            ready(k)
            add(k, [got_y.at[k]])
            over_a[k].start()

    def finish():
        ready(spans - 1)
        for item in over_a:
            item.wait_recv()
        add(spans - 1, [got_y.at[spans - 1]] + [got_a.at[k] for k in range(spans - 1)])
        start_all([over_b, x_own, c_own, keep_own])

    def pass_on():
        over_b.wait_recv()
        start_all([x_other, c_other, keep_other])

    def share():
        x_own.wait_recv()
        c_x_own.start()
        x_other.wait_recv()
        c_x_other.start()

    def end():
        for item in (c_own, c_other, c_x_own, c_x_other):
            item.wait_recv()
        for item in (*to_y, *over_a, over_b, x_own, x_other, c_own, c_other, c_x_own, c_x_other):
            item.wait_send()
        keep_own.wait()
        keep_other.wait()

    return [begin, across, finish, pass_on, share, end]


def return_scratch(spans, count, n, copied):
    dma = pltpu.SemaphoreType.DMA
    one = pltpu.VMEM((spans, 2, count, n), BF16)
    return [
        one,
        *([one] if copied else []),
        pltpu.VMEM((max(spans - 1, 1), 2, count, n), BF16),
        pltpu.VMEM((count, n), BF16),
        dma((2 * spans + 6,)),
        dma((2 * spans + 6,)),
        dma((spans + 2,)),
    ]


def sum_parts(spans, bufs, gots, sends, recvs):
    a, y = lax.axis_index("a"), lax.axis_index("y")
    b, x, c = place()
    steps = []

    def hop(step, targets):
        copies = [
            remote_to(buf, got.at[step + k], sends.at[i, step + k], recvs.at[i, step + k], axis, other)
            for k, (axis, other) in enumerate(targets)
            for i, (buf, got) in enumerate(zip(bufs, gots))
        ]

        def begin():
            start_all(copies)

        def end():
            for copy in copies:
                copy.wait()
            for buf, got in zip(bufs, gots):
                buf[...] = functools.reduce(jnp.add, [buf[...]] + [got[step + k] for k in range(len(targets))])

        steps.extend([begin, end])

    for step, target in enumerate((("c", 1 - c), ("x", 1 - x), ("b", 1 - b), ("y", 1 - y))):
        hop(step, [target])
    if spans > 1:
        hop(4, [("a", lax.rem(a + k, spans)) for k in range(1, spans)])
    return steps


def gelu_both(v):
    inner = 0.7978845608028654 * (v + 0.044715 * (v * v * v))
    t = jnp.tanh(inner)
    slope = 0.7978845608028654 * (1.0 + 0.134145 * (v * v))
    return 0.5 * v * (1.0 + t), 0.5 * (1.0 + t) + 0.5 * v * (1.0 - t * t) * slope


def backward_kernel(
    spans, heads, hd, hidden, gf, n2, cot_all, gu, wgu, wf, wqkv, wo, n1, qkv_all, ctx_all, lse_all,
    resid, tokens, cotangent, keep, gain1, gain2, vec, segc, segr, onehot,
    dattn_all, o_f, o_g, o_u, o_o, o_q, o_k, o_v, out, grad_input, sums, table,
    sib, mid, diag, last, sib2, mid2, diag2, last2, acc, acc2, dattn, dresid, held, parts, ggu, gatt, diags,
    got_sums, got_table, moves, *scratch
):
    total, hc = wo.shape
    fc = gf.shape[4]
    rows, width = resid.shape
    count = gf.shape[3]
    length = segr.shape[2]
    scratch = list(scratch)

    def take(n):
        out = scratch[:n]
        del scratch[:n]
        return out

    cot_load = pltpu.make_async_copy(cot_all, held, moves.at[1])
    cot_load.start()
    meet_all(spans)
    dn2_source, dn1_source, out_source = (types.SimpleNamespace(parts=parts) for _ in range(3))
    dn2_sum = scatter_parts(dn2_share, dn2_source, acc, sib, mid, diag, last, *take(2))
    dn1_sum = scatter_parts(dn1_share, dn1_source, acc, sib, mid, diag, last, *take(2))
    out_sum = scatter_parts(out_share, out_source, acc2, sib2, mid2, diag2, last2, *take(2))
    dattn_in = gather_parts(dattn_share, dattn, dattn_all, *take(3))
    summed = sum_parts(spans, [sums, table], [got_sums, got_table], *take(2))
    pieces = []
    for part, result in ((gf, o_f), (ggu.at[0], o_g), (ggu.at[1], o_u)):
        for first in (0, count // 2):
            at = pl.ds(first, count // 2)
            if part is gf:
                pieces.append(return_parts(spans, part, 0, fc, at, result, *take(7)))
            else:
                got_y, got_a, got_b, *sems = take(6)
                pieces.append(return_parts(spans, part, 0, fc, at, result, got_y, None, got_a, got_b, *sems))
    for i, result in enumerate((o_o, o_q, o_k, o_v)):
        got_y, got_a, got_b, *sems = take(6)
        pieces.append(return_parts(spans, gatt.at[i], 0, hc, pl.ds(0, count), result, got_y, None, got_a, got_b, *sems))
    steps = {}
    for name, piece in zip(("f", "F", "g", "G", "u", "U", "o", "q", "k", "v"), pieces):
        for k, item in enumerate(piece):
            steps[name + str(k)] = item
    for name, parts_of in (("d", dn2_sum), ("e", dn1_sum), ("x", out_sum), ("n", dattn_in), ("s", summed)):
        for k, item in enumerate(parts_of):
            steps[name + "_" + str(k)] = item

    def step(function):
        steps[function.__name__] = function
        return function

    n2_load = pltpu.make_async_copy(n2, held, moves.at[11])
    n1_load = pltpu.make_async_copy(n1, held, moves.at[10])

    @step
    def setup():
        sums[...] = jnp.zeros_like(sums)
        table[...] = jnp.zeros_like(table)

    @step
    def second_norm():
        def body(at):
            value, dn2 = resid[at, :], acc[at, :]
            inv = lax.rsqrt(jnp.mean(value * value, axis=-1, keepdims=True) + eps)
            inner = dn2 * gain2[...]
            grad = (
                cotangent[at, :].astype(F32)
                + inv * inner
                - value * (inv * inv * inv * jnp.mean(inner * value, axis=-1, keepdims=True))
            )
            dresid[at, :] = grad
            sums[1:2, :] += jnp.sum(dn2 * value * inv, axis=0, keepdims=True)
            sums[2:3, :] += jnp.sum(value * value, axis=0, keepdims=True)
            dattn[at, :] = (keep[at, :] * grad).astype(BF16)

        in_rows(0, rows, body)

    wide = max(count, 256)

    def weight_grad(store, factor):
        for first in range(0, total, wide):
            value = dot_first(held[:, first : first + wide], factor).astype(BF16)
            for owner in range(first // count, (first + wide) // count):
                at = owner * count - first
                store[owner // 4, owner // 2 % 2, owner % 2] = value[at : at + count]

    @step
    def first_norm():
        def body(at):
            value, dn1 = tokens[at, :].astype(F32), acc[at, :]
            inv = lax.rsqrt(jnp.mean(value * value, axis=-1, keepdims=True) + eps)
            inner = dn1 * gain1[...]
            grad_input[at, :] = (
                dresid[at, :]
                + inv * inner
                - value * (inv * inv * inv * jnp.mean(inner * value, axis=-1, keepdims=True))
            )
            sums[0:1, :] += jnp.sum(dn1 * value * inv, axis=0, keepdims=True)

        in_rows(0, rows, body)

    @step
    def final():
        def body(at):
            value = resid[at, :] + acc2[at, :]
            out[at, :] = value.astype(BF16)
            sums[3:4, :] += jnp.sum(value * value, axis=0, keepdims=True)

        in_rows(0, rows, body)

    @step
    def tables():
        buckets = lax.dot_general(
            diags[...], onehot[...], (((1,), (1,)), ((), ())), precision=highest, preferred_element_type=F32
        )
        table[slot(*place()), 0:heads, 0 : buckets.shape[1]] = buckets

    def first_half(v_dgu, v_out):
        out_source.parts = v_out
        @step
        def dhidden():
            def inner(v_wf, v_gu):
                wf_load = pltpu.make_async_copy(wf, v_wf, moves.at[0])

                def fetch_gu(m):
                    at = pl.ds(pl.multiple_of(m * rows, rows), rows)
                    slot_of = lax.rem(m, 2)
                    return pltpu.make_async_copy(gu.at[at], v_gu.at[slot_of], moves.at[12 + slot_of])

                start_all([wf_load, fetch_gu(0)])
                wf_load.wait()
                cot_load.wait()

                def body(m, _):
                    at = pl.ds(pl.multiple_of(m * rows, rows), rows)

                    @pl.when(m < 7)
                    def _():
                        fetch_gu(m + 1).start()

                    grad = flat_dot(held[at, :], v_wf[...])
                    fetch_gu(m).wait()
                    both = v_gu[lax.rem(m, 2)]
                    v_dgu[at, :fc] = (grad * both[:, :fc]).astype(BF16)
                    v_dgu[at, fc:] = (grad * both[:, fc:]).astype(BF16)
                    return 0

                lax.fori_loop(0, 8, body, 0)
                n2_load.start()

            pl.run_scoped(inner, pltpu.VMEM(wf.shape, BF16), pltpu.VMEM((2, rows, 2 * fc), F32))

        def with_out(v_wf, v_hidden):
            loads = [pltpu.make_async_copy(wf, v_wf, moves.at[0]), pltpu.make_async_copy(hidden, v_hidden, moves.at[12])]

            def make(m):
                at = pl.ds(pl.multiple_of(m * rows, rows), rows)
                v_out[m] = dot_last(v_hidden[at, :], v_wf[...]).astype(BF16)

            out_source.make = make
            start_all(loads)
            for load in loads:
                load.wait()
            for item in backward_out(types.SimpleNamespace(**steps)):
                item()

        def with_dn2(v_wgu):
            load = pltpu.make_async_copy(wgu, v_wgu, moves.at[0])

            def make(m):
                at = pl.ds(pl.multiple_of(m * rows, rows), rows)
                parts[m] = dot_last(v_dgu[at, :], v_wgu[...]).astype(BF16)

            dn2_source.make = make
            load.start()
            load.wait()
            for item in backward_dn2(types.SimpleNamespace(**steps)):
                item()

        @step
        def grad_g():
            n2_load.wait()
            weight_grad(ggu.at[0], v_dgu[:, :fc])

        @step
        def grad_u():
            weight_grad(ggu.at[1], v_dgu[:, fc:])

        for item in backward_start(types.SimpleNamespace(**steps)):
            item()
        pl.run_scoped(with_dn2, pltpu.VMEM(wgu.shape, BF16))
        pl.run_scoped(with_out, pltpu.VMEM(wf.shape, BF16), pltpu.VMEM(hidden.shape, BF16))
        for item in backward_first(types.SimpleNamespace(**steps)):
            item()

    def second_half(v_qkv, qkv, ctx, lse, dctx, dqkv, shear, v_o):
        loads = [
            pltpu.make_async_copy(src, dst, moves.at[k])
            for src, dst, k in ((wo, v_o, 1), (qkv_all, qkv, 12), (ctx_all, ctx, 13), (lse_all, lse, 14))
        ]
        qkv_load = pltpu.make_async_copy(wqkv, v_qkv, moves.at[0])
        start_all([*loads, qkv_load])
        steps["in_qkv"] = qkv_load.wait

        @step
        def to_ctx():
            copies = [
                pltpu.make_async_copy(dattn_all.at[m], held.at[pl.ds(m * rows, rows)], moves.at[2 + m]) for m in range(8)
            ]
            start_all(copies)
            for copy in (*loads, *copies):
                copy.wait()

            def body(m, _):
                at = pl.ds(pl.multiple_of(m * rows, rows), rows)
                dctx[at, :] = flat_dot(held[at, :], v_o[...]).astype(BF16)
                return 0

            lax.fori_loop(0, 8, body, 0)

        @step
        def grad_o():
            weight_grad(gatt.at[0], ctx[...])
            n1_load.start()

        def attend_back(h):
            bias = shear_bias(vec[h : h + 1, :], length)
            q_cols, k_cols, v_cols = (slice(k * hc + h * hd, k * hc + (h + 1) * hd) for k in range(3))
            for s in range(2):
                at = slice(s * length, (s + 1) * length)
                same = segc[s] == segr[s]
                q, k, v, d = qkv[at, q_cols], qkv[at, k_cols], qkv[at, v_cols], dctx[at, q_cols]
                scores = jnp.where(same, dot_last(q, k) + bias, far_below)
                probs = jnp.exp(scores - lse[at, h : h + 1])
                dprobs = dot_last(d, v)
                dqkv[at, v_cols] = dot_first(probs.astype(BF16), d).astype(BF16)
                product = probs * dprobs
                dscores = product - probs * jnp.sum(product, axis=1, keepdims=True)
                if s == 0:
                    shear[...] = dscores
                else:
                    shear[...] += dscores
                dlogits = dscores.astype(BF16)
                dqkv[at, q_cols] = flat_dot(dlogits, k).astype(BF16)
                dqkv[at, k_cols] = dot_first(dlogits, q).astype(BF16)

            def shift(g, carry):
                group = shear[pl.ds(pl.multiple_of(g * 8, 8), 8), :]
                group = jnp.concatenate([group, jnp.zeros_like(group)], axis=1)
                return carry + pltpu.roll(group, 2 * length - g * 8, 1)

            shifted = lax.fori_loop(0, length // 8, shift, jnp.zeros((8, 2 * length), F32), unroll=8)
            line = shifted[0:1, :]
            for r in range(1, 8):
                line = line + pltpu.roll(shifted[r : r + 1, :], 2 * length - r, 1)
            diags[h : h + 1, :] = line

        for h in range(heads):
            steps["h" + str(h)] = functools.partial(attend_back, h)

        for i, name in enumerate(("q", "k", "v")):

            def grad_of(i=i):
                if i == 0:
                    n1_load.wait()
                weight_grad(gatt.at[1 + i], dqkv[:, i * hc : (i + 1) * hc])

            steps["grad_" + name] = grad_of

        def make(m):
            at = pl.ds(pl.multiple_of(m * rows, rows), rows)
            parts[m] = dot_last(dqkv[at, :], v_qkv[...]).astype(BF16)

        dn1_source.make = make

        for item in backward_second(types.SimpleNamespace(**steps)):
            item()

    pl.run_scoped(first_half, pltpu.VMEM((8 * rows, 2 * fc), BF16), pltpu.VMEM((8, rows, width), BF16))
    pl.run_scoped(
        second_half,
        pltpu.VMEM((total, 3 * hc), BF16),
        pltpu.VMEM((8 * rows, 3 * hc), BF16),
        pltpu.VMEM((8 * rows, hc), BF16),
        pltpu.VMEM((8 * rows, heads), F32),
        pltpu.VMEM((8 * rows, hc), BF16),
        pltpu.VMEM((8 * rows, 3 * hc), BF16),
        pltpu.VMEM((length, length), F32),
        pltpu.VMEM((total, hc), BF16),
    )
    for name in ("f", "F", "g", "G", "u", "U", "o", "q", "k", "v"):
        steps[name + "5"]()


dn2_share, dattn_share, dn1_share, out_share = (0.625, 0.75, 0.75, 0.75)


def backward_start(n):
    return (
        n.F0, n.dhidden, n.F1,
    )


def backward_dn2(n):
    return (
        n.d_0, n.d_4, n.f0, n.d_1, n.d_2, n.d_6, n.d_5, n.d_3,
    )


def backward_out(n):
    return (
        n.d_9, n.d_8, n.d_7, n.F2, n.grad_g, n.g0, n.f1, n.setup, n.G0, n.d_10,
        n.second_norm, n.n_0, n.grad_u, n.x_0, n.u0, n.x_1, n.x_2, n.x_4, n.n_1, n.x_3,
        n.x_6, n.g1, n.n_2, n.U0, n.x_5, n.x_8, n.x_7, n.f2, n.x_9, n.G1,
    )


def backward_first(n):
    return (
    )


def backward_second(n):
    return (
        n.F3, n.n_3, n.n_4, n.n_5, n.n_6, n.n_7, n.u1, n.to_ctx, n.h0, n.grad_o,
        n.h1, n.U1, n.f3, n.g2, n.h2, n.o0, n.G2, n.h3, n.u2, n.in_qkv,
        n.o1, n.e_0, n.e_1, n.e_4, n.e_2, n.grad_q, n.x_10, n.q0, n.final, n.e_3,
        n.e_6, n.u3, n.tables, n.grad_k, n.e_5, n.e_9, n.G3, n.e_8, n.k0, n.U2,
        n.g3, n.q1, n.k1, n.grad_v, n.v0, n.q2, n.e_7, n.e_10, n.first_norm, n.s_0,
        n.s_1, n.s_2, n.g4, n.o2, n.U3, n.v1, n.q3, n.s_3, n.f4, n.G4,
        n.F4, n.s_4, n.k2, n.o3, n.s_5, n.s_6, n.v2, n.U4, n.s_7, n.s_8,
        n.k3, n.o4, n.v3, n.u4, n.k4, n.q4, n.s_9, n.v4,
    )


def backward(
    spans, hidden, grad_f, n2, cot_all, gu, wgu, wf, wqkv, wo, n1, qkv, ctx, lse, resid, tokens, cotangent, keep, gain1, gain2, vec, segc, segr, onehot, hd, number
):
    rows, width = tokens.shape
    heads, length = vec.shape[0], segr.shape[2]
    total, hc = wo.shape
    fc = grad_f.shape[1]
    count = total // (4 * spans)
    dma, shape, vmem = pltpu.SemaphoreType.DMA, jax.ShapeDtypeStruct, pltpu.VMEM
    scratch = scatter_scratch(rows, width)[:4] + scatter_scratch(rows, width)[:4]
    scratch += [
        vmem((rows, width), F32),
        vmem((rows, width), F32),
        vmem((rows, width), BF16),
        vmem((rows, width), F32),
        vmem((8 * rows, width), BF16),
        vmem((8, rows, width), BF16),
        vmem((2, spans, 2, 2, count, fc), BF16),
        vmem((4, spans, 2, 2, count, hc), BF16),
        vmem((heads, 2 * length), F32),
        vmem((3 + spans, 8, width), F32),
        vmem((3 + spans, 8, 8, 128), F32),
        dma((15,)),
    ]
    scratch += [dma((10,))] * 6
    scratch += [dma((9,)), dma((9,)), dma, dma((2, 3 + spans)), dma((2, 3 + spans))]
    for i in range(6):
        scratch += return_scratch(spans, count // 2, fc, i < 2)
    for _ in range(4):
        scratch += return_scratch(spans, count, hc, False)
    outs = pl.pallas_call(
        functools.partial(backward_kernel, spans, heads, hd),
        out_shape=[shape((8, rows, width), BF16)]
        + [shape((count, 8 * fc), BF16)] * 3
        + [shape((count, 8 * hc), BF16)] * 4
        + [shape((rows, width), BF16), shape((rows, width), F32), shape((8, width), F32), shape((8, 8, 128), F32)],
        in_specs=[any_space] * 13 + [in_vmem] * 10,
        out_specs=[any_space] * 8 + [in_vmem] * 4,
        scratch_shapes=scratch,
        compiler_params=pltpu.CompilerParams(collective_id=number, has_side_effects=True, vmem_limit_bytes=62 * MIB),
    )(
        hidden,
        grad_f.reshape(spans, 2, 2, count, fc),
        n2,
        cot_all,
        gu,
        wgu,
        wf,
        wqkv,
        wo,
        n1,
        qkv,
        ctx,
        lse,
        resid,
        tokens,
        cotangent,
        keep,
        gain1[None, :],
        gain2[None, :],
        vec,
        segc,
        segr,
        onehot,
    )
    return outs[1:]


def last_kernel(count, entries, *refs):
    came, gone = refs[: count + 3], refs[count + 3 :]
    for narrow, wide in zip(came[:-1], gone):
        wide[...] = narrow[...].astype(wide.dtype)

    @pl.when(pl.program_id(0) == 0)
    def _():
        sums, (gain1, gain2, norms) = came[-1], gone[count + 2 :]
        gain1[...] = sums[0:1, :]
        gain2[...] = sums[1:2, :]
        norms[...] = jnp.sqrt(jnp.sum(sums[2:4, :], axis=1, keepdims=True) / entries)


def last(grads, out, grad_input, sums, entries):
    steps = max(min(grads[0].shape[0] // 16, 8), 1)
    arrays = [*grads, out, grad_input]
    count = len(grads)

    def rows_of(array):
        return pl.BlockSpec((array.shape[0] // steps, array.shape[1]), lambda i: (i, 0))

    def whole(*shape):
        return pl.BlockSpec(shape, lambda i: (0, 0))

    width = sums.shape[1]
    shape = jax.ShapeDtypeStruct
    return pl.pallas_call(
        functools.partial(last_kernel, count, entries),
        grid=(steps,),
        in_specs=[*map(rows_of, arrays), whole(*sums.shape)],
        out_specs=[*map(rows_of, arrays), whole(1, width), whole(1, width), whole(2, 1)],
        out_shape=[shape(array.shape, F32) for array in grads]
        + [shape(out.shape, out.dtype), shape(grad_input.shape, F32)]
        + [shape((1, width), F32)] * 2
        + [shape((2, 1), F32)],
        compiler_params=pltpu.CompilerParams(vmem_limit_bytes=62 * MIB),
    )(*arrays, sums)


def per_device(
    tokens,
    w_query,
    w_key,
    w_value,
    w_attn_out,
    w_gate,
    w_up,
    w_ff_out,
    gain_attn,
    gain_ffn,
    rel_table,
    doc_lengths,
    cotangent,
):
    rows, width = tokens.shape
    n_buckets, heads_all = rel_table.shape
    heads = heads_all // 8
    hc = w_query.shape[1] // 8
    fc = w_gate.shape[1] // 8
    hd = hc // heads
    length = 4 * rows

    ends = jnp.cumsum(doc_lengths, axis=1).astype(jnp.int32)
    offset = np.arange(-length, length)
    distance = np.abs(offset)
    far = 8 + np.sum(distance[:, None] >= np.array(thresholds), axis=1)
    bucket = np.where(offset > 0, 16, 0) + np.where(distance < 8, distance, far)
    onehot = (np.arange(n_buckets)[:, None] == bucket[None, :]).astype(np.float32)
    order = np.roll(onehot, length, axis=1)

    spans = lax.axis_size("a")
    weights = (w_query, w_key, w_value, w_attn_out, w_gate, w_up, w_ff_out)
    (cot_all, n2, n1, wqkv, wo, wgu, wf, gate_up, hidden, grad_f, qkv, ctx, lse, resid, segc, segr, keep, vec) = forward(
        spans, tokens, cotangent, weights, ends, gain_attn, gain_ffn, rel_table, jnp.asarray(onehot), hd, 0
    )
    grad_f, grad_g, grad_u, grad_o, grad_q, grad_k, grad_v, out, grad_input, sums, table_sums = backward(
        spans, hidden, grad_f, n2, cot_all, gate_up, wgu, wf, wqkv, wo, n1, qkv, ctx, lse, resid, tokens, cotangent, keep, gain_attn, gain_ffn,
        vec, segc, segr, jnp.asarray(order), hd, 1
    )
    dtable = table_sums[:, :heads, :n_buckets].reshape(heads_all, n_buckets).T
    entries = rows * width * 16 * spans
    grads = [grad_q, grad_k, grad_v, grad_o, grad_g, grad_u, grad_f]
    *grads, out, grad_input, dgain_attn, dgain_ffn, norms = last(grads, out, grad_input, sums, entries)
    return (out, grad_input, *grads, dgain_attn[0], dgain_ffn[0], dtable, norms[:, 0])


def solution(mesh):
    owners, copies = mesh.shape["fsdp"], mesh.shape["rep"]
    finer = Mesh(mesh.devices.reshape(owners // 4, 2, 2, copies // 2, 2), ("a", "b", "y", "x", "c"))
    owner = ("a", "b", "y")
    piece = P(owner + ("x", "c"), None)
    shard = P(owner, None)
    return jax.shard_map(
        per_device,
        mesh=finer,
        in_specs=(piece,) + (shard,) * 7 + (P(), P(), P(), shard, piece),
        out_specs=(piece, piece) + (shard,) * 7 + (P(), P(), P(), P()),
        check_vma=False,
    )
```
